32 devices in a mesh: dp: 16 (over z, x, core), mp: 2 (over y).
Axes of the slice: x: 2, y: 2, z: 4, core: 2. Of those that a mesh axis runs over, the one named last changes fastest.
Arguments:
- text_rows: bfloat16 [8192, 768], P('dp'), may hold values from -6 to 6
- visual_rows: bfloat16 [8192, 768], P('dp'), may hold values from -6 to 6
- text_mask: int32 [8192], P('dp'), may hold values 0 or 1
- visual_mask: int32 [8192], P('dp'), may hold values 0 or 1
- text_places: int32 [8192], P('dp'), may hold values from 0 to 511
- text_boxes: int32 [8192, 2], P('dp'), may hold values from 0 to 31
- visual_boxes: int32 [8192, 2], P('dp'), may hold values from 0 to 31
- mask_embed: bfloat16 [2, 768], replicated, may hold values from -6 to 6
- w_qkv: bfloat16 [2, 3, 768, 768], P(None, None, None, 'mp'), may hold values from -0.21875 to 0.21875
- w_out: bfloat16 [2, 768, 768], P(None, 'mp'), may hold values from -1.75 to 1.75
- rel_table: float32 [128, 12], P(None, 'mp'), may hold values from -3 to 3
- ln_gain: float32 [2, 2, 768], replicated, may hold values from 0.5 to 1.5
- ln_bias: float32 [2, 2, 768], replicated, may hold values from -2 to 2
- w_up: bfloat16 [2, 768, 3072], P(None, None, 'mp'), may hold values from -0.21875 to 0.21875
- b_up: float32 [2, 3072], P(None, 'mp'), may hold values from -3 to 3
- w_down: bfloat16 [2, 3072, 768], P(None, 'mp'), may hold values from -0.109375 to 0.109375
- b_down: float32 [2, 768], replicated, may hold values from -2 to 2
- text_cotangent: bfloat16 [8192, 768], P('dp'), may hold values from -6 to 6
- visual_cotangent: bfloat16 [8192, 768], P('dp'), may hold values from -6 to 6
Outputs:
- text_out: bfloat16 [8192, 768], P('dp')
- visual_out: bfloat16 [8192, 768], P('dp')
- text_input_grad: bfloat16 [8192, 768], P('dp')
- visual_input_grad: bfloat16 [8192, 768], P('dp')
- mask_embed_grad: float32 [2, 768], replicated
- w_qkv_grad: float32 [2, 3, 768, 768], P(None, None, None, 'mp')
- w_out_grad: float32 [2, 768, 768], P(None, 'mp')
- rel_table_grad: float32 [128, 12], P(None, 'mp')
- ln_gain_grad: float32 [2, 2, 768], replicated
- ln_bias_grad: float32 [2, 2, 768], replicated
- w_up_grad: float32 [2, 768, 3072], P(None, 'dp', 'mp')
- b_up_grad: float32 [2, 3072], P(None, ('mp', 'dp'))
- w_down_grad: float32 [2, 3072, 768], P(None, 'mp', 'dp')
- b_down_grad: float32 [2, 768], P(None, 'dp')
The draws below stay inside these ranges and needn't reach their ends.
Inputs may be any that keep to these rules, and one draw needn't show every extreme that they name: `text_mask`: one flag a row. `visual_mask`: one flag a row. `text_places`: positions inside the page. `text_boxes`: horizontal, then vertical coordinate. `visual_boxes`: horizontal, then vertical coordinate.
All inputs are finite; a program needn't handle non-finite values. No bound on the sum of `text_mask` or of `visual_mask` on one device may be relied on, other than what follows from the above.
Results may differ from the reference program's by a relative error of at most 0.018.
Values may be sent and summed in bfloat16 or wider, within the bound.
No kernel may reach another device: no remote copies, remote signals or barrier semaphores. Data moves between devices by JAX's collectives and lax.ppermute only.
A program may use at most 256 MiB of HBM per device.

```python
from functools import partial
import jax
import jax.numpy as jnp
from jax import lax

D = 768
H = 12
HD = 64
FF = 3072
PAGE = 512
REL_1D = 64
REL_2D = 32
BUCKETS = 128
PAGES = 16
TOKENS = 8192
N_MP = 2


def touch_ends(values, rng, smallest, high):
    extent = values.shape
    index_at = [jax.random.randint(jax.random.fold_in(rng, axis), (), 0, extent[axis]) for axis in range(len(extent))]
    values = values.at[tuple(index_at)].set(smallest)
    longest = extent.index(max(extent))
    index_at[longest] = (index_at[longest] + 1) % extent[longest]
    return values.at[tuple(index_at)].set(high)


def strengthened(values, rng, source, target, shards_of, factor):
    owner, partner = [(jnp.arange(values.shape[position]) // (values.shape[position] // shards_of)).reshape([-1 if axis == position else 1 for axis in range(values.ndim)]) for position in (source, target)]
    chosen = jax.random.permutation(rng, shards_of)[partner]
    strong = (owner == chosen) | (owner == (partner + shards_of // 2) % shards_of)
    return jnp.where(strong, factor * values, values)


def block_levels(own_key, extent, shards, smallest, largest):
    factor_of, own = 1.0, jax.random.fold_in(own_key, 6)
    for axis_at, blocks in shards:
        heights = jnp.exp(jax.random.uniform(jax.random.fold_in(own, axis_at), (blocks,), jnp.float32, smallest / len(shards), largest / len(shards)))
        factor_of = factor_of * jnp.repeat(heights, extent[axis_at] // blocks).reshape([-1 if axis == axis_at else 1 for axis in range(len(extent))])
    return factor_of


def normal_values(stream_key, shape, scale, reach, split=(), kind=jnp.bfloat16):
    drawn = jax.random.normal(stream_key, shape, jnp.float32) * scale
    if len(split) > 0:
        drawn = block_levels(stream_key, shape, split, -0.22, 0.18) * drawn
    return jnp.clip(drawn, min=-reach, max=reach).astype(kind)


def noise_with(key, extent, scale, bound, cuts, heavy, kind=jnp.bfloat16):
    result = scale * jax.random.normal(key, extent, jnp.float32)
    if cuts:
        result = result * block_levels(key, extent, cuts, -0.22, 0.18)
    return jnp.clip(strengthened(result, jax.random.fold_in(key, 3), *heavy), -bound, bound).astype(kind)


def setup_inputs(seed: int = 0) -> dict:
    keys = jax.random.split(jax.random.key(seed), 20)
    return {
        "text_rows": normal_values(keys[0], (TOKENS, D), 1.0, 6.0, ((0, 16),)),
        "visual_rows": normal_values(keys[1], (TOKENS, D), 1.0, 6.0, ((0, 16),)),
        "text_mask": touch_ends((jax.random.randint(keys[2], (TOKENS,), 0, 20) < 3).astype(jnp.int32), jax.random.fold_in(keys[2], 1), 0, 1),
        "visual_mask": touch_ends((jax.random.randint(keys[3], (TOKENS,), 0, 20) < 3).astype(jnp.int32), jax.random.fold_in(keys[3], 1), 0, 1),
        "text_places": touch_ends(jax.random.randint(keys[4], (TOKENS,), 0, PAGE), jax.random.fold_in(keys[4], 1), 0, PAGE - 1).astype(jnp.int32),
        "text_boxes": touch_ends(jax.random.randint(keys[5], (TOKENS, 2), 0, REL_2D), jax.random.fold_in(keys[5], 1), 0, REL_2D - 1).astype(jnp.int32),
        "visual_boxes": touch_ends(jax.random.randint(keys[6], (TOKENS, 2), 0, REL_2D), jax.random.fold_in(keys[6], 1), 0, REL_2D - 1).astype(jnp.int32),
        "mask_embed": normal_values(keys[7], (2, D), 1.0, 6.0),
        "w_qkv": normal_values(keys[8], (2, 3, D, D), D ** -0.5, 0.21875, ((3, 2),)),
        "w_out": normal_values(keys[9], (2, D, D), (D // 64) ** -0.5, 1.75, ((1, 2),)),
        "rel_table": normal_values(keys[10], (BUCKETS, H), 0.5, 3.0, ((1, 2),), jnp.float32),
        "ln_gain": jnp.clip(1.0 + 0.1 * jax.random.normal(keys[11], (2, 2, D), jnp.float32), 0.5, 1.5),
        "ln_bias": normal_values(keys[12], (2, 2, D), 0.3, 2.0, (), jnp.float32),
        "w_up": normal_values(keys[13], (2, D, FF), D ** -0.5, 0.21875, ((2, 2),)),
        "b_up": normal_values(keys[14], (2, FF), 0.5, 3.0, ((1, 2),), jnp.float32),
        "w_down": normal_values(keys[15], (2, FF, D), FF ** -0.5, 0.109375, ((1, 2),)),
        "b_down": normal_values(keys[16], (2, D), 0.3, 2.0, (), jnp.float32),
        "text_cotangent": noise_with(keys[17], (TOKENS, D), 1.0, 6.0, ((0, 16),), (0, 1, 16, 2.0)),
        "visual_cotangent": noise_with(keys[18], (TOKENS, D), 1.0, 6.0, ((0, 16),), (0, 1, 16, 2.0)),
    }


@jax.custom_vjp
def low(v):
    return lax.optimization_barrier(v.astype(jnp.bfloat16)).astype(jnp.float32)

@jax.custom_vjp
def low_back(v):
    return v

def low_keep(v):
    return (low(v), None)

def low_pass(kept, grad):
    return (grad,)

def back_keep(v):
    return (v, None)

def back_low(kept, grad):
    return (low(grad),)
low.defvjp(low_keep, low_pass)
low_back.defvjp(back_keep, back_low)

def matmul(left_operand, right_operand):
    return jnp.dot(left_operand, right_operand, precision=lax.Precision.HIGHEST, preferred_element_type=jnp.float32)

def norm_rows(values, gain_row, shift_row):
    average = lax.optimization_barrier(jnp.mean(values, axis=-1, keepdims=True))
    centred = values - average
    spread = lax.optimization_barrier(jnp.mean(centred * centred, axis=-1, keepdims=True))
    return centred * lax.rsqrt(spread + 1e-05) * gain_row + shift_row

def bucket_index(places, box_coords):
    line_half = REL_1D // 2
    plane_half = REL_2D // 2
    line_bucket = jnp.clip(places[None, :] - places[:, None], -line_half, line_half - 1) + line_half
    across = jnp.clip(box_coords[None, :, 0] - box_coords[:, None, 0], -plane_half, plane_half - 1) + plane_half + REL_1D
    downward = jnp.clip(box_coords[None, :, 1] - box_coords[:, None, 1], -plane_half, plane_half - 1) + plane_half + REL_1D + REL_2D
    return (line_bucket, across, downward)

def page_attention(table_heads, pieces):
    queries, key_rows, value_rows, places, box_coords = pieces
    query_heads = queries.reshape(PAGE, H, HD)
    key_heads = key_rows.reshape(PAGE, H, HD)
    value_heads = value_rows.reshape(PAGE, H, HD)
    raw_scores = jnp.einsum('qhd,khd->hqk', query_heads, key_heads, precision=lax.Precision.HIGHEST, preferred_element_type=jnp.float32) * HD ** (-0.5)
    raw_scores = low_back(raw_scores)
    line_bucket, across, downward = bucket_index(places, box_coords)
    bias_terms = jnp.take(table_heads, line_bucket, axis=1) + jnp.take(table_heads, across, axis=1) + jnp.take(table_heads, downward, axis=1)
    weights = jax.nn.softmax(raw_scores + bias_terms, axis=-1)
    context = jnp.einsum('hqk,khd->qhd', low(weights), value_heads, precision=lax.Precision.HIGHEST, preferred_element_type=jnp.float32)
    return context.reshape(PAGE, D)

def layer_forward(text_mask, visual_mask, text_places, text_boxes, visual_boxes, text_rows, visual_rows, mask_embed, w_qkv, w_out, rel_table, ln_gain, ln_bias, w_up, b_up, w_down, b_down):
    visual_places = jnp.arange(TOKENS, dtype=jnp.int32) % PAGE
    inputs = (text_rows, visual_rows)
    flag_rows = (text_mask, visual_mask)
    places = (text_places, visual_places)
    box_coords = (text_boxes, visual_boxes)
    table_heads = rel_table.T
    head_width = D // N_MP
    unit_width = FF // N_MP
    embedded = [jnp.where(flag_rows[modality][:, None] == 1, mask_embed[modality][None, :], inputs[modality]) for modality in range(2)]
    attended_values = [jnp.zeros((TOKENS, D), jnp.float32) for group in range(N_MP)]
    for modality in range(2):
        embed_low = low(embedded[modality])
        queries = low(low_back(matmul(embed_low, w_qkv[modality, 0])))
        key_rows = low(low_back(matmul(embed_low, w_qkv[modality, 1])))
        value_rows = low(low_back(matmul(embed_low, w_qkv[modality, 2])))
        context = lax.map(jax.checkpoint(partial(page_attention, table_heads)), (queries.reshape(PAGES, PAGE, D), key_rows.reshape(PAGES, PAGE, D), value_rows.reshape(PAGES, PAGE, D), places[modality].reshape(PAGES, PAGE), box_coords[modality].reshape(PAGES, PAGE, 2)))
        context = low(low_back(context.reshape(TOKENS, D)))
        for group in range(N_MP):
            lower = group * head_width
            attended_values[group] = attended_values[group] + matmul(context[:, lower:lower + head_width], w_out[modality, lower:lower + head_width])
    mixed_sum = jnp.zeros((TOKENS, D), jnp.float32)
    for group in range(N_MP):
        mixed_sum = mixed_sum + low(low_back(attended_values[group]))
    results = []
    for modality in range(2):
        hidden = norm_rows(embedded[modality] + mixed_sum, ln_gain[modality, 0], ln_bias[modality, 0])
        pre_act = low_back(matmul(low(hidden), w_up[modality]) + b_up[modality])
        activation = low(jax.nn.gelu(pre_act, approximate=False))
        down_total = jnp.zeros((TOKENS, D), jnp.float32) + b_down[modality]
        for group in range(N_MP):
            lower = group * unit_width
            down_total = down_total + low(low_back(matmul(activation[:, lower:lower + unit_width], w_down[modality, lower:lower + unit_width])))
        results.append(norm_rows(hidden + down_total, ln_gain[modality, 1], ln_bias[modality, 1]))
    return (results[0], results[1])

def reference(text_rows, visual_rows, text_mask, visual_mask, text_places, text_boxes, visual_boxes, mask_embed, w_qkv, w_out, rel_table, ln_gain, ln_bias, w_up, b_up, w_down, b_down, text_cotangent, visual_cotangent):
    floats = tuple((member.astype(jnp.float32) for member in (text_rows, visual_rows, mask_embed, w_qkv, w_out, rel_table, ln_gain, ln_bias, w_up, b_up, w_down, b_down)))
    results, pullback = jax.vjp(partial(layer_forward, text_mask, visual_mask, text_places, text_boxes, visual_boxes), *floats)
    gradients = pullback((text_cotangent.astype(jnp.float32), visual_cotangent.astype(jnp.float32)))
    return (results[0].astype(jnp.bfloat16), results[1].astype(jnp.bfloat16), gradients[0].astype(jnp.bfloat16), gradients[1].astype(jnp.bfloat16), gradients[2], gradients[3], gradients[4], gradients[5], gradients[6], gradients[7], gradients[8], gradients[9], gradients[10], gradients[11])
```

```python
from functools import partial

import jax
import jax.numpy as jnp
from jax import lax
from jax.experimental import pallas as pl
from jax.experimental.pallas import tpu as pltpu
from jax.sharding import PartitionSpec as P

D = 768
HD = 64
PAGE = 512
REL_1D = 64
REL_2D = 32
COARSE = 16
BLOCK = 768
BF = jnp.bfloat16
F32 = jnp.float32
VMEM_BYTES = 58 * 1024 * 1024


def mm(a, b):
    return lax.dot_general(a, b, (((1,), (0,)), ((), ())), preferred_element_type=F32)


def mm_nt(a, b):
    return lax.dot_general(a, b, (((1,), (1,)), ((), ())), preferred_element_type=F32)


def iota(shape, dim):
    return lax.broadcasted_iota(jnp.int32, shape, dim)


def row_sum(x):
    return jnp.sum(x, axis=-1, keepdims=True)


def row_mean(x):
    return jnp.mean(x, axis=-1, keepdims=True)


def col_sum(x):
    return jnp.sum(x, axis=0, keepdims=True)


def line_buckets(cols, rows):
    half = REL_1D // 2
    return jnp.clip(rows[0, 0:1, :] - cols[0, :, 0:1], -half, half - 1) + half


def place_lanes(cols):
    lane = iota((PAGE, 128), 1)
    code = lane & 63
    across = jnp.broadcast_to(cols[0, :, 1:2], (PAGE, 128))
    down = jnp.broadcast_to(cols[0, :, 2:3], (PAGE, 128)) + REL_2D
    return jnp.where(jnp.where(code < REL_2D, across, down) == code, 1.0, 0.0)


def table_plane(table_row):
    b = iota((128, 128), 0)
    lane = iota((128, 128), 1)
    c = lane & 63
    half = REL_2D // 2
    shift = jnp.clip((c & 31) - (b & 31), -half, half - 1) + half + REL_1D
    index = jnp.where(c >= REL_2D, shift + REL_2D, shift)
    spread = jnp.broadcast_to(table_row, (128, 128))
    values = jnp.take_along_axis(spread, index, axis=1)
    values = jnp.where((b >> 5) == (c >> 5), values, 0.0)
    high = values.astype(BF).astype(F32)
    return jnp.where(lane < 64, high, values - high).astype(BF)


def forward_kernel(rows_per_step, heads, has_partial, *refs):
    (cols, rows, raw, membed, wqkv, table, wout), refs = refs[:7], refs[7:]
    if has_partial:
        partial_ref, refs = refs[0], refs[1:]
    emb, qkv, prob, ctx, att, idx_s, bias_s = refs
    masked = cols[0, :, 3:4] == 1
    embedded = jnp.where(masked, membed[0].astype(F32), raw[...].astype(F32)).astype(BF)
    emb[...] = embedded
    qkv[0] = (mm(embedded, wqkv[0, 0]) * HD ** (-0.5)).astype(BF)
    qkv[1] = mm(embedded, wqkv[0, 1]).astype(BF)
    qkv[2] = mm(embedded, wqkv[0, 2]).astype(BF)
    idx_s[...] = line_buckets(cols, rows)
    onehot = place_lanes(cols).astype(BF)
    planes = jnp.concatenate([table_plane(table[h : h + 1, :]) for h in range(heads)], axis=1)
    bias_s[...] = mm(onehot, planes).astype(BF)
    for h in range(heads):
        head = slice(HD * h, HD * (h + 1))
        keys = jnp.concatenate([onehot, qkv[1, :, head]], axis=1)
        values = qkv[2, :, head]
        for start in range(0, PAGE, rows_per_step):
            part = slice(start, start + rows_per_step)
            left = jnp.concatenate(
                [bias_s[part, 128 * h : 128 * (h + 1)], qkv[0, part, head]], axis=1
            )
            scores = mm_nt(left, keys)
            spread = jnp.broadcast_to(table[h : h + 1, :], (rows_per_step, 128))
            line = [
                jnp.take_along_axis(spread, idx_s[part, 128 * b : 128 * (b + 1)], axis=1)
                for b in range(PAGE // 128)
            ]
            scores = scores + jnp.concatenate(line, axis=1)
            exponent = jnp.exp(scores - jnp.max(scores, axis=-1, keepdims=True))
            weights = (exponent * (1.0 / row_sum(exponent))).astype(BF)
            prob[h, part, :] = weights
            ctx[part, head] = mm(weights, values).astype(BF)
    attended = mm(ctx[...], wout[0])
    if has_partial:
        att[...] = (partial_ref[...] + attended).astype(BF)
    else:
        att[...] = attended


def gelu_both(x):
    z = jnp.abs(x)
    t = 1.0 / (1.0 + (0.3275911 * 0.5**0.5) * z)
    poly = t * (
        0.127414796
        + t * (-0.142248368 + t * (0.7107068705 + t * (-0.7265760135 + t * 0.5307027145)))
    )
    bell = jnp.exp(-0.5 * x * x)
    tail = poly * bell
    phi = jnp.where(x >= 0, 1.0 - tail, tail)
    return x * phi, phi + x * bell * 0.3989422804014327


def copy_list(ids, up_own, down_own, up_recv, down_recv, up_s, down_s, sems):
    mp, q = ids[1], ids[2]
    half = up_own.shape[2]
    quarter = half // 4
    copies = []
    for t in range(half // BLOCK):
        span = slice(BLOCK * t, BLOCK * (t + 1))
        copies.append((up_own.at[mp, :, span], up_s.at[:, span]))
    for j in range(4):
        place = pl.multiple_of(half + quarter * (q ^ j), 128)
        copies.append((up_recv[j], up_s.at[:, pl.ds(place, quarter)]))
    for t in range(half // BLOCK):
        span = slice(BLOCK * t, BLOCK * (t + 1))
        copies.append((down_own.at[mp, span, :], down_s.at[span, :]))
    for j in range(4):
        place = pl.multiple_of(half + quarter * (q ^ j), 128)
        copies.append((down_recv[j], down_s.at[pl.ds(place, quarter), :]))
    return [pltpu.make_async_copy(a, b, sems.at[i]) for i, (a, b) in enumerate(copies)]


def ffn_kernel(
    ids,
    cols,
    emb,
    att_own,
    att_peer,
    gain,
    shift,
    b_up,
    b_down,
    cot_text,
    cot_visual,
    up_own,
    down_own,
    uy,
    ux,
    uc,
    dy,
    dx,
    dc,
    out,
    dfirst,
    act,
    dpre,
    hid_low,
    dlow,
    bup_grad,
    vectors,
    up_s,
    down_s,
    cot_s,
    slope_s,
    norm1,
    hidden,
    work,
    dcomb,
    sems,
    cot_sem,
):
    mp = ids[1]
    up_recv = (uy, uc.at[0], ux, uc.at[1])
    down_recv = (dy, dc.at[0], dx, dc.at[1])
    copies = copy_list(ids, up_own, down_own, up_recv, down_recv, up_s, down_s, sems)
    n_own = up_own.shape[2] // BLOCK
    per_side = n_own + 4
    for i in range(n_own):
        copies[i].start()
        copies[per_side + i].start()
    for i in range(n_own, per_side):
        copies[i].start()
        copies[per_side + i].start()

    @pl.when(mp == 0)
    def _():
        c = pltpu.make_async_copy(cot_text, cot_s, cot_sem)
        c.start()
        c.wait()

    @pl.when(mp != 0)
    def _():
        c = pltpu.make_async_copy(cot_visual, cot_s, cot_sem)
        c.start()
        c.wait()

    total = emb[...].astype(F32) + (att_own[...].astype(F32) + att_peer[...].astype(F32))
    centred = total - row_mean(total)
    inv1 = lax.rsqrt(row_mean(centred * centred) + 1e-05)
    n1 = centred * inv1
    norm1[...] = n1
    hid = n1 * gain[0, 0:1, :] + shift[0, 0:1, :]
    hidden[...] = hid
    hid_low[...] = hid.astype(BF)
    n_blocks = up_s.shape[1] // BLOCK
    for t in range(n_blocks):
        if t < n_own:
            copies[t].wait()
            copies[per_side + t].wait()
        elif t == n_own:
            for i in range(n_own, per_side):
                copies[i].wait()
                copies[per_side + i].wait()
        span = slice(BLOCK * t, BLOCK * (t + 1))
        pre = mm(hid_low[...], up_s[:, span]) + b_up[:, span]
        value, slope = gelu_both(pre)
        act[:, span] = value.astype(BF)
        slope_s[:, span] = slope
        down = mm(act[:, span], down_s[span, :])
        if t == 0:
            work[...] = down
        else:
            work[...] += down
    combined = hidden[...] + work[...] + b_down[0]
    centred2 = combined - row_mean(combined)
    inv2 = lax.rsqrt(row_mean(centred2 * centred2) + 1e-05)
    n2 = centred2 * inv2
    out[...] = (n2 * gain[0, 1:2, :] + shift[0, 1:2, :]).astype(BF)
    cot = cot_s[...].astype(F32)
    vectors[1:2, :] = col_sum(cot * n2)
    vectors[2:3, :] = col_sum(cot)
    scaled = cot * gain[0, 1:2, :]
    back = inv2 * (scaled - row_mean(scaled) - n2 * row_mean(scaled * n2))
    dcomb[...] = back
    vectors[0:1, :] = col_sum(back)
    dlow[...] = back.astype(BF)
    for t in range(n_blocks):
        span = slice(BLOCK * t, BLOCK * (t + 1))
        dact = mm_nt(dlow[...], down_s[span, :])
        low = (dact * slope_s[:, span]).astype(BF)
        dpre[:, span] = low
        bup_grad[:, span] = col_sum(low.astype(F32))
        dhid = mm_nt(low, up_s[:, span])
        if t == 0:
            work[...] = dhid
        else:
            work[...] += dhid
    dhidden = dcomb[...] + work[...]
    n1 = norm1[...]
    vectors[3:4, :] = col_sum(dhidden * n1)
    vectors[4:5, :] = col_sum(dhidden)
    scaled1 = dhidden * gain[0, 0:1, :]
    first = inv1 * (scaled1 - row_mean(scaled1) - n1 * row_mean(scaled1 * n1))
    dfirst[...] = first.astype(BF)
    masked = cols[0, :, 3:4] == 1
    vectors[5:6, :] = col_sum(jnp.where(masked, first, 0.0))
    vectors[6:8, :] = jnp.zeros((2, D), F32)


def put_pairs(ids, values, first_pair, rows, keep, send, span):
    upper = ids[0] & 1
    base = ids[0] >> 1
    for i in range(values.shape[0] // (2 * rows)):
        a = values[2 * rows * i : 2 * rows * i + rows]
        b = values[2 * rows * i + rows : 2 * rows * (i + 1)]
        rel = (first_pair + i) ^ base
        place = ((rel & 1) << 2) | (rel >> 1)
        keep[place, :, span] = jnp.where(upper == 0, a, b).astype(BF)
        send[place, :, span] = jnp.where(upper == 0, b, a).astype(BF)


def weight_grad_kernel(ids, left, right, keep, send, left_t):
    @pl.when(pl.program_id(0) == 0)
    def _():
        left_t[...] = left[...].T

    put_pairs(
        ids, mm(left_t[...], right[...]), 0, D // COARSE, keep, send, slice(0, right.shape[1])
    )


def backward_kernel(
    rows_per_step,
    heads,
    ids,
    cols,
    rows,
    emb,
    qkv,
    prob,
    ctx,
    wout,
    wqkv,
    first_own,
    first_peer,
    keep,
    send,
    demb,
    sums,
    mask_grad,
    idx_s,
    band_s,
    dctx_s,
    dctx_t,
    q_t,
    ds_s,
    dsb_s,
    dq_s,
    dk_t,
    dv_t,
):
    dmixed = (first_own[...].astype(F32) + first_peer[...].astype(F32)).astype(BF)
    dctx = mm_nt(dmixed, wout[0]).astype(BF)
    dctx_s[...] = dctx
    dctx_t[...] = dctx.T
    q_t[...] = qkv[0].T
    buckets = line_buckets(cols, rows)
    idx_s[...] = buckets
    band_s[...] = jnp.where((buckets > 0) & (buckets < REL_1D - 1), 1.0, 0.0).astype(BF)
    lane = iota((PAGE, 128), 1)
    hot_boxes = place_lanes(cols)
    hot_places = jnp.where((cols[0, :, 0:1] & 63) == lane - 64, 1.0, 0.0)
    hot_right = jnp.where(lane < 64, hot_boxes, hot_places).astype(BF)
    r = iota((64, PAGE), 0)
    box_code = jnp.where(r < REL_2D, rows[0, 1:2, :], rows[0, 2:3, :] + REL_2D)
    boxes_t = jnp.where(box_code == r, 1.0, 0.0).astype(BF)
    places_t = jnp.where((rows[0, 0:1, :] & 63) == r, 1.0, 0.0).astype(BF)
    b = iota((128, 128), 0)
    c = iota((128, 128), 1)
    box_at = (b & 31) + (c & 63) - 32
    box_index = jnp.clip(box_at, 0, 31) + jnp.where(b >= REL_2D, REL_2D, 0)
    place_index = 64 + ((b + c - 32) & 63)
    diagonal = jnp.where(b < 64, box_index, place_index)
    valid_box = (box_at >= 0) & (box_at < 32) & ((b >> 5) == (c >> 6))
    valid = jnp.where(
        b < 64, jnp.where(valid_box, 1.0, 0.0), jnp.where(c < 64, 1.0, 0.0)
    )
    for h in range(heads):
        head = slice(HD * h, HD * (h + 1))
        values = qkv[2, :, head]
        low_sum = jnp.zeros((1, PAGE), F32)
        for start in range(0, PAGE, rows_per_step):
            part = slice(start, start + rows_per_step)
            dprobs = mm_nt(dctx_s[part, head], values)
            weights = prob[h, part, :].astype(F32)
            product = weights * dprobs
            dscores = product - weights * row_sum(product)
            low = dscores.astype(BF)
            ds_s[part, :] = low
            dsb_s[part, :] = low * band_s[part, :]
            low_sum += col_sum(jnp.where(idx_s[part, :] == 0, low.astype(F32), 0.0))
        dq_s[:, head] = (mm(ds_s[...], qkv[1, :, head]) * HD ** (-0.5)).astype(BF)
        dv_t[head, :] = mm(dctx_t[head, :], prob[h]).astype(BF)
        left = jnp.concatenate([q_t[head, :], boxes_t], axis=0)
        both = mm(left, ds_s[...])
        dk_t[head, :] = both[:HD].astype(BF)
        first = jnp.concatenate([both[HD:], mm(places_t, dsb_s[...])], axis=0)
        high = first.astype(BF)
        rest = (first - high.astype(F32)).astype(BF)
        pairs = mm(high, hot_right) + mm(rest, hot_right)
        folded = valid * jnp.take_along_axis(pairs, diagonal, axis=1)
        sums[h, 0:1, :] = col_sum(folded[:64])
        line = col_sum(folded[64:])
        lane_row = iota((1, 128), 1)
        sums[h, 1:2, :] = jnp.where(lane_row == 0, row_sum(low_sum), line)
    if heads < sums.shape[0]:
        sums[heads:] = jnp.zeros((sums.shape[0] - heads, 2, 128), F32)
    width = heads * HD
    shard = (3 * D + 2 * width) // COARSE
    span = slice(0, width)
    emb_t = emb[...].T
    per = D // (2 * shard)
    put_pairs(ids, mm(emb_t, dq_s[...]), 0, shard, keep, send, span)
    put_pairs(ids, mm_nt(emb_t, dk_t[...]), per, shard, keep, send, span)
    put_pairs(ids, mm_nt(emb_t, dv_t[...]), 2 * per, shard, keep, send, span)
    out_grad = mm(ctx[...].T, dmixed)
    put_pairs(ids, out_grad[:, :width], 3 * per, shard, keep, send, span)
    put_pairs(ids, out_grad[:, width:], 3 * per + 1, shard, keep, send, span)
    part = mm_nt(dq_s[...], wqkv[0, 0])
    part += mm_nt(dk_t[...].T, wqkv[0, 1])
    part += mm_nt(dv_t[...].T, wqkv[0, 2])
    demb[...] = part.astype(BF)
    mask_grad[...] = col_sum(jnp.where(cols[0, :, 3:4] == 1, part, 0.0))


def unpack_kernel(ids, pieces_text, pieces_visual, qkv_grad, out_grad):
    width = pieces_text.shape[2]
    shard = pieces_text.shape[1]
    per = D // shard
    me = ids[0]
    for m, pieces in enumerate((pieces_text, pieces_visual)):
        for s in range(COARSE):
            rel = s ^ me
            place = ((rel & 1) << 3) | ((rel & 2) << 1) | (rel >> 2)
            block = pieces[place].astype(F32)
            if s < 3 * per:
                qkv_grad[m, s // per, shard * (s % per) : shard * (s % per + 1), :] = block
            else:
                half, at = divmod(s - 3 * per, 2)
                out_grad[m, shard * at : shard * (at + 1), width * half : width * (half + 1)] = block


def params():
    return pltpu.CompilerParams(vmem_limit_bytes=VMEM_BYTES)


def cost():
    return pl.CostEstimate(flops=1000, bytes_accessed=1000, transcendentals=0)


def after(value, *others):
    return lax.optimization_barrier((value,) + others)[0]


def at_modality(m, shape):
    zeros = (0,) * (len(shape) - 1)
    return pl.BlockSpec(shape, lambda *_: (m,) + zeros)


def at_own(shape):
    zeros = (0,) * (len(shape) - 1)
    return pl.BlockSpec(shape, lambda i, ids: (ids[1],) + zeros)


def whole(shape):
    zeros = (0,) * len(shape)
    return pl.BlockSpec(shape, lambda *_: zeros)


ANY = pl.BlockSpec(memory_space=pl.ANY)


def sds(shape, dtype):
    return jax.ShapeDtypeStruct(shape, dtype)


def attention_forward(m, heads, cols, rows, raw, membed, w_qkv, table, w_out, partial_sum):
    width = heads * HD
    has_partial = partial_sum is not None
    in_specs = [
        at_modality(m, (1, PAGE, 8)),
        at_modality(m, (1, 8, PAGE)),
        whole((PAGE, D)),
        at_modality(m, (1, 1, D)),
        at_modality(m, (1, 3, D, width)),
        whole((8, 128)),
        at_modality(m, (1, width, D)),
    ]
    args = [cols, rows, raw, membed, w_qkv, table, w_out]
    if has_partial:
        in_specs.append(whole((PAGE, D)))
        args.append(partial_sum)
    shapes = (
        ((PAGE, D), BF),
        ((3, PAGE, width), BF),
        ((heads, PAGE, PAGE), BF),
        ((PAGE, width), BF),
        ((PAGE, D), BF if has_partial else F32),
    )
    return pl.pallas_call(
        partial(forward_kernel, 256, heads, has_partial),
        grid=(1,),
        in_specs=in_specs,
        out_specs=tuple(whole(s) for s, _ in shapes),
        out_shape=tuple(sds(s, t) for s, t in shapes),
        scratch_shapes=[pltpu.VMEM((PAGE, PAGE), jnp.int32), pltpu.VMEM((PAGE, 128 * heads), BF)],
        cost_estimate=cost(),
        compiler_params=params(),
    )(*args)


def feed_forward(ids, cols, emb, att_own, att_peer, gain, shift, b_up, b_down, cots, own, recv):
    units = b_up.shape[1]
    up_own, down_own = own
    n_copies = 2 * (up_own.shape[2] // BLOCK + 4)
    shapes = (
        ((PAGE, D), BF),
        ((PAGE, D), BF),
        ((PAGE, units), BF),
        ((PAGE, units), BF),
        ((PAGE, D), BF),
        ((PAGE, D), BF),
        ((1, units), F32),
        ((8, D), F32),
    )
    rows_f32 = pltpu.VMEM((PAGE, D), F32)
    return pl.pallas_call(
        ffn_kernel,
        grid_spec=pltpu.PrefetchScalarGridSpec(
            num_scalar_prefetch=1,
            grid=(1,),
            in_specs=[
                at_own((1, PAGE, 8)),
                whole((PAGE, D)),
                whole((PAGE, D)),
                whole((PAGE, D)),
                at_own((1, 2, D)),
                at_own((1, 2, D)),
                whole((1, units)),
                at_own((1, 1, D)),
            ]
            + [ANY] * 10,
            out_specs=tuple(whole(s) for s, _ in shapes),
            scratch_shapes=[
                pltpu.VMEM((D, units), BF),
                pltpu.VMEM((units, D), BF),
                pltpu.VMEM((PAGE, D), BF),
                pltpu.VMEM((PAGE, units), F32),
                rows_f32,
                rows_f32,
                rows_f32,
                rows_f32,
                pltpu.SemaphoreType.DMA((n_copies,)),
                pltpu.SemaphoreType.DMA,
            ],
        ),
        out_shape=tuple(sds(s, t) for s, t in shapes),
        cost_estimate=cost(),
        compiler_params=params(),
    )(
        ids, cols, emb, att_own, att_peer, gain, shift, b_up, b_down, *cots, up_own, down_own, *recv
    )


def weight_grad(ids, left, right):
    units = right.shape[1]
    shape = (COARSE // 2, D // COARSE, units)
    spec = pl.BlockSpec((COARSE // 2, D // COARSE, BLOCK), lambda t, ids: (0, 0, t))
    return pl.pallas_call(
        weight_grad_kernel,
        grid_spec=pltpu.PrefetchScalarGridSpec(
            num_scalar_prefetch=1,
            grid=(units // BLOCK,),
            in_specs=[whole((PAGE, D)), pl.BlockSpec((PAGE, BLOCK), lambda t, ids: (0, t))],
            out_specs=(spec, spec),
            scratch_shapes=[pltpu.VMEM((D, PAGE), BF)],
        ),
        out_shape=(sds(shape, BF), sds(shape, BF)),
        cost_estimate=cost(),
        compiler_params=params(),
    )(ids, left, right)


def attention_backward(m, heads, ids, cols, rows, saved, w_out, w_qkv, first_own, first_peer):
    emb, qkv, prob, ctx = saved
    width = heads * HD
    shard = (3 * D + 2 * width) // COARSE
    shapes = (
        ((COARSE // 2, shard, width), BF),
        ((COARSE // 2, shard, width), BF),
        ((PAGE, D), BF),
        ((8, 2, 128), F32),
        ((1, D), F32),
    )
    square = pltpu.VMEM((PAGE, PAGE), BF)
    flat = pltpu.VMEM((PAGE, width), BF)
    tall = pltpu.VMEM((width, PAGE), BF)
    return pl.pallas_call(
        partial(backward_kernel, 256, heads),
        grid_spec=pltpu.PrefetchScalarGridSpec(
            num_scalar_prefetch=1,
            grid=(1,),
            in_specs=[
                at_modality(m, (1, PAGE, 8)),
                at_modality(m, (1, 8, PAGE)),
                whole(emb.shape),
                whole(qkv.shape),
                whole(prob.shape),
                whole(ctx.shape),
                at_modality(m, (1, width, D)),
                at_modality(m, (1, 3, D, width)),
                whole((PAGE, D)),
                whole((PAGE, D)),
            ],
            out_specs=tuple(whole(s) for s, _ in shapes),
            scratch_shapes=[
                pltpu.VMEM((PAGE, PAGE), jnp.int32),
                square,
                flat,
                tall,
                tall,
                square,
                square,
                flat,
                tall,
                tall,
            ],
        ),
        out_shape=tuple(sds(s, t) for s, t in shapes),
        cost_estimate=cost(),
        compiler_params=params(),
    )(ids, cols, rows, emb, qkv, prob, ctx, w_out, w_qkv, first_own, first_peer)


def unpack(ids, text, visual, heads):
    width = heads * HD
    shapes = ((2, 3, D, width), (2, width, D))
    return pl.pallas_call(
        unpack_kernel,
        grid_spec=pltpu.PrefetchScalarGridSpec(
            num_scalar_prefetch=1,
            grid=(1,),
            in_specs=[whole(text.shape), whole(visual.shape)],
            out_specs=tuple(whole(s) for s in shapes),
        ),
        out_shape=tuple(sds(s, F32) for s in shapes),
        cost_estimate=cost(),
        compiler_params=params(),
    )(ids, text, visual)


def bucket_fold():
    source = jnp.arange(256, dtype=jnp.int32)[:, None]
    bucket = jnp.arange(REL_1D + 2 * REL_2D, dtype=jnp.int32)[None, :]
    half = REL_2D // 2
    offset = jnp.clip((source & 63) - 32, -half, half - 1) + half
    plane = REL_1D + offset + jnp.where(source >= 64, REL_2D, 0)
    line = source - 128
    last = REL_1D - 1
    box_part = jnp.where(plane == bucket, 1.0, 0.0) + jnp.where(
        (source < 64) & (bucket == last), 1.0, 0.0
    )
    line_part = jnp.where((line < last) & (line == bucket), 1.0, 0.0) - jnp.where(
        (line < last) & (bucket == last), 1.0, 0.0
    )
    return jnp.where(source < 128, box_part, line_part).astype(F32)


def on_device(
    n_dp,
    text_rows,
    visual_rows,
    text_mask,
    visual_mask,
    text_places,
    text_boxes,
    visual_boxes,
    mask_embed,
    w_qkv,
    w_out,
    rel_table,
    ln_gain,
    ln_bias,
    w_up,
    b_up,
    w_down,
    b_down,
    text_cotangent,
    visual_cotangent,
):
    heads = rel_table.shape[1]
    half_units = w_up.shape[2]
    quarter = half_units // 4
    dp = lax.axis_index("dp")
    mp = lax.axis_index("mp")
    bits = n_dp.bit_length() - 1
    fine_bits = bits - 4
    me = dp >> fine_bits
    q = dp & 3
    ids = jnp.stack([me, mp, q]).astype(jnp.int32)

    def swap(x, flip):
        return lax.ppermute(x, "dp", [(i, i ^ flip) for i in range(n_dp)])

    def cross(x):
        return lax.ppermute(x, "mp", [(0, 1), (1, 0)])

    up_y = cross(lax.dynamic_slice(w_up, (1 - mp, 0, quarter * q), (1, D, quarter))[0])
    down_y = cross(lax.dynamic_slice(w_down, (1 - mp, quarter * q, 0), (1, quarter, D))[0])
    bias_peer = cross(lax.dynamic_slice(b_up, (1 - mp, 0), (1, half_units)))
    b_up_all = jnp.concatenate(
        [lax.dynamic_slice(b_up, (mp, 0), (1, half_units)), bias_peer], axis=1
    )

    visual_places = jnp.arange(PAGE, dtype=jnp.int32)
    zero = jnp.zeros((PAGE,), jnp.int32)
    rows = jnp.stack(
        [
            jnp.stack(
                [text_places, text_boxes[:, 0], text_boxes[:, 1], text_mask] + [zero] * 4
            ),
            jnp.stack(
                [visual_places, visual_boxes[:, 0], visual_boxes[:, 1], visual_mask] + [zero] * 4
            ),
        ]
    )
    cols = jnp.transpose(rows, (0, 2, 1))
    table = jnp.pad(rel_table.T, ((0, 8 - heads), (0, 0)))
    membed = mask_embed.reshape(2, 1, D)
    forward = partial(attention_forward, heads=heads, cols=cols, rows=rows, membed=membed)
    forward = partial(forward, w_qkv=w_qkv, table=table, w_out=w_out)
    *saved_text, att_text = forward(0, raw=text_rows, partial_sum=None)
    up_x = swap(after(up_y, att_text), 2)
    *saved_visual, att = forward(1, raw=visual_rows, partial_sum=att_text)
    att_peer = cross(att)
    down_x = swap(after(down_y, att), 2)
    up_c = swap(jnp.stack([up_y, up_x]), 1)
    down_c = swap(jnp.stack([down_y, down_x]), 1)

    emb_own = jnp.where(mp == 0, saved_text[0], saved_visual[0])
    out, first_own, act, dpre, hid_low, dlow, bup_grad, vectors = feed_forward(
        ids,
        cols,
        emb_own,
        att,
        att_peer,
        ln_gain,
        ln_bias,
        b_up_all,
        b_down.reshape(2, 1, D),
        (text_cotangent, visual_cotangent),
        (w_up, w_down),
        (up_y, up_x, up_c, down_y, down_x, down_c),
    )
    first_peer = cross(first_own)

    f0 = 1 << fine_bits

    def sum_x(keep, r1):
        n = keep.shape[0] // 2
        return (keep[n:].astype(F32) + r1[n:].astype(F32)).astype(BF)

    def part_z(keep, r1, r2, j):
        return keep[j].astype(F32) + r1[j].astype(F32) + r2[j].astype(F32)

    def parts_z(keep, r1, r2):
        return [part_z(keep, r1, r2, j).astype(BF) for j in (1, 2, 3)]

    def swap_z(parts):
        return [swap(part, 4 * j * f0) for j, part in zip((1, 2, 3), parts)]

    def after_all(values, others):
        return lax.optimization_barrier((tuple(values), others))[0]

    def sum_z(keep, r1, r2, got):
        total = part_z(keep, r1, r2, 0)
        for g in got:
            total = total + g.astype(F32)
        for b in range(fine_bits):
            total = total + swap(total, 1 << b)
        return total

    def gather_z(piece):
        return jnp.stack([piece] + [swap(piece, 4 * j * f0) for j in (1, 2, 3)])

    def own_rows(total):
        count = D // n_dp
        return lax.dynamic_slice(total, (count * (dp & (f0 - 1)), 0), (count, total.shape[1]))

    def both(total):
        own = total[:, :half_units]
        peer = cross(total[:, half_units:].astype(BF)).astype(F32)
        return jnp.stack([jnp.where(mp == 0, own, peer), jnp.where(mp == 0, peer, own)])

    backward = partial(attention_backward, heads=heads, ids=ids, cols=cols, rows=rows)
    backward = partial(backward, w_out=w_out, w_qkv=w_qkv, first_own=first_own)

    def small_sums(sums_t, sums_v, mask_t, mask_v):
        sums = (sums_t + sums_v)[:heads].reshape(heads, 256)
        table_grad = jnp.dot(
            sums, bucket_fold(), precision=lax.Precision.HIGHEST, preferred_element_type=F32
        )
        small = jnp.concatenate(
            [
                bup_grad[0],
                vectors[:6].reshape(-1),
                table_grad.reshape(-1),
                mask_t[0],
                mask_v[0],
            ]
        ).reshape(8, -1)
        return small

    dn_keep, dn_send = weight_grad(ids, dlow, act)
    dn_1 = swap(dn_send, f0)
    up_keep, up_send = weight_grad(ids, after(hid_low, dn_send), dpre)
    up_1 = swap(up_send, f0)
    dn_half = sum_x(dn_keep, after(dn_1, up_send))
    dn_2 = swap(dn_half, 2 * f0)
    up_half = sum_x(up_keep, after(up_1, dn_half))
    first_peer = after(first_peer, up_half)
    t_keep, t_send, demb_t, sums_t, mask_t = backward(0, saved=saved_text, first_peer=first_peer)
    t_1 = swap(t_send, f0)
    demb_t_peer = cross(demb_t)
    v_keep, v_send, demb_v, sums_v, mask_v = backward(
        1, saved=saved_visual, first_peer=after(first_peer, t_send)
    )
    v_1 = swap(v_send, f0)
    demb_v_peer = cross(demb_v)
    dn_2 = after(dn_2, v_send)
    t_half = sum_x(t_keep, after(t_1, dn_2))
    t_2 = swap(t_half, 2 * f0)
    v_half = sum_x(v_keep, after(v_1, t_half))
    v_2 = swap(v_half, 2 * f0)
    dn_parts = parts_z(dn_keep, dn_1, after(dn_2, v_half))
    dn_z = swap_z(dn_parts)
    up_2 = swap(after(up_half, *dn_parts), 2 * f0)
    small = small_sums(sums_t, sums_v, mask_t, mask_v)
    stages = [1 << b for b in range(bits)]
    small_got = swap(after(small, *dn_parts), stages[0])
    out_peer = cross(after(out, v_send))
    t_parts = parts_z(t_keep, t_1, after(t_2, *dn_parts))
    t_z = swap_z(t_parts)
    small = small + after(small_got, *t_parts)
    small_got = swap(small, stages[1])
    v_parts = parts_z(v_keep, v_1, after(v_2, *t_parts))
    v_z = swap_z(v_parts)
    small = small + after(small_got, *v_parts)
    small_got = swap(small, stages[2])
    dn_total = own_rows(sum_z(dn_keep, dn_1, dn_2, after_all(dn_z, v_parts)))
    t_piece = sum_z(t_keep, t_1, t_2, after_all(t_z, dn_total)).astype(BF)
    t_four = gather_z(t_piece)
    small = small + after(small_got, t_piece)
    small_got = swap(small, stages[3])
    v_piece = sum_z(v_keep, v_1, v_2, after_all(v_z, t_piece)).astype(BF)
    v_four = gather_z(v_piece)
    small = small + after(small_got, v_piece)
    for stage in stages[4:]:
        small = small + swap(small, stage)
    small_other = cross(small)
    t_four = after(t_four, v_piece)
    t_four_x = swap(t_four, 2 * f0)
    v_four = after(v_four, t_four)
    v_four_x = swap(v_four, 2 * f0)
    up_parts = parts_z(up_keep, up_1, after(up_2, v_four))
    up_z = swap_z(up_parts)
    t_eight = jnp.concatenate([t_four, after(t_four_x, *up_parts)])
    t_eight_c = swap(t_eight, f0)
    v_eight = jnp.concatenate([v_four, after(v_four_x, t_eight)])
    v_eight_c = swap(v_eight, f0)
    up_total = own_rows(sum_z(up_keep, up_1, up_2, after_all(up_z, v_eight)))
    demb_t_peer = after(demb_t_peer, t_piece)
    demb_v_peer = after(demb_v_peer, v_piece)
    out_peer = after(out_peer, v_four)
    w_up_grad = both(up_total)
    w_down_grad = jnp.transpose(both(dn_total), (0, 2, 1))
    w_qkv_grad, w_out_grad = unpack(
        ids,
        jnp.concatenate([t_eight, t_eight_c]),
        jnp.concatenate([v_eight, v_eight_c]),
        heads,
    )

    def input_grad(m, part, part_peer, mask):
        first = jnp.where(mp == m, first_own, first_peer).astype(F32)
        total = first + (part.astype(F32) + part_peer.astype(F32))
        return jnp.where(mask[:, None] == 1, 0.0, total).astype(BF)

    text_grad = input_grad(0, demb_t, demb_t_peer, text_mask)
    visual_grad = input_grad(1, demb_v, demb_v_peer, visual_mask)
    text_out = jnp.where(mp == 0, out, out_peer)
    visual_out = jnp.where(mp == 0, out_peer, out)

    other = small_other.reshape(-1)
    small = small.reshape(-1)
    units = 2 * half_units
    at = units + 6 * D
    end = at + rel_table.size
    mask_both = (small[end:] + other[end:]).reshape(2, D)
    first_slot = jnp.where(mp == 0, small, other)
    second_slot = jnp.where(mp == 0, other, small)
    own_bup = small[:units]
    other_bup = jnp.concatenate([other[half_units:units], other[:half_units]])
    slot_vectors = jnp.stack([first_slot[units:at], second_slot[units:at]]).reshape(2, 6, D)
    mask_total = mask_both + slot_vectors[:, 5]
    gain_grad = jnp.stack([slot_vectors[:, 3], slot_vectors[:, 1]], axis=1)
    shift_grad = jnp.stack([slot_vectors[:, 4], slot_vectors[:, 2]], axis=1)
    rel_grad = small[at:end].reshape(heads, -1).T
    per = half_units // n_dp
    own_bup = lax.dynamic_slice(own_bup, (per * dp,), (per,))
    other_bup = lax.dynamic_slice(other_bup, (per * dp,), (per,))
    b_up_grad = jnp.stack(
        [jnp.where(mp == 0, own_bup, other_bup), jnp.where(mp == 0, other_bup, own_bup)]
    )
    count = D // n_dp
    b_down_grad = lax.dynamic_slice(slot_vectors[:, 0], (0, count * dp), (2, count))
    return (
        text_out,
        visual_out,
        text_grad,
        visual_grad,
        mask_total,
        w_qkv_grad,
        w_out_grad,
        rel_grad,
        gain_grad,
        shift_grad,
        w_up_grad,
        b_up_grad,
        w_down_grad,
        b_down_grad,
    )


def solution(mesh):
    in_specs = (
        P("dp", None),
        P("dp", None),
        P("dp"),
        P("dp"),
        P("dp"),
        P("dp", None),
        P("dp", None),
        P(),
        P(None, None, None, "mp"),
        P(None, "mp", None),
        P(None, "mp"),
        P(),
        P(),
        P(None, None, "mp"),
        P(None, "mp"),
        P(None, "mp", None),
        P(),
        P("dp", None),
        P("dp", None),
    )
    out_specs = (
        P("dp", None),
        P("dp", None),
        P("dp", None),
        P("dp", None),
        P(),
        P(None, None, None, "mp"),
        P(None, "mp", None),
        P(None, "mp"),
        P(),
        P(),
        P(None, "dp", "mp"),
        P(None, ("mp", "dp")),
        P(None, "mp", "dp"),
        P(None, "dp"),
    )
    return jax.shard_map(
        partial(on_device, mesh.shape["dp"]),
        mesh=mesh,
        in_specs=in_specs,
        out_specs=out_specs,
        check_vma=False,
    )
```

```python
from functools import partial

import jax
import jax.numpy as jnp
from jax import lax
from jax.experimental import pallas as pl
from jax.experimental.pallas import tpu as pltpu
from jax.sharding import PartitionSpec as P

D = 768
HD = 64
PAGE = 512
REL_1D = 64
REL_2D = 32
COARSE = 16
BLOCK = 768
BF = jnp.bfloat16
F32 = jnp.float32
CLAIM = 20_000_000_000
WIDE = 60


def mm(a, b):
    return lax.dot_general(a, b, (((1,), (0,)), ((), ())), preferred_element_type=F32)


def mm_nt(a, b):
    return lax.dot_general(a, b, (((1,), (1,)), ((), ())), preferred_element_type=F32)


def iota(shape, dim):
    return lax.broadcasted_iota(jnp.int32, shape, dim)


def row_sum(x):
    return jnp.sum(x, axis=-1, keepdims=True)


def row_mean(x):
    return jnp.mean(x, axis=-1, keepdims=True)


def col_sum(x):
    return jnp.sum(x, axis=0, keepdims=True)


def start_all(pairs, sems, first=0):
    copies = []
    for i, (source, target) in enumerate(pairs):
        copy = pltpu.make_async_copy(source, target, sems.at[first + i])
        copy.start()
        copies.append(copy)
    return copies


def wait_all(copies):
    for copy in copies:
        copy.wait()


def line_buckets(cols, rows):
    half = REL_1D // 2
    return jnp.clip(cols[:, 0:1] - rows[0:1, :], -half, half - 1) + half


def place_lanes(cols):
    lane = iota((PAGE, 128), 1)
    code = lane & 63
    across = jnp.broadcast_to(cols[:, 1:2], (PAGE, 128))
    down = jnp.broadcast_to(cols[:, 2:3], (PAGE, 128)) + REL_2D
    return jnp.where(jnp.where(code < REL_2D, across, down) == code, 1.0, 0.0)


def table_plane(table_row):
    b = iota((128, 128), 0)
    lane = iota((128, 128), 1)
    c = lane & 63
    half = REL_2D // 2
    shift = jnp.clip((c & 31) - (b & 31), -half, half - 1) + half + REL_1D
    index = jnp.where(c >= REL_2D, shift + REL_2D, shift)
    spread = jnp.broadcast_to(table_row, (128, 128))
    values = jnp.take_along_axis(spread, index, axis=1)
    values = jnp.where((b >> 5) == (c >> 5), values, 0.0)
    high = values.astype(BF).astype(F32)
    return jnp.where(lane < 64, high, values - high).astype(BF)


def forward_kernel(
    m, heads, has_partial, places, boxes, mask, membed, table, raw, wqkv, wout, *refs
):
    if has_partial:
        partial_ref, refs = refs[0], refs[1:]
    outputs, att, refs = refs[:7], refs[7], refs[8:]
    places_s, boxes_s, mask_s, membed_s, table_s, raw_s, wqkv_s, wout_s = refs[:8]
    emb_s, qkv_s, expo_s, ctx_s, inverse_s, cols_s, rows_s = refs[8:15]
    att_s, idx_s, bias_s, v_t, in_sems, out_sems = refs[15:]
    emb, qkv, expo, ctx_t, inverse, cols, rows = outputs
    sources = (places, boxes, mask, membed, table, raw, wqkv.at[m], wout.at[m])
    loads = start_all(list(zip(sources, refs[:8])), in_sems)
    wait_all(loads[:6])
    row_id = iota((8, PAGE), 0)
    place_row = jnp.broadcast_to(places_s[...], (8, PAGE))
    mask_row = jnp.where(row_id == 3, jnp.broadcast_to(mask_s[...], (8, PAGE)), 0)
    facts = jnp.where(row_id == 0, place_row, mask_row).astype(F32)
    turned = boxes_s[...].astype(F32)
    facts = jnp.where(row_id == 1, turned[0:1, :], facts)
    facts = jnp.where(row_id == 2, turned[1:2, :], facts)
    rows_s[...] = facts.astype(jnp.int32)
    cols_s[...] = facts.T.astype(jnp.int32)
    masked = cols_s[:, 3:4] == 1
    filler = membed_s[m : m + 1, :].astype(F32)
    embedded = jnp.where(masked, filler, raw_s[...].astype(F32)).astype(BF)
    emb_s[...] = embedded
    stores = start_all([(emb_s, emb), (cols_s, cols), (rows_s, rows)], out_sems)
    loads[6].wait()
    qkv_s[0] = (mm(embedded, wqkv_s[0]) * HD ** (-0.5)).astype(BF)
    qkv_s[1] = mm(embedded, wqkv_s[1]).astype(BF)
    values = mm(embedded, wqkv_s[2]).astype(BF)
    qkv_s[2] = values
    v_t[...] = values.T
    stores += start_all([(qkv_s, qkv)], out_sems, 3)
    idx_s[...] = line_buckets(cols_s, rows_s)
    onehot = place_lanes(cols_s).astype(BF)
    planes = jnp.concatenate([table_plane(table_s[h : h + 1, :]) for h in range(heads)], axis=1)
    bias_s[...] = mm(onehot, planes).astype(BF)
    inverse_s[...] = jnp.zeros((8, PAGE), F32)
    for h in range(heads):
        head = slice(HD * h, HD * (h + 1))
        keys = jnp.concatenate([onehot, qkv_s[1, :, head]], axis=1)
        queries = jnp.concatenate(
            [bias_s[:, 128 * h : 128 * (h + 1)], qkv_s[0, :, head]], axis=1
        )
        spread = jnp.broadcast_to(table_s[h : h + 1, :], (PAGE, 128))
        line = [
            jnp.take_along_axis(spread, idx_s[:, 128 * b : 128 * (b + 1)], axis=1)
            for b in range(PAGE // 128)
        ]
        scores = mm_nt(keys, queries) + jnp.concatenate(line, axis=1)
        exponent = jnp.exp(scores - jnp.max(scores, axis=0, keepdims=True))
        scale = 1.0 / col_sum(exponent)
        inverse_s[h : h + 1, :] = scale
        expo_s[h] = exponent.astype(BF)
        stores += start_all([(expo_s.at[h], expo.at[h])], out_sems, 4 + h)
        ctx_s[head, :] = (mm(v_t[head, :], expo_s[h]) * scale).astype(BF)
    stores += start_all([(ctx_s, ctx_t), (inverse_s, inverse)], out_sems, 4 + heads)
    loads[7].wait()
    attended = mm(ctx_s[...].T, wout_s[...])
    if has_partial:
        att_s[...] = (partial_ref[...] + attended).astype(BF)
        stores += start_all([(att_s, att)], out_sems, 6 + heads)
    else:
        att[...] = attended
    wait_all(stores)


def gelu_both(x):
    z = jnp.abs(x)
    t = 1.0 / (1.0 + (0.3275911 * 0.5**0.5) * z)
    poly = t * (
        0.127414796
        + t * (-0.142248368 + t * (0.7107068705 + t * (-0.7265760135 + t * 0.5307027145)))
    )
    bell = jnp.exp(-0.5 * x * x)
    tail = poly * bell
    phi = jnp.where(x >= 0, 1.0 - tail, tail)
    return x * phi, phi + x * bell * 0.3989422804014327


def copy_list(ids, up_own, down_own, up_recv, down_recv, up_s, down_s, sems):
    mp, q = ids[1], ids[2]
    half = up_own.shape[2]
    quarter = half // 4
    copies = []
    for t in range(half // BLOCK):
        span = slice(BLOCK * t, BLOCK * (t + 1))
        copies.append((up_own.at[mp, :, span], up_s.at[:, span]))
    for j in range(4):
        place = pl.multiple_of(half + quarter * (q ^ j), 128)
        copies.append((up_recv[j], up_s.at[:, pl.ds(place, quarter)]))
    for t in range(half // BLOCK):
        span = slice(BLOCK * t, BLOCK * (t + 1))
        copies.append((down_own.at[mp, span, :], down_s.at[span, :]))
    for j in range(4):
        place = pl.multiple_of(half + quarter * (q ^ j), 128)
        copies.append((down_recv[j], down_s.at[pl.ds(place, quarter), :]))
    return [pltpu.make_async_copy(a, b, sems.at[i]) for i, (a, b) in enumerate(copies)]


def ffn_kernel(
    ids,
    cols_text,
    cols_visual,
    emb_text,
    emb_visual,
    cot_text,
    cot_visual,
    att_own,
    att_peer,
    gain_both,
    shift_both,
    b_up_own,
    b_up_peer,
    b_down_both,
    up_own,
    down_own,
    uy,
    ux,
    uc,
    ud,
    dy,
    dx,
    dc,
    dd,
    out,
    dfirst,
    act,
    dpre,
    hid_low,
    dlow,
    small,
    up_s,
    down_s,
    slope_s,
    norm1,
    hidden,
    work,
    dcomb,
    out_s,
    dfirst_s,
    cols,
    emb,
    cot_s,
    att_own_s,
    att_peer_s,
    gain_s,
    shift_s,
    b_up_both,
    b_up_far,
    b_down_s,
    b_up,
    sems,
    own_sems,
    out_sems,
):
    mp = ids[1]
    text = mp == 0
    plain = start_all(
        [
            (att_own, att_own_s),
            (att_peer, att_peer_s),
            (gain_both, gain_s),
            (shift_both, shift_s),
            (b_up_own, b_up_both),
            (b_up_peer, b_up_far),
            (b_down_both, b_down_s),
        ],
        own_sems,
    )
    at = len(plain)

    @pl.when(text)
    def _():
        start_all([(emb_text, emb), (cols_text, cols), (cot_text, cot_s)], own_sems, at)

    @pl.when(mp != 0)
    def _():
        start_all([(emb_visual, emb), (cols_visual, cols), (cot_visual, cot_s)], own_sems, at)

    chosen = [
        pltpu.make_async_copy(a, b, own_sems.at[at + i])
        for i, (a, b) in enumerate([(emb_text, emb), (cols_text, cols), (cot_text, cot_s)])
    ]
    up_recv = (uy, uc, ux, ud)
    down_recv = (dy, dc, dx, dd)
    copies = copy_list(ids, up_own, down_own, up_recv, down_recv, up_s, down_s, sems)
    n_own = up_own.shape[2] // BLOCK
    per_side = n_own + 4
    for i in range(n_own):
        copies[i].start()
        copies[per_side + i].start()
    for i in range(n_own, per_side):
        copies[i].start()
        copies[per_side + i].start()
    wait_all(plain)
    wait_all(chosen)
    half_units = b_up_own.shape[1]
    b_up[:, :half_units] = jnp.where(text, b_up_both[0:1, :], b_up_both[1:2, :])
    b_up[:, half_units:] = b_up_far[...]
    gain = jnp.where(text, gain_s[0], gain_s[1])
    shift = jnp.where(text, shift_s[0], shift_s[1])
    b_down = jnp.where(text, b_down_s[0:1, :], b_down_s[1:2, :])
    total = emb[...].astype(F32) + (att_own_s[...].astype(F32) + att_peer_s[...].astype(F32))
    centred = total - row_mean(total)
    inv1 = lax.rsqrt(row_mean(centred * centred) + 1e-05)
    n1 = centred * inv1
    norm1[...] = n1
    hid = n1 * gain[0:1, :] + shift[0:1, :]
    hidden[...] = hid
    hid_low[...] = hid.astype(BF)
    n_blocks = up_s.shape[1] // BLOCK
    for t in range(n_blocks):
        if t < n_own:
            copies[t].wait()
            copies[per_side + t].wait()
        elif t == n_own:
            for i in range(n_own, per_side):
                copies[i].wait()
                copies[per_side + i].wait()
        span = slice(BLOCK * t, BLOCK * (t + 1))
        pre = mm(hid_low[...], up_s[:, span]) + b_up[:, span]
        value, slope = gelu_both(pre)
        act[:, span] = value.astype(BF)
        slope_s[:, span] = slope
        down = mm(act[:, span], down_s[span, :])
        if t == 0:
            work[...] = down
        else:
            work[...] += down
    combined = hidden[...] + work[...] + b_down
    centred2 = combined - row_mean(combined)
    inv2 = lax.rsqrt(row_mean(centred2 * centred2) + 1e-05)
    n2 = centred2 * inv2
    out_s[...] = (n2 * gain[1:2, :] + shift[1:2, :]).astype(BF)
    stores = start_all([(out_s, out)], out_sems)
    cot = cot_s[...].astype(F32)
    small[5:6, :] = col_sum(cot * n2)
    small[6:7, :] = col_sum(cot)
    scaled = cot * gain[1:2, :]
    back = inv2 * (scaled - row_mean(scaled) - n2 * row_mean(scaled * n2))
    dcomb[...] = back
    small[4:5, :] = col_sum(back)
    dlow[...] = back.astype(BF)
    for t in range(n_blocks):
        span = slice(BLOCK * t, BLOCK * (t + 1))
        dact = mm_nt(dlow[...], down_s[span, :])
        low = (dact * slope_s[:, span]).astype(BF)
        dpre[:, span] = low
        small[t : t + 1, :] = col_sum(low.astype(F32))
        dhid = mm_nt(low, up_s[:, span])
        if t == 0:
            work[...] = dhid
        else:
            work[...] += dhid
    dhidden = dcomb[...] + work[...]
    n1 = norm1[...]
    small[7:8, :] = col_sum(dhidden * n1)
    small[8:9, :] = col_sum(dhidden)
    scaled1 = dhidden * gain[0:1, :]
    first = inv1 * (scaled1 - row_mean(scaled1) - n1 * row_mean(scaled1 * n1))
    dfirst_s[...] = first.astype(BF)
    stores += start_all([(dfirst_s, dfirst)], out_sems, 1)
    masked = cols[:, 3:4] == 1
    small[9:10, :] = col_sum(jnp.where(masked, first, 0.0))
    small[10:24, :] = jnp.zeros((14, D), F32)
    wait_all(stores)


def place_of(rel, z_first):
    x, low, high = rel & 1, (rel >> 1) & 1, rel >> 2
    if z_first:
        return (low << 2) | (high << 1) | x
    return (x << 2) | (low << 1) | high


def put_pairs(ids, values, rows, at, keep, send, span, z_first=False):
    upper = ids[0] & 1
    base = ids[0] >> 1
    spot = slice(at, at + rows)
    for i in range(values.shape[0] // (2 * rows)):
        a = values[2 * rows * i : 2 * rows * i + rows].astype(F32)
        b = values[2 * rows * i + rows : 2 * rows * (i + 1)].astype(F32)
        place = place_of(i ^ base, z_first)
        keep[place, spot, span] = jnp.where(upper == 0, a, b).astype(BF)
        send[place, spot, span] = jnp.where(upper == 0, b, a).astype(BF)


def weight_grad_kernel(z_first, ids, left, right, keep, send, keep_s, send_s, sems):
    left_t = left[...].T
    copies = []
    for t in range(right.shape[1] // BLOCK):
        span = slice(BLOCK * t, BLOCK * (t + 1))
        product = mm(left_t, right[:, span])
        put_pairs(ids, product, D // COARSE, 0, keep_s, send_s, span, z_first)
        for i, (source, target) in enumerate(((keep_s, keep), (send_s, send))):
            copy = pltpu.make_async_copy(
                source.at[:, :, span], target.at[:, :, span], sems.at[2 * t + i]
            )
            copy.start()
            copies.append(copy)
    for copy in copies:
        copy.wait()


def add_row(small, before, row, half, values):
    span = slice(128 * half, 128 * (half + 1))
    small[row : row + 1, span] = before[row : row + 1, span] + values


def backward_kernel(modality, heads, ids, *refs):
    n_in = 10 if modality == 0 else 9
    inputs, (dmixed_ref, before), refs = refs[:n_in], refs[n_in : n_in + 2], refs[n_in + 2 :]
    (keep, send, demb, small), refs = refs[:4], refs[4:]
    local, refs = refs[:n_in], refs[n_in:]
    cols, rows, inverse, wout, qkv, ctx_t, expo, emb, wqkv = local[:9]
    keep_s, send_s, demb_s, idx_s, band_s, dctx, dctx_t, k_t, ds_s, dsb_s, dq_t, dk, dv = refs[:13]
    grads_s, hist_s, low_s, in_sems, out_sems = refs[13:]
    sources = list(inputs)
    sources[3] = sources[3].at[modality]
    sources[8] = sources[8].at[modality]
    pairs = []
    for i, (source, target) in enumerate(zip(sources, local)):
        if i == 6:
            pairs += [(source.at[h], target.at[h]) for h in range(heads)]
        else:
            pairs.append((source, target))
    loads = start_all(pairs, in_sems)
    wait_all(loads[:4])
    small[...] = before[...]
    dmixed = dmixed_ref[...]
    back = mm_nt(wout[...], dmixed)
    for h in range(heads):
        head = slice(HD * h, HD * (h + 1))
        dctx_t[head, :] = (back[HD * h : HD * (h + 1)] * inverse[h : h + 1, :]).astype(BF)
    dctx[...] = dctx_t[...].T
    buckets = line_buckets(cols, rows)
    idx_s[...] = buckets
    band_s[...] = jnp.where((buckets > 0) & (buckets < REL_1D - 1), 1.0, 0.0).astype(BF)
    lane = iota((PAGE, 128), 1)
    hot_boxes = place_lanes(cols)
    hot_places = jnp.where((cols[:, 0:1] & 63) == lane - 64, 1.0, 0.0)
    hot_right = jnp.where(lane < 64, hot_boxes, hot_places).astype(BF)
    r = iota((64, PAGE), 0)
    box_code = jnp.where(r < REL_2D, rows[1:2, :], rows[2:3, :] + REL_2D)
    boxes_t = jnp.where(box_code == r, 1.0, 0.0).astype(BF)
    places_t = jnp.where((rows[0:1, :] & 63) == r, 1.0, 0.0).astype(BF)
    b = iota((128, 128), 0)
    c = iota((128, 128), 1)
    box_at = (b & 31) - (c & 63) + 32
    box_index = jnp.clip(box_at, 0, 31) + jnp.where(b >= REL_2D, REL_2D, 0)
    place_index = 64 + ((b - c + 32) & 63)
    diagonal = jnp.where(b < 64, box_index, place_index)
    valid_box = (box_at >= 0) & (box_at < 32) & ((b >> 5) == (c >> 6))
    valid = jnp.where(
        b < 64, jnp.where(valid_box, 1.0, 0.0), jnp.where(c < 64, 1.0, 0.0)
    )
    lane_row = iota((1, 128), 1)
    wait_all(loads[4:6])
    k_t[...] = qkv[1].T
    overlap = back * ctx_t[...].astype(F32)
    shared = jnp.concatenate(
        [col_sum(overlap[HD * h : HD * (h + 1)]) for h in range(heads)], axis=0
    )
    shared = shared * inverse[0:heads, :]
    for h in range(heads):
        head = slice(HD * h, HD * (h + 1))
        loads[6 + h].wait()
        turn = h % 2
        dprobs = mm(qkv[2, :, head], dctx_t[head, :])
        low = (expo[h].astype(F32) * (dprobs - shared[h : h + 1, :])).astype(BF)
        ds_s[turn] = low
        dsb_s[turn] = low * band_s[...]
        low_s[h : h + 1, :] = col_sum(jnp.where(idx_s[...] == 0, low.astype(F32), 0.0))
        both = mm(jnp.concatenate([k_t[head, :], boxes_t], axis=0), ds_s[turn])
        dq_t[head, :] = (both[:HD] * HD ** (-0.5)).astype(BF)
        hist_s[h, 0:64, :] = both[HD:]
        hist_s[h, 64:128, :] = mm(places_t, dsb_s[turn])
        dk[:, head] = mm(ds_s[turn], qkv[0, :, head]).astype(BF)
        dv[:, head] = mm(expo[h], dctx[:, head]).astype(BF)
    first = hist_s[...].reshape(128 * heads, PAGE)
    high = first.astype(BF)
    rest = (first - high.astype(F32)).astype(BF)
    pairs = mm(high, hot_right) + mm(rest, hot_right)
    for h in range(heads):
        mine = pairs[128 * h : 128 * (h + 1)]
        folded = valid * jnp.take_along_axis(mine, diagonal, axis=1)
        add_row(small, before, 12 + h, 0, col_sum(folded[:64]))
        line = col_sum(folded[64:])
        tail = row_sum(low_s[h : h + 1, :])
        add_row(small, before, 12 + h, 1, jnp.where(lane_row == 0, tail, line))
    width = heads * HD
    span = slice(0, width)
    wait_all(loads[6 + heads :])
    emb_t = emb[...].T
    grads_s[0:D, :] = mm_nt(emb_t, dq_t[...]).astype(BF)
    grads_s[D : 2 * D, :] = mm(emb_t, dk[...]).astype(BF)
    grads_s[2 * D : 3 * D, :] = mm(emb_t, dv[...]).astype(BF)
    rows_qkv = 3 * D // COARSE
    rows_out = 2 * width // COARSE
    put_pairs(ids, grads_s[...], rows_qkv, 0, keep_s, send_s, span)
    for i, context in enumerate((ctx_t, local[9]) if modality == 0 else ()):
        out_grad = mm(context[...], dmixed)
        grads_s[0:width, :] = out_grad[:, :width].astype(BF)
        grads_s[width : 2 * width, :] = out_grad[:, width:].astype(BF)
        at = rows_qkv + rows_out * i
        put_pairs(ids, grads_s[0 : 2 * width, :], rows_out, at, keep_s, send_s, span)
    stores = start_all([(send_s, send), (keep_s, keep)], out_sems)
    part = mm_nt(dq_t[...].T, wqkv[0])
    part += mm_nt(dk[...], wqkv[1])
    part += mm_nt(dv[...], wqkv[2])
    demb_s[...] = part.astype(BF)
    stores += start_all([(demb_s, demb)], out_sems, 2)
    mask_row = col_sum(jnp.where(cols[:, 3:4] == 1, part, 0.0))
    small[10 + modality : 11 + modality, :] = before[10 + modality : 11 + modality, :] + mask_row
    wait_all(stores)


def mix_kernel(own, peer, dmixed):
    dmixed[...] = (own[...].astype(F32) + peer[...].astype(F32)).astype(BF)


def unpack_kernel(modality, ids, *refs):
    sources, (qkv_grad, out_grad, stage, sems) = refs[:4], refs[-4:]
    rows, width = sources[0].shape[1:]
    rows_qkv = 3 * D // COARSE
    rows_out = 2 * width // COARSE
    per_half = COARSE // 2
    count = 1 + (rows - rows_qkv) // rows_out
    me = ids[0]
    copies = []
    for group, source in enumerate(sources):
        for at in range(4):
            slot = 4 * group + at
            stage[slot] = source[at].astype(F32)
            rel = (group >> 1) | ((group & 1) << 1) | ((at >> 1) << 2) | ((at & 1) << 3)
            s = rel ^ me
            spot = pl.ds(pl.multiple_of(rows_qkv * s, 8), rows_qkv)
            targets = [qkv_grad.at[modality, spot, :]]
            low = pl.ds(pl.multiple_of(rows_out * (s & (per_half - 1)), 8), rows_out)
            half = pl.ds(pl.multiple_of(width * (s // per_half), 128), width)
            for m in range(count - 1):
                targets.append(out_grad.at[m, low, half])
            start = 0
            for i, target in enumerate(targets):
                size = rows_qkv if i == 0 else rows_out
                copy = pltpu.make_async_copy(
                    stage.at[slot, pl.ds(start, size), :], target, sems.at[count * slot + i]
                )
                copy.start()
                copies.append(copy)
                start += size
    for copy in copies:
        copy.wait()


def fold_matrix():
    bucket = iota((128, 256), 0)
    source = iota((128, 256), 1)
    half = REL_2D // 2
    offset = jnp.clip((source & 63) - 32, -half, half - 1) + half
    plane = REL_1D + offset + jnp.where(source >= 64, REL_2D, 0)
    line = source - 128
    last = REL_1D - 1
    box_part = jnp.where(plane == bucket, 1.0, 0.0)
    box_part += jnp.where(source < 64, jnp.where(bucket == last, 1.0, 0.0), 0.0)
    line_part = jnp.where(line == bucket, 1.0, 0.0) - jnp.where(bucket == last, 1.0, 0.0)
    line_part = jnp.where(line < last, line_part, 0.0)
    return jnp.where(source < 128, box_part, line_part)


def small_kernel(heads, ids, own, other, mask_grad, table_grad, gain_grad, shift_grad):
    first = ids[1] == 0
    slot = (
        jnp.where(first, own[...], other[...]),
        jnp.where(first, other[...], own[...]),
    )
    sums = own[12:24, 0:256]
    table = lax.dot_general(
        fold_matrix(),
        sums,
        (((1,), (1,)), ((), ())),
        precision=lax.Precision.HIGHEST,
        preferred_element_type=F32,
    )
    table_grad[...] = table[:, :heads]
    for m in range(2):
        mask_grad[m : m + 1, :] = (
            own[10 + m : 11 + m, :] + other[10 + m : 11 + m, :] + slot[m][9:10, :]
        )
        gain_grad[m, 0:1, :] = slot[m][7:8, :]
        gain_grad[m, 1:2, :] = slot[m][5:6, :]
        shift_grad[m, 0:1, :] = slot[m][8:9, :]
        shift_grad[m, 1:2, :] = slot[m][6:7, :]


def params(megabytes):
    return pltpu.CompilerParams(vmem_limit_bytes=megabytes * 1024 * 1024)


def cost(units=1000):
    return pl.CostEstimate(flops=units, bytes_accessed=1000, transcendentals=0)


def after(value, *others):
    return lax.optimization_barrier((value,) + others)[0]


VM = pl.BlockSpec(memory_space=pltpu.VMEM)
SM = pl.BlockSpec(memory_space=pltpu.SMEM)
ANY = pl.BlockSpec(memory_space=pl.ANY)


def sds(shape, dtype):
    return jax.ShapeDtypeStruct(shape, dtype)


def attention_forward(m, heads, places, boxes, mask, raw, membed, w_qkv, table, w_out, partial_sum):
    width = heads * HD
    has_partial = partial_sum is not None
    args = [places, boxes, mask, membed, table, raw, w_qkv, w_out]
    specs = [ANY] * len(args)
    locals_in = [
        pltpu.VMEM(a.shape if i < 6 else a.shape[1:], a.dtype) for i, a in enumerate(args)
    ]
    if has_partial:
        args.append(partial_sum)
        specs.append(VM)
    shapes = (
        ((PAGE, D), BF),
        ((3, PAGE, width), BF),
        ((heads, PAGE, PAGE), BF),
        ((width, PAGE), BF),
        ((8, PAGE), F32),
        ((PAGE, 8), jnp.int32),
        ((8, PAGE), jnp.int32),
        ((PAGE, D), BF if has_partial else F32),
    )
    return pl.pallas_call(
        partial(forward_kernel, m, heads, has_partial),
        in_specs=specs,
        out_specs=(ANY,) * 7 + ((ANY,) if has_partial else (VM,)),
        out_shape=tuple(sds(s, t) for s, t in shapes),
        scratch_shapes=locals_in
        + [pltpu.VMEM(s, t) for s, t in shapes[:7]]
        + [
            pltpu.VMEM((PAGE, D), BF),
            pltpu.VMEM((PAGE, PAGE), jnp.int32),
            pltpu.VMEM((PAGE, 128 * heads), BF),
            pltpu.VMEM((width, PAGE), BF),
            pltpu.SemaphoreType.DMA((8,)),
            pltpu.SemaphoreType.DMA((7 + heads,)),
        ],
        cost_estimate=cost(),
        compiler_params=params(WIDE),
    )(*args)


def feed_forward(ids, cols, embs, cots, att_own, att_peer, gain, shift, b_up, b_peer, b_down, own, recv):
    units = 2 * b_up.shape[1]
    up_own, down_own = own
    n_copies = 2 * (up_own.shape[2] // BLOCK + 4)
    args = [*cols, *embs, *cots, att_own, att_peer, gain, shift, b_up, b_peer, b_down]
    shapes = (
        ((PAGE, D), BF),
        ((PAGE, D), BF),
        ((PAGE, units), BF),
        ((PAGE, units), BF),
        ((PAGE, D), BF),
        ((PAGE, D), BF),
        ((24, D), F32),
    )
    rows_f32 = pltpu.VMEM((PAGE, D), F32)
    rows_low = pltpu.VMEM((PAGE, D), BF)
    return pl.pallas_call(
        ffn_kernel,
        in_specs=[SM] + [ANY] * (len(args) + 10),
        out_specs=(ANY, ANY) + (VM,) * 5,
        scratch_shapes=[
            pltpu.VMEM((D, units), BF),
            pltpu.VMEM((units, D), BF),
            pltpu.VMEM((PAGE, units), F32),
            rows_f32,
            rows_f32,
            rows_f32,
            rows_f32,
            rows_low,
            rows_low,
            pltpu.VMEM((PAGE, 8), jnp.int32),
            rows_low,
            rows_low,
        ]
        + [pltpu.VMEM(a.shape, a.dtype) for a in args[6:]]
        + [
            pltpu.VMEM((1, units), F32),
            pltpu.SemaphoreType.DMA((n_copies,)),
            pltpu.SemaphoreType.DMA((10,)),
            pltpu.SemaphoreType.DMA((2,)),
        ],
        out_shape=tuple(sds(s, t) for s, t in shapes),
        cost_estimate=cost(),
        compiler_params=params(52),
    )(ids, *args, up_own, down_own, *recv)


def weight_grad(ids, left, right, z_first):
    units = right.shape[1]
    shape = (COARSE // 2, D // COARSE, units)
    return pl.pallas_call(
        partial(weight_grad_kernel, z_first),
        in_specs=[SM, VM, VM],
        out_specs=(ANY, ANY),
        scratch_shapes=[
            pltpu.VMEM(shape, BF),
            pltpu.VMEM(shape, BF),
            pltpu.SemaphoreType.DMA((2 * (units // BLOCK),)),
        ],
        out_shape=(sds(shape, BF), sds(shape, BF)),
        cost_estimate=cost(),
        compiler_params=params(52),
    )(ids, left, right)


def mixed_gradient(own, peer, units):
    whole = pl.BlockSpec(own.shape, lambda i: (0, 0))
    return pl.pallas_call(
        mix_kernel,
        grid=(1,),
        in_specs=[whole, whole],
        out_specs=whole,
        out_shape=sds(own.shape, BF),
        cost_estimate=cost(units),
        compiler_params=params(WIDE),
    )(own, peer)


def attention_backward(m, heads, ids, saved, w_out, w_qkv, dmixed, before, ctx_other):
    emb, qkv, expo, ctx_t, inverse, cols, rows = saved
    width = heads * HD
    shard = 3 * D // COARSE
    args = [cols, rows, inverse, w_out, qkv, ctx_t, expo, emb, w_qkv]
    if m == 0:
        shard += 4 * width // COARSE
        args.append(ctx_other)
    shapes = (
        ((COARSE // 2, shard, width), BF),
        ((COARSE // 2, shard, width), BF),
        ((PAGE, D), BF),
        (before.shape, F32),
    )
    square = pltpu.VMEM((PAGE, PAGE), BF)
    flat = pltpu.VMEM((PAGE, width), BF)
    tall = pltpu.VMEM((width, PAGE), BF)
    return pl.pallas_call(
        partial(backward_kernel, m, heads),
        in_specs=[SM] + [ANY] * len(args) + [VM, VM],
        out_specs=(ANY, ANY, ANY, VM),
        scratch_shapes=[
            pltpu.VMEM(a.shape[1:] if i in (3, 8) else a.shape, a.dtype)
            for i, a in enumerate(args)
        ]
        + [pltpu.VMEM(s, t) for s, t in shapes[:3]]
        + [
            pltpu.VMEM((PAGE, PAGE), jnp.int32),
            square,
            flat,
            tall,
            tall,
            pltpu.VMEM((2, PAGE, PAGE), BF),
            pltpu.VMEM((2, PAGE, PAGE), BF),
            tall,
            flat,
            flat,
            pltpu.VMEM((3 * D, width), BF),
            pltpu.VMEM((heads, 128, PAGE), F32),
            pltpu.VMEM((8, PAGE), F32),
            pltpu.SemaphoreType.DMA((len(args) + heads - 1,)),
            pltpu.SemaphoreType.DMA((3,)),
        ],
        out_shape=tuple(sds(s, t) for s, t in shapes),
        cost_estimate=cost(),
        compiler_params=params(WIDE),
    )(ids, *args, dmixed, before)


def unpack(modality, ids, parts, heads, filled):
    width = heads * HD
    shapes = ((2, 3 * D, width), (2, width, D))
    rows = parts[0].shape[1]
    extra = () if filled is None else tuple(filled)
    return pl.pallas_call(
        partial(unpack_kernel, modality),
        in_specs=[SM] + [VM] * 4 + [ANY] * len(extra),
        out_specs=(ANY, ANY),
        scratch_shapes=[
            pltpu.VMEM((COARSE, rows, width), F32),
            pltpu.SemaphoreType.DMA((3 * COARSE,)),
        ],
        out_shape=tuple(sds(s, F32) for s in shapes),
        input_output_aliases={5: 0, 6: 1} if extra else {},
        cost_estimate=cost(),
        compiler_params=params(16),
    )(ids, *parts, *extra)


def small_outputs(ids, own, other, heads):
    shapes = ((2, D), (REL_1D + 2 * REL_2D, heads), (2, 2, D), (2, 2, D))
    return pl.pallas_call(
        partial(small_kernel, heads),
        in_specs=[SM, VM, VM],
        out_specs=(VM,) * len(shapes),
        out_shape=tuple(sds(s, F32) for s in shapes),
        cost_estimate=cost(),
        compiler_params=params(8),
    )(ids, own, other)


def on_device(
    n_dp,
    text_rows,
    visual_rows,
    text_mask,
    visual_mask,
    text_places,
    text_boxes,
    visual_boxes,
    mask_embed,
    w_qkv,
    w_out,
    rel_table,
    ln_gain,
    ln_bias,
    w_up,
    b_up,
    w_down,
    b_down,
    text_cotangent,
    visual_cotangent,
):
    heads = rel_table.shape[1]
    half_units = w_up.shape[2]
    quarter = half_units // 4
    dp = lax.axis_index("dp")
    mp = lax.axis_index("mp")
    bits = n_dp.bit_length() - 1
    fine_bits = bits - 4
    me = dp >> fine_bits
    q = dp & 3
    ids = jnp.stack([me, mp, q]).astype(jnp.int32)

    def swap(x, flip):
        return lax.ppermute(x, "dp", [(i, i ^ flip) for i in range(n_dp)])

    def cross(x):
        return lax.ppermute(x, "mp", [(0, 1), (1, 0)])

    up_y = cross(lax.dynamic_slice(w_up, (1 - mp, 0, quarter * q), (1, D, quarter))[0])
    b_up_peer = cross(lax.dynamic_slice(b_up, (1 - mp, 0), (1, half_units)))

    table = rel_table.T
    forward = partial(attention_forward, heads=heads, membed=mask_embed, w_qkv=w_qkv)
    forward = partial(forward, table=table, w_out=w_out)
    *saved_text, att_t = forward(
        0,
        places=text_places.reshape(1, PAGE),
        boxes=text_boxes.T,
        mask=text_mask.reshape(1, PAGE),
        raw=text_rows,
        partial_sum=None,
    )
    up_y = after(up_y, att_t)
    down_part = lax.dynamic_slice(
        after(w_down, att_t), (1 - mp, quarter * q, 0), (1, quarter, D)
    )
    down_y = cross(down_part[0])
    up_x = swap(up_y, 2)
    up_c = swap(up_y, 1)
    *saved_visual, att = forward(
        1,
        places=jnp.arange(PAGE, dtype=jnp.int32).reshape(1, PAGE),
        boxes=visual_boxes.T,
        mask=visual_mask.reshape(1, PAGE),
        raw=visual_rows,
        partial_sum=att_t,
    )
    att_peer = cross(after(att, up_x))
    down_y = after(down_y, att)
    down_x = swap(down_y, 2)
    down_c = swap(down_y, 1)
    up_d = swap(up_x, 1)
    down_d = swap(down_x, 1)

    out, first_own, act, dpre, hid_low, dlow, small = feed_forward(
        ids,
        (saved_text[5], saved_visual[5]),
        (saved_text[0], saved_visual[0]),
        (text_cotangent, visual_cotangent),
        att,
        att_peer,
        ln_gain,
        ln_bias,
        b_up,
        b_up_peer,
        b_down,
        (w_up, w_down),
        (up_y, up_x, up_c, up_d, down_y, down_x, down_c, down_d),
    )
    first_peer = cross(first_own)

    f0 = 1 << fine_bits
    x_first = (f0, 2 * f0, 4 * f0, 8 * f0)
    z_first = (f0, 4 * f0, 8 * f0, 2 * f0)

    def half_sum(keep, *got):
        n = got[-1].shape[0] // 2
        total = keep[n : 2 * n].astype(F32)
        for g in got:
            total = total + g[n : 2 * n].astype(F32)
        return total.astype(BF)

    def last_sum(keep, *got):
        total = keep[0].astype(F32)
        for g in got:
            total = total + g[0].astype(F32)
        for b in range(fine_bits):
            total = total + swap(total, 1 << b)
        return total

    def after_all(values, *others):
        return lax.optimization_barrier((tuple(values), others))[0]

    def own_rows(total):
        count = D // n_dp
        return lax.dynamic_slice(total, (count * (dp & (f0 - 1)), 0), (count, total.shape[1]))

    def select_half(total, half):
        return lax.dynamic_slice(total, (0, half_units * half), (total.shape[0], half_units))

    backward = partial(attention_backward, heads=heads, ids=ids, w_out=w_out, w_qkv=w_qkv)

    dn_keep, dn_send = weight_grad(ids, dlow, act, False)
    dn_1 = swap(dn_send, f0)
    up_keep, up_send = weight_grad(ids, after(hid_low, dn_send), dpre, True)
    up_1 = swap(up_send, f0)
    dmixed = mixed_gradient(first_own, after(first_peer, up_send), CLAIM)
    dn_2s = half_sum(dn_keep, after(dn_1, dmixed))
    dn_2 = swap(dn_2s, x_first[1])
    up_2s = half_sum(up_keep, after(up_1, dn_2s))
    up_2 = swap(up_2s, z_first[1])
    dmixed = after(dmixed, up_2s)
    out_peer = cross(after(out, up_2s))
    t_keep, t_send, demb_t, small = backward(
        0, saved=saved_text, dmixed=dmixed, before=small, ctx_other=saved_visual[3]
    )
    t_1 = swap(t_send, f0)
    v_keep, v_send, demb_v, small = backward(
        1, saved=saved_visual, dmixed=after(dmixed, t_send), before=small, ctx_other=None
    )
    v_1 = swap(v_send, f0)
    def both(total, peer):
        own = select_half(total, 0)
        peer = peer.astype(F32)
        return jnp.stack([jnp.where(mp == 0, own, peer), jnp.where(mp == 0, peer, own)])

    def input_grad(m, part, part_peer, mask):
        first = jnp.where(mp == m, first_own, first_peer).astype(F32)
        total = first + (part.astype(F32) + part_peer.astype(F32))
        return jnp.where(mask[:, None] == 1, 0.0, total).astype(BF)

    out_peer = after(out_peer, v_send)
    text_out = jnp.where(mp == 0, out, out_peer)
    visual_out = jnp.where(mp == 0, out_peer, out)
    small_got = swap(after(small, text_out), 1)
    dn_3s = half_sum(dn_keep, dn_1, after(dn_2, text_out))
    dn_3 = swap(dn_3s, x_first[2])
    up_3s = half_sum(up_keep, up_1, after(up_2, dn_3s))
    up_3 = swap(up_3s, z_first[2])
    small = small + after(small_got, up_3s)
    small_got = swap(small, 2)
    t_2s = half_sum(t_keep, after(t_1, small))
    t_2 = swap(t_2s, x_first[1])
    v_2s = half_sum(v_keep, after(v_1, t_2s))
    v_2 = swap(v_2s, x_first[1])
    small = small + after(small_got, v_2s)
    small_got = swap(small, 4)
    dn_4s = half_sum(dn_keep, dn_1, dn_2, after(dn_3, small))
    dn_4 = swap(dn_4s, x_first[3])
    t_3s = half_sum(t_keep, t_1, after(t_2, dn_4s))
    t_3 = swap(t_3s, x_first[2])
    small = small + after(small_got, t_3s)
    small_got = swap(small, 8)
    up_4s = half_sum(up_keep, up_1, up_2, after(up_3, small))
    up_4 = swap(up_4s, z_first[3])
    v_3s = half_sum(v_keep, v_1, after(v_2, up_4s))
    v_3 = swap(v_3s, x_first[2])
    dn_total = own_rows(last_sum(dn_keep, dn_1, dn_2, dn_3, after(dn_4, v_3s)))
    dn_cross = cross(select_half(dn_total, 1).astype(BF))
    t_4s = half_sum(t_keep, t_1, t_2, after(t_3, dn_total))
    t_4 = swap(t_4s, x_first[3])
    small = small + after(small_got, t_4s)
    for b in range(4, bits):
        small = small + swap(small, 1 << b)
    small_other = cross(small)
    v_4s = half_sum(v_keep, v_1, v_2, after(v_3, small))
    v_4 = swap(v_4s, x_first[3])
    up_total = own_rows(last_sum(up_keep, up_1, up_2, up_3, after(up_4, v_4s)))
    up_cross = cross(select_half(up_total, 1).astype(BF))
    w_down_grad = jnp.transpose(both(dn_total, after(dn_cross, up_total)), (0, 2, 1))
    demb_t_peer = cross(after(demb_t, w_down_grad))
    t_piece = last_sum(t_keep, t_1, t_2, t_3, after(t_4, w_down_grad)).astype(BF)
    t_g2 = swap(t_piece, x_first[3])
    small_other = after(small_other, t_piece)
    mask_total, rel_grad, gain_grad, shift_grad = small_outputs(ids, small, small_other, heads)
    per = half_units // n_dp
    own_bup = lax.dynamic_slice(small[:4].reshape(1, -1), (0, per * dp), (1, per))
    other_bup = lax.dynamic_slice(
        small_other[:4].reshape(1, -1), (0, half_units + per * dp), (1, per)
    )
    b_up_grad = jnp.where(
        jnp.arange(2, dtype=jnp.int32)[:, None] == mp, own_bup, other_bup
    )
    count = D // n_dp
    own_bd = lax.dynamic_slice(small, (4, count * dp), (1, count))
    other_bd = lax.dynamic_slice(small_other, (4, count * dp), (1, count))
    b_down_grad = jnp.where(jnp.arange(2, dtype=jnp.int32)[:, None] == mp, own_bd, other_bd)
    v_4 = after(v_4, mask_total, b_up_grad, b_down_grad)
    v_piece = last_sum(v_keep, v_1, v_2, v_3, v_4).astype(BF)
    v_g2 = swap(v_piece, x_first[3])
    w_up_grad = both(up_total, after(up_cross, v_piece))
    t_two = jnp.stack([t_piece, after(t_g2, w_up_grad)])
    t_g1 = swap(t_two, x_first[2])
    v_two = jnp.stack([v_piece, after(v_g2, t_two)])
    v_g1 = swap(v_two, x_first[2])
    text_grad = input_grad(0, demb_t, after(demb_t_peer, v_two), text_mask)
    demb_v_peer = cross(after(demb_v, text_grad))
    t_four = jnp.concatenate([t_two, after(t_g1, text_grad)])
    t_gx = swap(t_four, x_first[1])
    t_gc = swap(t_four, f0)
    v_four = jnp.concatenate([v_two, after(v_g1, t_four)])
    v_gx = swap(v_four, x_first[1])
    v_gc = swap(v_four, f0)
    t_gx = after(t_gx, v_four)
    t_gxc = swap(t_gx, f0)
    visual_grad = input_grad(1, demb_v, after(demb_v_peer, t_gx), visual_mask)
    t_gc = after(t_gc, visual_grad)
    filled = unpack(0, ids, (t_four, t_gx, t_gc, t_gxc), heads, None)
    v_gx = after(v_gx, *filled)
    v_gxc = swap(v_gx, f0)
    visual_parts = (v_four, v_gx, v_gc, v_gxc)
    w_qkv_grad, w_out_grad = unpack(1, ids, visual_parts, heads, filled)
    w_qkv_grad = w_qkv_grad.reshape(2, 3, D, heads * HD)

    return (
        text_out,
        visual_out,
        text_grad,
        visual_grad,
        mask_total,
        w_qkv_grad,
        w_out_grad,
        rel_grad,
        gain_grad,
        shift_grad,
        w_up_grad,
        b_up_grad,
        w_down_grad,
        b_down_grad,
    )


def solution(mesh):
    in_specs = (
        P("dp", None),
        P("dp", None),
        P("dp"),
        P("dp"),
        P("dp"),
        P("dp", None),
        P("dp", None),
        P(),
        P(None, None, None, "mp"),
        P(None, "mp", None),
        P(None, "mp"),
        P(),
        P(),
        P(None, None, "mp"),
        P(None, "mp"),
        P(None, "mp", None),
        P(),
        P("dp", None),
        P("dp", None),
    )
    out_specs = (
        P("dp", None),
        P("dp", None),
        P("dp", None),
        P("dp", None),
        P(),
        P(None, None, None, "mp"),
        P(None, "mp", None),
        P(None, "mp"),
        P(),
        P(),
        P(None, "dp", "mp"),
        P(None, ("mp", "dp")),
        P(None, "mp", "dp"),
        P(None, "dp"),
    )
    return jax.shard_map(
        partial(on_device, mesh.shape["dp"]),
        mesh=mesh,
        in_specs=in_specs,
        out_specs=out_specs,
        check_vma=False,
    )
```

```python
from functools import partial

import jax
import jax.numpy as jnp
from jax import lax
from jax.experimental import pallas as pl
from jax.experimental.pallas import tpu as pltpu
from jax.sharding import PartitionSpec as P

D = 768
HD = 64
PAGE = 512
REL_1D = 64
REL_2D = 32
COARSE = 16
BLOCK = 768
BF = jnp.bfloat16
F32 = jnp.float32
CLAIM = 20_000_000_000
WIDE = 60


def mm(a, b):
    return lax.dot_general(a, b, (((1,), (0,)), ((), ())), preferred_element_type=F32)


def mm_nt(a, b):
    return lax.dot_general(a, b, (((1,), (1,)), ((), ())), preferred_element_type=F32)


def iota(shape, dim):
    return lax.broadcasted_iota(jnp.int32, shape, dim)


def row_sum(x):
    return jnp.sum(x, axis=-1, keepdims=True)


def row_mean(x):
    return jnp.mean(x, axis=-1, keepdims=True)


def col_sum(x):
    return jnp.sum(x, axis=0, keepdims=True)


def start_all(pairs, sems, first=0):
    copies = []
    for i, (source, target) in enumerate(pairs):
        copy = pltpu.make_async_copy(source, target, sems.at[first + i])
        copy.start()
        copies.append(copy)
    return copies


def wait_all(copies):
    for copy in copies:
        copy.wait()


def line_buckets(cols, rows):
    half = REL_1D // 2
    return jnp.clip(cols[:, 0:1] - rows[0:1, :], -half, half - 1) + half


def place_lanes(cols):
    lane = iota((PAGE, 128), 1)
    code = lane & 63
    across = jnp.broadcast_to(cols[:, 1:2], (PAGE, 128))
    down = jnp.broadcast_to(cols[:, 2:3], (PAGE, 128)) + REL_2D
    return jnp.where(jnp.where(code < REL_2D, across, down) == code, 1.0, 0.0)


def table_plane(table_row):
    b = iota((128, 128), 0)
    lane = iota((128, 128), 1)
    c = lane & 63
    half = REL_2D // 2
    shift = jnp.clip((c & 31) - (b & 31), -half, half - 1) + half + REL_1D
    index = jnp.where(c >= REL_2D, shift + REL_2D, shift)
    spread = jnp.broadcast_to(table_row, (128, 128))
    values = jnp.take_along_axis(spread, index, axis=1)
    values = jnp.where((b >> 5) == (c >> 5), values, 0.0)
    high = values.astype(BF).astype(F32)
    return jnp.where(lane < 64, high, values - high).astype(BF)


def forward_kernel(
    m, heads, has_partial, places, boxes, mask, membed, table, raw, wqkv, wout, *refs
):
    if has_partial:
        partial_ref, refs = refs[0], refs[1:]
    outputs, att, refs = refs[:7], refs[7], refs[8:]
    places_s, boxes_s, mask_s, membed_s, table_s, raw_s, wqkv_s, wout_s = refs[:8]
    emb_s, qkv_s, expo_s, ctx_s, inverse_s, cols_s, rows_s = refs[8:15]
    att_s, idx_s, bias_s, v_t, in_sems, out_sems = refs[15:]
    emb, qkv, expo, ctx_t, inverse, cols, rows = outputs
    sources = (places, boxes, mask, membed, table, raw, wqkv.at[m], wout.at[m])
    loads = start_all(list(zip(sources, refs[:8])), in_sems)
    wait_all(loads[:6])
    row_id = iota((8, PAGE), 0)
    place_row = jnp.broadcast_to(places_s[...], (8, PAGE))
    mask_row = jnp.where(row_id == 3, jnp.broadcast_to(mask_s[...], (8, PAGE)), 0)
    facts = jnp.where(row_id == 0, place_row, mask_row).astype(F32)
    turned = boxes_s[...].astype(F32)
    facts = jnp.where(row_id == 1, turned[0:1, :], facts)
    facts = jnp.where(row_id == 2, turned[1:2, :], facts)
    rows_s[...] = facts.astype(jnp.int32)
    cols_s[...] = facts.T.astype(jnp.int32)
    masked = cols_s[:, 3:4] == 1
    filler = membed_s[m : m + 1, :].astype(F32)
    embedded = jnp.where(masked, filler, raw_s[...].astype(F32)).astype(BF)
    emb_s[...] = embedded
    stores = start_all([(emb_s, emb), (cols_s, cols), (rows_s, rows)], out_sems)
    loads[6].wait()
    qkv_s[0] = (mm(embedded, wqkv_s[0]) * HD ** (-0.5)).astype(BF)
    qkv_s[1] = mm(embedded, wqkv_s[1]).astype(BF)
    values = mm(embedded, wqkv_s[2]).astype(BF)
    qkv_s[2] = values
    v_t[...] = values.T
    stores += start_all([(qkv_s, qkv)], out_sems, 3)
    idx_s[...] = line_buckets(cols_s, rows_s)
    onehot = place_lanes(cols_s).astype(BF)
    planes = jnp.concatenate([table_plane(table_s[h : h + 1, :]) for h in range(heads)], axis=1)
    bias_s[...] = mm(onehot, planes).astype(BF)
    inverse_s[...] = jnp.zeros((8, PAGE), F32)
    for h in range(heads):
        head = slice(HD * h, HD * (h + 1))
        keys = jnp.concatenate([onehot, qkv_s[1, :, head]], axis=1)
        queries = jnp.concatenate(
            [bias_s[:, 128 * h : 128 * (h + 1)], qkv_s[0, :, head]], axis=1
        )
        spread = jnp.broadcast_to(table_s[h : h + 1, :], (PAGE, 128))
        line = [
            jnp.take_along_axis(spread, idx_s[:, 128 * b : 128 * (b + 1)], axis=1)
            for b in range(PAGE // 128)
        ]
        scores = mm_nt(keys, queries) + jnp.concatenate(line, axis=1)
        exponent = jnp.exp(scores - jnp.max(scores, axis=0, keepdims=True))
        scale = 1.0 / col_sum(exponent)
        inverse_s[h : h + 1, :] = scale
        expo_s[h] = exponent.astype(BF)
        stores += start_all([(expo_s.at[h], expo.at[h])], out_sems, 4 + h)
        ctx_s[head, :] = (mm(v_t[head, :], expo_s[h]) * scale).astype(BF)
    stores += start_all([(ctx_s, ctx_t), (inverse_s, inverse)], out_sems, 4 + heads)
    loads[7].wait()
    attended = mm(ctx_s[...].T, wout_s[...])
    if has_partial:
        att_s[...] = (partial_ref[...] + attended).astype(BF)
        stores += start_all([(att_s, att)], out_sems, 6 + heads)
    else:
        att[...] = attended
    wait_all(stores)


def gelu_both(x):
    z = jnp.abs(x)
    t = 1.0 / (1.0 + (0.3275911 * 0.5**0.5) * z)
    poly = t * (
        0.127414796
        + t * (-0.142248368 + t * (0.7107068705 + t * (-0.7265760135 + t * 0.5307027145)))
    )
    bell = jnp.exp(-0.5 * x * x)
    tail = poly * bell
    phi = jnp.where(x >= 0, 1.0 - tail, tail)
    return x * phi, phi + x * bell * 0.3989422804014327


def copy_list(ids, up_own, down_own, up_recv, down_recv, up_s, down_s, sems):
    mp, q = ids[1], ids[2]
    half = up_own.shape[2]
    quarter = half // 4
    copies = []
    for t in range(half // BLOCK):
        span = slice(BLOCK * t, BLOCK * (t + 1))
        copies.append((up_own.at[mp, :, span], up_s.at[:, span]))
    for j in range(4):
        place = pl.multiple_of(half + quarter * (q ^ j), 128)
        copies.append((up_recv[j], up_s.at[:, pl.ds(place, quarter)]))
    for t in range(half // BLOCK):
        span = slice(BLOCK * t, BLOCK * (t + 1))
        copies.append((down_own.at[mp, span, :], down_s.at[span, :]))
    for j in range(4):
        place = pl.multiple_of(half + quarter * (q ^ j), 128)
        copies.append((down_recv[j], down_s.at[pl.ds(place, quarter), :]))
    return [pltpu.make_async_copy(a, b, sems.at[i]) for i, (a, b) in enumerate(copies)]


def ffn_kernel(
    ids,
    cols_text,
    cols_visual,
    emb_text,
    emb_visual,
    cot_text,
    cot_visual,
    att_own,
    att_peer,
    gain_both,
    shift_both,
    b_up_own,
    b_up_peer,
    b_down_both,
    up_own,
    down_own,
    uy,
    ux,
    uc,
    ud,
    dy,
    dx,
    dc,
    dd,
    out,
    dfirst,
    act,
    dpre,
    hid_low,
    dlow,
    small,
    up_s,
    down_s,
    slope_s,
    norm1,
    hidden,
    work,
    dcomb,
    out_s,
    dfirst_s,
    cols,
    emb,
    cot_s,
    att_own_s,
    att_peer_s,
    gain_s,
    shift_s,
    b_up_both,
    b_up_far,
    b_down_s,
    b_up,
    sems,
    own_sems,
    out_sems,
):
    mp = ids[1]
    text = mp == 0
    plain = start_all(
        [
            (att_own, att_own_s),
            (att_peer, att_peer_s),
            (gain_both, gain_s),
            (shift_both, shift_s),
            (b_up_own, b_up_both),
            (b_up_peer, b_up_far),
            (b_down_both, b_down_s),
        ],
        own_sems,
    )
    at = len(plain)

    @pl.when(text)
    def _():
        start_all([(emb_text, emb), (cols_text, cols), (cot_text, cot_s)], own_sems, at)

    @pl.when(mp != 0)
    def _():
        start_all([(emb_visual, emb), (cols_visual, cols), (cot_visual, cot_s)], own_sems, at)

    chosen = [
        pltpu.make_async_copy(a, b, own_sems.at[at + i])
        for i, (a, b) in enumerate([(emb_text, emb), (cols_text, cols), (cot_text, cot_s)])
    ]
    up_recv = (uy, uc, ux, ud)
    down_recv = (dy, dc, dx, dd)
    copies = copy_list(ids, up_own, down_own, up_recv, down_recv, up_s, down_s, sems)
    n_own = up_own.shape[2] // BLOCK
    per_side = n_own + 4
    for i in range(n_own):
        copies[i].start()
        copies[per_side + i].start()
    for i in range(n_own, per_side):
        copies[i].start()
        copies[per_side + i].start()
    wait_all(plain)
    wait_all(chosen)
    half_units = b_up_own.shape[1]
    b_up[:, :half_units] = jnp.where(text, b_up_both[0:1, :], b_up_both[1:2, :])
    b_up[:, half_units:] = b_up_far[...]
    gain = jnp.where(text, gain_s[0], gain_s[1])
    shift = jnp.where(text, shift_s[0], shift_s[1])
    b_down = jnp.where(text, b_down_s[0:1, :], b_down_s[1:2, :])
    total = emb[...].astype(F32) + (att_own_s[...].astype(F32) + att_peer_s[...].astype(F32))
    centred = total - row_mean(total)
    inv1 = lax.rsqrt(row_mean(centred * centred) + 1e-05)
    n1 = centred * inv1
    norm1[...] = n1
    hid = n1 * gain[0:1, :] + shift[0:1, :]
    hidden[...] = hid
    hid_low[...] = hid.astype(BF)
    n_blocks = up_s.shape[1] // BLOCK

    def landed(first):
        if first < n_own:
            copies[first].wait()
            copies[per_side + first].wait()
        elif first == n_own:
            for i in range(n_own, per_side):
                copies[i].wait()
                copies[per_side + i].wait()

    def before_gelu(t):
        landed(t)
        span = slice(BLOCK * t, BLOCK * (t + 1))
        return mm(hid_low[...], up_s[:, span]) + b_up[:, span]

    pre = before_gelu(0)
    low = None
    for t in range(n_blocks):
        following = before_gelu(t + 1) if t + 1 < n_blocks else None
        span = slice(BLOCK * t, BLOCK * (t + 1))
        value, slope = gelu_both(pre)
        low = value.astype(BF)
        act[:, span] = low
        slope_s[:, span] = slope
        down = mm(low, down_s[span, :])
        if t == 0:
            work[...] = down
        else:
            work[...] += down
        pre = following
    combined = hidden[...] + work[...] + b_down
    centred2 = combined - row_mean(combined)
    inv2 = lax.rsqrt(row_mean(centred2 * centred2) + 1e-05)
    n2 = centred2 * inv2
    out_s[...] = (n2 * gain[1:2, :] + shift[1:2, :]).astype(BF)
    stores = start_all([(out_s, out)], out_sems)
    cot = cot_s[...].astype(F32)
    small[5:6, :] = col_sum(cot * n2)
    small[6:7, :] = col_sum(cot)
    scaled = cot * gain[1:2, :]
    back = inv2 * (scaled - row_mean(scaled) - n2 * row_mean(scaled * n2))
    dcomb[...] = back
    small[4:5, :] = col_sum(back)
    dlow[...] = back.astype(BF)
    dact = mm_nt(dlow[...], down_s[0:BLOCK, :])
    for t in range(n_blocks):
        span = slice(BLOCK * t, BLOCK * (t + 1))
        later = slice(BLOCK * (t + 1), BLOCK * (t + 2))
        following = mm_nt(dlow[...], down_s[later, :]) if t + 1 < n_blocks else None
        low = (dact * slope_s[:, span]).astype(BF)
        dpre[:, span] = low
        small[t : t + 1, :] = col_sum(low.astype(F32))
        dhid = mm_nt(low, up_s[:, span])
        if t == 0:
            work[...] = dhid
        else:
            work[...] += dhid
        dact = following
    dhidden = dcomb[...] + work[...]
    n1 = norm1[...]
    small[7:8, :] = col_sum(dhidden * n1)
    small[8:9, :] = col_sum(dhidden)
    scaled1 = dhidden * gain[0:1, :]
    first = inv1 * (scaled1 - row_mean(scaled1) - n1 * row_mean(scaled1 * n1))
    dfirst_s[...] = first.astype(BF)
    stores += start_all([(dfirst_s, dfirst)], out_sems, 1)
    masked = cols[:, 3:4] == 1
    small[9:10, :] = col_sum(jnp.where(masked, first, 0.0))
    small[10:24, :] = jnp.zeros((14, D), F32)
    wait_all(stores)


def place_of(rel, z_first):
    x, low, high = rel & 1, (rel >> 1) & 1, rel >> 2
    if z_first:
        return (low << 2) | (x << 1) | high
    return (x << 2) | (low << 1) | high


def put_pairs(ids, values, rows, at, keep, send, span, z_first=False):
    upper = ids[0] & 1
    base = ids[0] >> 1
    spot = slice(at, at + rows)
    for i in range(values.shape[0] // (2 * rows)):
        a = values[2 * rows * i : 2 * rows * i + rows].astype(F32)
        b = values[2 * rows * i + rows : 2 * rows * (i + 1)].astype(F32)
        place = place_of(i ^ base, z_first)
        keep[place, spot, span] = jnp.where(upper == 0, a, b).astype(BF)
        send[place, spot, span] = jnp.where(upper == 0, b, a).astype(BF)


def weight_grad_kernel(z_first, ids, left, right, keep, send, keep_s, send_s, sems):
    left_t = left[...].T
    copies = []
    for t in range(right.shape[1] // BLOCK):
        span = slice(BLOCK * t, BLOCK * (t + 1))
        product = mm(left_t, right[:, span])
        put_pairs(ids, product, D // COARSE, 0, keep_s, send_s, span, z_first)
        for i, (source, target) in enumerate(((keep_s, keep), (send_s, send))):
            copy = pltpu.make_async_copy(
                source.at[:, :, span], target.at[:, :, span], sems.at[2 * t + i]
            )
            copy.start()
            copies.append(copy)
    for copy in copies:
        copy.wait()


def add_row(small, before, row, half, values):
    span = slice(128 * half, 128 * (half + 1))
    small[row : row + 1, span] = before[row : row + 1, span] + values


def backward_kernel(modality, heads, ids, *refs):
    n_in = 12 if modality == 0 else 11
    inputs, before, refs = refs[:n_in], refs[n_in], refs[n_in + 1 :]
    (keep, send, demb, small), refs = refs[:4], refs[4:]
    local, refs = refs[:n_in], refs[n_in:]
    cols, rows, inverse, wout, first_own, first_peer, qkv, ctx_t, expo, emb, wqkv = local[:11]
    keep_s, send_s, demb_s, idx_s, band_s, dctx, dctx_t, k_t, ds_s, dsb_s, dq_t, dk, dv = refs[:13]
    grads_s, hist_s, low_s, in_sems, out_sems = refs[13:]
    sources = list(inputs)
    sources[3] = sources[3].at[modality]
    sources[10] = sources[10].at[modality]
    pairs = []
    for i, (source, target) in enumerate(zip(sources, local)):
        if i == 8:
            pairs += [(source.at[h], target.at[h]) for h in range(heads)]
        else:
            pairs.append((source, target))
    loads = start_all(pairs, in_sems)
    wait_all(loads[:6])
    small[...] = before[...]
    dmixed = (first_own[...].astype(F32) + first_peer[...].astype(F32)).astype(BF)
    back = mm_nt(wout[...], dmixed)
    for h in range(heads):
        head = slice(HD * h, HD * (h + 1))
        dctx_t[head, :] = (back[HD * h : HD * (h + 1)] * inverse[h : h + 1, :]).astype(BF)
    dctx[...] = dctx_t[...].T
    buckets = line_buckets(cols, rows)
    idx_s[...] = buckets
    band_s[...] = jnp.where((buckets > 0) & (buckets < REL_1D - 1), 1.0, 0.0).astype(BF)
    lane = iota((PAGE, 128), 1)
    hot_boxes = place_lanes(cols)
    hot_places = jnp.where((cols[:, 0:1] & 63) == lane - 64, 1.0, 0.0)
    hot_right = jnp.where(lane < 64, hot_boxes, hot_places).astype(BF)
    r = iota((64, PAGE), 0)
    box_code = jnp.where(r < REL_2D, rows[1:2, :], rows[2:3, :] + REL_2D)
    boxes_t = jnp.where(box_code == r, 1.0, 0.0).astype(BF)
    places_t = jnp.where((rows[0:1, :] & 63) == r, 1.0, 0.0).astype(BF)
    b = iota((128, 128), 0)
    c = iota((128, 128), 1)
    box_at = (b & 31) - (c & 63) + 32
    box_index = jnp.clip(box_at, 0, 31) + jnp.where(b >= REL_2D, REL_2D, 0)
    place_index = 64 + ((b - c + 32) & 63)
    diagonal = jnp.where(b < 64, box_index, place_index)
    valid_box = (box_at >= 0) & (box_at < 32) & ((b >> 5) == (c >> 6))
    valid = jnp.where(
        b < 64, jnp.where(valid_box, 1.0, 0.0), jnp.where(c < 64, 1.0, 0.0)
    )
    lane_row = iota((1, 128), 1)
    wait_all(loads[6:8])
    k_t[...] = qkv[1].T
    overlap = back * ctx_t[...].astype(F32)
    shared = jnp.concatenate(
        [col_sum(overlap[HD * h : HD * (h + 1)]) for h in range(heads)], axis=0
    )
    shared = shared * inverse[0:heads, :]
    for h in range(heads):
        head = slice(HD * h, HD * (h + 1))
        loads[8 + h].wait()
        turn = h % 2
        dprobs = mm(qkv[2, :, head], dctx_t[head, :])
        low = (expo[h].astype(F32) * (dprobs - shared[h : h + 1, :])).astype(BF)
        ds_s[turn] = low
        dsb_s[turn] = low * band_s[...]
        low_s[h : h + 1, :] = col_sum(jnp.where(idx_s[...] == 0, low.astype(F32), 0.0))
        both = mm(jnp.concatenate([k_t[head, :], boxes_t], axis=0), ds_s[turn])
        dq_t[head, :] = (both[:HD] * HD ** (-0.5)).astype(BF)
        hist_s[h, 0:64, :] = both[HD:]
        hist_s[h, 64:128, :] = mm(places_t, dsb_s[turn])
        dk[:, head] = mm(ds_s[turn], qkv[0, :, head]).astype(BF)
        dv[:, head] = mm(expo[h], dctx[:, head]).astype(BF)
    first = hist_s[...].reshape(128 * heads, PAGE)
    high = first.astype(BF)
    rest = (first - high.astype(F32)).astype(BF)
    pairs = mm(high, hot_right) + mm(rest, hot_right)
    for h in range(heads):
        mine = pairs[128 * h : 128 * (h + 1)]
        folded = valid * jnp.take_along_axis(mine, diagonal, axis=1)
        add_row(small, before, 12 + h, 0, col_sum(folded[:64]))
        line = col_sum(folded[64:])
        tail = row_sum(low_s[h : h + 1, :])
        add_row(small, before, 12 + h, 1, jnp.where(lane_row == 0, tail, line))
    width = heads * HD
    span = slice(0, width)
    wait_all(loads[8 + heads :])
    emb_t = emb[...].T
    grads_s[0:D, :] = mm_nt(emb_t, dq_t[...]).astype(BF)
    grads_s[D : 2 * D, :] = mm(emb_t, dk[...]).astype(BF)
    grads_s[2 * D : 3 * D, :] = mm(emb_t, dv[...]).astype(BF)
    rows_qkv = 3 * D // COARSE
    rows_out = 2 * width // COARSE
    put_pairs(ids, grads_s[...], rows_qkv, 0, keep_s, send_s, span)
    for i, context in enumerate((ctx_t, local[11]) if modality == 0 else ()):
        out_grad = mm(context[...], dmixed)
        grads_s[0:width, :] = out_grad[:, :width].astype(BF)
        grads_s[width : 2 * width, :] = out_grad[:, width:].astype(BF)
        at = rows_qkv + rows_out * i
        put_pairs(ids, grads_s[0 : 2 * width, :], rows_out, at, keep_s, send_s, span)
    stores = start_all([(send_s, send), (keep_s, keep)], out_sems)
    part = mm_nt(dq_t[...].T, wqkv[0])
    part += mm_nt(dk[...], wqkv[1])
    part += mm_nt(dv[...], wqkv[2])
    demb_s[...] = part.astype(BF)
    stores += start_all([(demb_s, demb)], out_sems, 2)
    mask_row = col_sum(jnp.where(cols[:, 3:4] == 1, part, 0.0))
    small[10 + modality : 11 + modality, :] = before[10 + modality : 11 + modality, :] + mask_row
    wait_all(stores)


def gate_kernel(ids, *refs):
    passed = refs[-1]
    for i in range(ids.shape[0]):
        passed[i] = ids[i]


def unpack_kernel(modality, groups, ids, *refs):
    sources = refs[: len(groups)]
    qkv_grad, out_grad, stage, sems = refs[-4:]
    rows, width = sources[0].shape[1:]
    rows_qkv = 3 * D // COARSE
    rows_out = 2 * width // COARSE
    per_half = COARSE // 2
    count = 1 + (rows - rows_qkv) // rows_out
    me = ids[0]
    copies = []
    slot = -1
    for (core, side, lower), source in zip(groups, sources):
        for at in range(source.shape[0]):
            slot += 1
            stage[slot] = source[at].astype(F32)
            low = (at >> 1) + lower
            rel = core | (side << 1) | (low << 2) | ((at & 1) << 3)
            s = rel ^ me
            spot = pl.ds(pl.multiple_of(rows_qkv * s, 8), rows_qkv)
            targets = [qkv_grad.at[modality, spot, :]]
            low = pl.ds(pl.multiple_of(rows_out * (s & (per_half - 1)), 8), rows_out)
            half = pl.ds(pl.multiple_of(width * (s // per_half), 128), width)
            for m in range(count - 1):
                targets.append(out_grad.at[m, low, half])
            start = 0
            for i, target in enumerate(targets):
                size = rows_qkv if i == 0 else rows_out
                copy = pltpu.make_async_copy(
                    stage.at[slot, pl.ds(start, size), :], target, sems.at[count * slot + i]
                )
                copy.start()
                copies.append(copy)
                start += size
    for copy in copies:
        copy.wait()


def fold_matrix():
    bucket = iota((128, 256), 0)
    source = iota((128, 256), 1)
    half = REL_2D // 2
    offset = jnp.clip((source & 63) - 32, -half, half - 1) + half
    plane = REL_1D + offset + jnp.where(source >= 64, REL_2D, 0)
    line = source - 128
    last = REL_1D - 1
    box_part = jnp.where(plane == bucket, 1.0, 0.0)
    box_part += jnp.where(source < 64, jnp.where(bucket == last, 1.0, 0.0), 0.0)
    line_part = jnp.where(line == bucket, 1.0, 0.0) - jnp.where(bucket == last, 1.0, 0.0)
    line_part = jnp.where(line < last, line_part, 0.0)
    return jnp.where(source < 128, box_part, line_part)


def small_kernel(heads, ids, own, other, mask_grad, table_grad, gain_grad, shift_grad):
    first = ids[1] == 0
    slot = (
        jnp.where(first, own[...], other[...]),
        jnp.where(first, other[...], own[...]),
    )
    sums = own[12:24, 0:256]
    table = lax.dot_general(
        sums,
        fold_matrix(),
        (((1,), (1,)), ((), ())),
        precision=lax.Precision.HIGHEST,
        preferred_element_type=F32,
    )
    table_grad[...] = table[:heads]
    for m in range(2):
        mask_grad[m : m + 1, :] = (
            own[10 + m : 11 + m, :] + other[10 + m : 11 + m, :] + slot[m][9:10, :]
        )
        gain_grad[m, 0:1, :] = slot[m][7:8, :]
        gain_grad[m, 1:2, :] = slot[m][5:6, :]
        shift_grad[m, 0:1, :] = slot[m][8:9, :]
        shift_grad[m, 1:2, :] = slot[m][6:7, :]


def params(megabytes):
    return pltpu.CompilerParams(vmem_limit_bytes=megabytes * 1024 * 1024)


def cost(units=1000):
    return pl.CostEstimate(flops=units, bytes_accessed=1000, transcendentals=0)


def after(value, *others):
    return lax.optimization_barrier((value,) + others)[0]


VM = pl.BlockSpec(memory_space=pltpu.VMEM)
SM = pl.BlockSpec(memory_space=pltpu.SMEM)
ANY = pl.BlockSpec(memory_space=pl.ANY)


def sds(shape, dtype):
    return jax.ShapeDtypeStruct(shape, dtype)


def attention_forward(m, heads, places, boxes, mask, raw, membed, w_qkv, table, w_out, partial_sum):
    width = heads * HD
    has_partial = partial_sum is not None
    args = [places, boxes, mask, membed, table, raw, w_qkv, w_out]
    specs = [ANY] * len(args)
    locals_in = [
        pltpu.VMEM(a.shape if i < 6 else a.shape[1:], a.dtype) for i, a in enumerate(args)
    ]
    if has_partial:
        args.append(partial_sum)
        specs.append(VM)
    shapes = (
        ((PAGE, D), BF),
        ((3, PAGE, width), BF),
        ((heads, PAGE, PAGE), BF),
        ((width, PAGE), BF),
        ((8, PAGE), F32),
        ((PAGE, 8), jnp.int32),
        ((8, PAGE), jnp.int32),
        ((PAGE, D), BF if has_partial else F32),
    )
    return pl.pallas_call(
        partial(forward_kernel, m, heads, has_partial),
        in_specs=specs,
        out_specs=(ANY,) * 7 + ((ANY,) if has_partial else (VM,)),
        out_shape=tuple(sds(s, t) for s, t in shapes),
        scratch_shapes=locals_in
        + [pltpu.VMEM(s, t) for s, t in shapes[:7]]
        + [
            pltpu.VMEM((PAGE, D), BF),
            pltpu.VMEM((PAGE, PAGE), jnp.int32),
            pltpu.VMEM((PAGE, 128 * heads), BF),
            pltpu.VMEM((width, PAGE), BF),
            pltpu.SemaphoreType.DMA((8,)),
            pltpu.SemaphoreType.DMA((7 + heads,)),
        ],
        cost_estimate=cost(),
        compiler_params=params(WIDE),
    )(*args)


def feed_forward(ids, cols, embs, cots, att_own, att_peer, gain, shift, b_up, b_peer, b_down, own, recv):
    units = 2 * b_up.shape[1]
    up_own, down_own = own
    n_copies = 2 * (up_own.shape[2] // BLOCK + 4)
    args = [*cols, *embs, *cots, att_own, att_peer, gain, shift, b_up, b_peer, b_down]
    shapes = (
        ((PAGE, D), BF),
        ((PAGE, D), BF),
        ((PAGE, units), BF),
        ((PAGE, units), BF),
        ((PAGE, D), BF),
        ((PAGE, D), BF),
        ((24, D), F32),
    )
    rows_f32 = pltpu.VMEM((PAGE, D), F32)
    rows_low = pltpu.VMEM((PAGE, D), BF)
    return pl.pallas_call(
        ffn_kernel,
        in_specs=[SM] + [ANY] * (len(args) + 10),
        out_specs=(ANY, ANY) + (VM,) * 5,
        scratch_shapes=[
            pltpu.VMEM((D, units), BF),
            pltpu.VMEM((units, D), BF),
            pltpu.VMEM((PAGE, units), F32),
            rows_f32,
            rows_f32,
            rows_f32,
            rows_f32,
            rows_low,
            rows_low,
            pltpu.VMEM((PAGE, 8), jnp.int32),
            rows_low,
            rows_low,
        ]
        + [pltpu.VMEM(a.shape, a.dtype) for a in args[6:]]
        + [
            pltpu.VMEM((1, units), F32),
            pltpu.SemaphoreType.DMA((n_copies,)),
            pltpu.SemaphoreType.DMA((10,)),
            pltpu.SemaphoreType.DMA((2,)),
        ],
        out_shape=tuple(sds(s, t) for s, t in shapes),
        cost_estimate=cost(),
        compiler_params=params(52),
    )(ids, *args, up_own, down_own, *recv)


def weight_grad(ids, left, right, z_first):
    units = right.shape[1]
    shape = (COARSE // 2, D // COARSE, units)
    return pl.pallas_call(
        partial(weight_grad_kernel, z_first),
        in_specs=[SM, VM, VM],
        out_specs=(ANY, ANY),
        scratch_shapes=[
            pltpu.VMEM(shape, BF),
            pltpu.VMEM(shape, BF),
            pltpu.SemaphoreType.DMA((2 * (units // BLOCK),)),
        ],
        out_shape=(sds(shape, BF), sds(shape, BF)),
        cost_estimate=cost(),
        compiler_params=params(52),
    )(ids, left, right)


def gate(ids, units, *waited):
    return pl.pallas_call(
        gate_kernel,
        in_specs=[SM] + [ANY] * len(waited),
        out_specs=SM,
        out_shape=sds(ids.shape, ids.dtype),
        cost_estimate=cost(units),
        compiler_params=params(WIDE),
    )(ids, *waited)


def attention_backward(m, heads, ids, saved, w_out, w_qkv, firsts, before, ctx_other):
    emb, qkv, expo, ctx_t, inverse, cols, rows = saved
    width = heads * HD
    shard = 3 * D // COARSE
    args = [cols, rows, inverse, w_out, *firsts, qkv, ctx_t, expo, emb, w_qkv]
    if m == 0:
        shard += 4 * width // COARSE
        args.append(ctx_other)
    shapes = (
        ((COARSE // 2, shard, width), BF),
        ((COARSE // 2, shard, width), BF),
        ((PAGE, D), BF),
        (before.shape, F32),
    )
    square = pltpu.VMEM((PAGE, PAGE), BF)
    flat = pltpu.VMEM((PAGE, width), BF)
    tall = pltpu.VMEM((width, PAGE), BF)
    return pl.pallas_call(
        partial(backward_kernel, m, heads),
        in_specs=[SM] + [ANY] * len(args) + [VM],
        out_specs=(ANY, ANY, ANY, VM),
        scratch_shapes=[
            pltpu.VMEM(a.shape[1:] if i in (3, 10) else a.shape, a.dtype)
            for i, a in enumerate(args)
        ]
        + [pltpu.VMEM(s, t) for s, t in shapes[:3]]
        + [
            pltpu.VMEM((PAGE, PAGE), jnp.int32),
            square,
            flat,
            tall,
            tall,
            pltpu.VMEM((2, PAGE, PAGE), BF),
            pltpu.VMEM((2, PAGE, PAGE), BF),
            tall,
            flat,
            flat,
            pltpu.VMEM((3 * D, width), BF),
            pltpu.VMEM((heads, 128, PAGE), F32),
            pltpu.VMEM((8, PAGE), F32),
            pltpu.SemaphoreType.DMA((len(args) + heads - 1,)),
            pltpu.SemaphoreType.DMA((3,)),
        ],
        out_shape=tuple(sds(s, t) for s, t in shapes),
        cost_estimate=cost(),
        compiler_params=params(WIDE),
    )(ids, *args, before)


def unpack(modality, ids, parts, groups, heads, filled):
    width = heads * HD
    shapes = ((2, 3 * D, width), (2, width, D))
    rows = parts[0].shape[1]
    extra = () if filled is None else tuple(filled)
    return pl.pallas_call(
        partial(unpack_kernel, modality, groups),
        in_specs=[SM] + [VM] * len(parts) + [ANY] * len(extra),
        out_specs=(ANY, ANY),
        scratch_shapes=[
            pltpu.VMEM((COARSE, rows, width), F32),
            pltpu.SemaphoreType.DMA((3 * COARSE,)),
        ],
        out_shape=tuple(sds(s, F32) for s in shapes),
        input_output_aliases={len(parts) + 1: 0, len(parts) + 2: 1} if extra else {},
        cost_estimate=cost(),
        compiler_params=params(16),
    )(ids, *parts, *extra)


def small_outputs(ids, own, other, heads):
    shapes = ((2, D), (heads, REL_1D + 2 * REL_2D), (2, 2, D), (2, 2, D))
    return pl.pallas_call(
        partial(small_kernel, heads),
        in_specs=[SM, VM, VM],
        out_specs=(VM,) * len(shapes),
        out_shape=tuple(sds(s, F32) for s in shapes),
        cost_estimate=cost(),
        compiler_params=params(8),
    )(ids, own, other)


def on_device(
    n_dp,
    text_rows,
    visual_rows,
    text_mask,
    visual_mask,
    text_places,
    text_boxes,
    visual_boxes,
    mask_embed,
    w_qkv,
    w_out,
    rel_table,
    ln_gain,
    ln_bias,
    w_up,
    b_up,
    w_down,
    b_down,
    text_cotangent,
    visual_cotangent,
):
    heads = rel_table.shape[1]
    half_units = w_up.shape[2]
    quarter = half_units // 4
    dp = lax.axis_index("dp")
    mp = lax.axis_index("mp")
    bits = n_dp.bit_length() - 1
    fine_bits = bits - 4
    me = dp >> fine_bits
    q = dp & 3
    ids = jnp.stack([me, mp, q]).astype(jnp.int32)

    def swap(x, flip):
        return lax.ppermute(x, "dp", [(i, i ^ flip) for i in range(n_dp)])

    def cross(x):
        return lax.ppermute(x, "mp", [(0, 1), (1, 0)])

    up_y = cross(lax.dynamic_slice(w_up, (1 - mp, 0, quarter * q), (1, D, quarter))[0])
    b_up_peer = cross(lax.dynamic_slice(b_up, (1 - mp, 0), (1, half_units)))

    table = rel_table.T
    forward = partial(attention_forward, heads=heads, membed=mask_embed, w_qkv=w_qkv)
    forward = partial(forward, table=table, w_out=w_out)
    *saved_text, att_t = forward(
        0,
        places=text_places.reshape(1, PAGE),
        boxes=text_boxes.T,
        mask=text_mask.reshape(1, PAGE),
        raw=text_rows,
        partial_sum=None,
    )
    up_y = after(up_y, att_t)
    down_part = lax.dynamic_slice(
        after(w_down, att_t), (1 - mp, quarter * q, 0), (1, quarter, D)
    )
    down_y = cross(down_part[0])
    up_x = swap(up_y, 2)
    up_c = swap(up_y, 1)
    *saved_visual, att = forward(
        1,
        places=jnp.arange(PAGE, dtype=jnp.int32).reshape(1, PAGE),
        boxes=visual_boxes.T,
        mask=visual_mask.reshape(1, PAGE),
        raw=visual_rows,
        partial_sum=att_t,
    )
    att_peer = cross(after(att, up_x))
    down_y = after(down_y, att)
    down_x = swap(down_y, 2)
    down_c = swap(down_y, 1)
    up_d = swap(up_x, 1)
    down_d = swap(down_x, 1)

    out, first_own, act, dpre, hid_low, dlow, small = feed_forward(
        ids,
        (saved_text[5], saved_visual[5]),
        (saved_text[0], saved_visual[0]),
        (text_cotangent, visual_cotangent),
        att,
        att_peer,
        ln_gain,
        ln_bias,
        b_up,
        b_up_peer,
        b_down,
        (w_up, w_down),
        (up_y, up_x, up_c, up_d, down_y, down_x, down_c, down_d),
    )
    first_peer = cross(first_own)

    f0 = 1 << fine_bits
    x_first = (f0, 2 * f0, 4 * f0, 8 * f0)
    z_first = (f0, 4 * f0, 2 * f0, 8 * f0)

    def half_sum(keep, *got):
        n = got[-1].shape[0] // 2
        total = keep[n : 2 * n].astype(F32)
        for g in got:
            total = total + g[n : 2 * n].astype(F32)
        return total.astype(BF)

    def last_sum(keep, *got):
        total = keep[0].astype(F32)
        for g in got:
            total = total + g[0].astype(F32)
        for b in range(fine_bits):
            total = total + swap(total, 1 << b)
        return total

    def after_all(values, *others):
        return lax.optimization_barrier((tuple(values), others))[0]

    def own_rows(total):
        count = D // n_dp
        return lax.dynamic_slice(total, (count * (dp & (f0 - 1)), 0), (count, total.shape[1]))

    def select_half(total, half):
        return lax.dynamic_slice(total, (0, half_units * half), (total.shape[0], half_units))

    backward = partial(attention_backward, heads=heads, w_out=w_out, w_qkv=w_qkv)

    dn_keep, dn_send = weight_grad(ids, dlow, act, False)
    dn_1 = swap(dn_send, f0)
    up_keep, up_send = weight_grad(ids, after(hid_low, dn_send), dpre, True)
    up_1 = swap(up_send, f0)
    ids = gate(ids, CLAIM, after(first_peer, up_send))
    dn_2s = half_sum(dn_keep, after(dn_1, ids))
    dn_2 = swap(dn_2s, x_first[1])
    up_2s = half_sum(up_keep, after(up_1, dn_2s))
    up_2 = swap(up_2s, z_first[1])
    out_peer = cross(after(out, up_send))
    firsts = (first_own, first_peer)
    t_keep, t_send, demb_t, small = backward(
        0, ids=after(ids, up_2s), saved=saved_text, firsts=firsts, before=small,
        ctx_other=saved_visual[3]
    )
    t_1 = swap(t_send, f0)
    v_keep, v_send, demb_v, small = backward(
        1, ids=after(ids, t_send, out_peer), saved=saved_visual, firsts=firsts, before=small,
        ctx_other=None
    )
    v_1 = swap(v_send, f0)
    def both(total, peer):
        own = select_half(total, 0)
        peer = peer.astype(F32)
        return jnp.stack([jnp.where(mp == 0, own, peer), jnp.where(mp == 0, peer, own)])

    def input_grad(m, part, part_peer, mask):
        first = jnp.where(mp == m, first_own, first_peer).astype(F32)
        total = first + (part.astype(F32) + part_peer.astype(F32))
        return jnp.where(mask[:, None] == 1, 0.0, total).astype(BF)

    ids = gate(after(ids, v_send), CLAIM, dn_2, up_2)
    t_1 = after(t_1, ids)
    t_2s = half_sum(t_keep, t_1)
    t_2 = swap(t_2s, x_first[1])
    v_2s = half_sum(v_keep, after(v_1, t_2s))
    v_2 = swap(v_2s, x_first[1])
    demb_t_peer = cross(after(demb_t, v_2s))
    dn_3s = half_sum(dn_keep, dn_1, after(dn_2, v_2s))
    dn_3 = swap(dn_3s, x_first[2])
    up_3s = half_sum(up_keep, up_1, after(up_2, dn_3s))
    up_3 = swap(up_3s, z_first[2])
    out_peer = after(out_peer, up_3s)
    text_out = jnp.where(mp == 0, out, out_peer)
    visual_out = jnp.where(mp == 0, out_peer, out)
    t_3s = half_sum(t_keep, t_1, after(t_2, text_out))
    t_3 = swap(t_3s, x_first[2])
    text_grad = input_grad(0, demb_t, after(demb_t_peer, t_3s), text_mask)
    demb_v_peer = cross(after(demb_v, text_grad))
    dn_4s = half_sum(dn_keep, dn_1, dn_2, after(dn_3, text_grad))
    dn_4 = swap(dn_4s, x_first[3])
    v_3s = half_sum(v_keep, v_1, after(v_2, dn_4s))
    v_3 = swap(v_3s, x_first[2])
    t_4s = half_sum(t_keep, t_1, t_2, after(t_3, v_3s))
    t_4 = swap(t_4s, x_first[3])
    v_4s = half_sum(v_keep, v_1, v_2, after(v_3, t_4s))
    v_4 = swap(v_4s, x_first[3])
    visual_grad = input_grad(1, demb_v, after(demb_v_peer, v_4s), visual_mask)
    t_piece = last_sum(t_keep, t_1, t_2, t_3, after(t_4, visual_grad)).astype(BF)
    t_g2 = swap(t_piece, x_first[3])
    up_4s = half_sum(up_keep, up_1, up_2, after(up_3, t_piece))
    up_4 = swap(up_4s, z_first[3])
    small_got = swap(after(small, up_4s), 1)
    dn_total = own_rows(last_sum(dn_keep, dn_1, dn_2, dn_3, after(dn_4, up_4s)))
    dn_cross = cross(select_half(dn_total, 1).astype(BF))
    small = small + after(small_got, dn_total)
    small_got = swap(small, 2)
    v_piece = last_sum(v_keep, v_1, v_2, v_3, after(v_4, small)).astype(BF)
    v_g2 = swap(v_piece, x_first[3])
    small = small + after(small_got, v_piece)
    small_got = swap(small, 4)
    w_down_grad = jnp.transpose(both(dn_total, after(dn_cross, small)), (0, 2, 1))
    t_two = jnp.stack([t_piece, after(t_g2, w_down_grad)])
    t_g1 = swap(t_two, x_first[2])
    t_x1 = swap(t_two, x_first[1])
    small = small + after(small_got, t_two)
    small_got = swap(small, 8)
    up_total = own_rows(last_sum(up_keep, up_1, up_2, up_3, after(up_4, small)))
    up_cross = cross(select_half(up_total, 1).astype(BF))
    v_two = jnp.stack([v_piece, after(v_g2, up_total)])
    v_g1 = swap(v_two, x_first[2])
    small = small + after(small_got, v_two)
    for b in range(4, bits):
        small = small + swap(small, 1 << b)
    small_other = cross(small)
    t_g1 = after(t_g1, small)
    t_x2 = swap(t_g1, x_first[1])
    t_four = jnp.concatenate([t_two, t_g1])
    v_four = jnp.concatenate([v_two, after(v_g1, t_four)])
    v_x = swap(v_four, x_first[1])
    t_x1 = after(t_x1, v_four)
    t_c = swap(t_four, f0)
    t_c1 = swap(t_x1, f0)
    v_c = swap(v_four, f0)
    w_up_grad = both(up_total, after(up_cross, t_x1))
    small_other = after(small_other, w_up_grad)
    mask_total, rel_grad, gain_grad, shift_grad = small_outputs(ids, small, small_other, heads)
    per = half_units // n_dp
    own_bup = lax.dynamic_slice(small[:4].reshape(1, -1), (0, per * dp), (1, per))
    other_bup = lax.dynamic_slice(
        small_other[:4].reshape(1, -1), (0, half_units + per * dp), (1, per)
    )
    b_up_grad = jnp.where(
        jnp.arange(2, dtype=jnp.int32)[:, None] == mp, own_bup, other_bup
    )
    count = D // n_dp
    own_bd = lax.dynamic_slice(small, (4, count * dp), (1, count))
    other_bd = lax.dynamic_slice(small_other, (4, count * dp), (1, count))
    b_down_grad = jnp.where(jnp.arange(2, dtype=jnp.int32)[:, None] == mp, own_bd, other_bd)
    t_x2 = after(t_x2, mask_total, b_up_grad, b_down_grad)
    t_c2 = swap(t_x2, f0)
    text_parts = (t_four, t_x1, t_x2, t_c, t_c1, t_c2)
    text_groups = ((0, 0, 0), (0, 1, 0), (0, 1, 1), (1, 0, 0), (1, 1, 0), (1, 1, 1))
    filled = unpack(0, ids, text_parts, text_groups, heads, None)
    v_x = after(v_x, *filled)
    v_xc = swap(v_x, f0)
    visual_parts = (v_four, v_x, v_c, v_xc)
    visual_groups = ((0, 0, 0), (0, 1, 0), (1, 0, 0), (1, 1, 0))
    w_qkv_grad, w_out_grad = unpack(1, ids, visual_parts, visual_groups, heads, filled)
    w_qkv_grad = w_qkv_grad.reshape(2, 3, D, heads * HD)

    rel_grad = rel_grad.T
    return (
        text_out,
        visual_out,
        text_grad,
        visual_grad,
        mask_total,
        w_qkv_grad,
        w_out_grad,
        rel_grad,
        gain_grad,
        shift_grad,
        w_up_grad,
        b_up_grad,
        w_down_grad,
        b_down_grad,
    )


def solution(mesh):
    in_specs = (
        P("dp", None),
        P("dp", None),
        P("dp"),
        P("dp"),
        P("dp"),
        P("dp", None),
        P("dp", None),
        P(),
        P(None, None, None, "mp"),
        P(None, "mp", None),
        P(None, "mp"),
        P(),
        P(),
        P(None, None, "mp"),
        P(None, "mp"),
        P(None, "mp", None),
        P(),
        P("dp", None),
        P("dp", None),
    )
    out_specs = (
        P("dp", None),
        P("dp", None),
        P("dp", None),
        P("dp", None),
        P(),
        P(None, None, None, "mp"),
        P(None, "mp", None),
        P(None, "mp"),
        P(),
        P(),
        P(None, "dp", "mp"),
        P(None, ("mp", "dp")),
        P(None, "mp", "dp"),
        P(None, "dp"),
    )
    return jax.shard_map(
        partial(on_device, mesh.shape["dp"]),
        mesh=mesh,
        in_specs=in_specs,
        out_specs=out_specs,
        check_vma=False,
    )
```

```python
from functools import partial

import jax
import jax.numpy as jnp
from jax import lax
from jax.experimental import pallas as pl
from jax.experimental.pallas import tpu as pltpu
from jax.sharding import PartitionSpec as P

D = 768
HD = 64
PAGE = 512
REL_1D = 64
REL_2D = 32
COARSE = 16
BLOCK = 768
BF = jnp.bfloat16
F32 = jnp.float32
CLAIM = 20_000_000_000
WIDE = 60


def mm(a, b):
    return lax.dot_general(a, b, (((1,), (0,)), ((), ())), preferred_element_type=F32)


def mm_nt(a, b):
    return lax.dot_general(a, b, (((1,), (1,)), ((), ())), preferred_element_type=F32)


def iota(shape, dim):
    return lax.broadcasted_iota(jnp.int32, shape, dim)


def row_sum(x):
    return jnp.sum(x, axis=-1, keepdims=True)


def row_mean(x):
    return jnp.mean(x, axis=-1, keepdims=True)


def col_sum(x):
    return jnp.sum(x, axis=0, keepdims=True)


def start_all(pairs, sems, first=0):
    copies = []
    for i, (source, target) in enumerate(pairs):
        copy = pltpu.make_async_copy(source, target, sems.at[first + i])
        copy.start()
        copies.append(copy)
    return copies


def wait_all(copies):
    for copy in copies:
        copy.wait()


def line_buckets(cols, rows):
    half = REL_1D // 2
    return jnp.clip(cols[:, 0:1] - rows[0:1, :], -half, half - 1) + half


def place_lanes(cols):
    lane = iota((PAGE, 128), 1)
    code = lane & 63
    across = jnp.broadcast_to(cols[:, 1:2], (PAGE, 128))
    down = jnp.broadcast_to(cols[:, 2:3], (PAGE, 128)) + REL_2D
    return jnp.where(jnp.where(code < REL_2D, across, down) == code, 1.0, 0.0)


def table_plane(table_row):
    b = iota((128, 128), 0)
    lane = iota((128, 128), 1)
    c = lane & 63
    half = REL_2D // 2
    shift = jnp.clip((c & 31) - (b & 31), -half, half - 1) + half + REL_1D
    index = jnp.where(c >= REL_2D, shift + REL_2D, shift)
    spread = jnp.broadcast_to(table_row, (128, 128))
    values = jnp.take_along_axis(spread, index, axis=1)
    values = jnp.where((b >> 5) == (c >> 5), values, 0.0)
    high = values.astype(BF).astype(F32)
    return jnp.where(lane < 64, high, values - high).astype(BF)


def forward_kernel(
    m, heads, has_partial, places, boxes, mask, membed, table, raw, wqkv, wout, *refs
):
    if has_partial:
        partial_ref, refs = refs[0], refs[1:]
    outputs, att, refs = refs[:7], refs[7], refs[8:]
    places_s, boxes_s, mask_s, membed_s, table_s, raw_s, wqkv_s, wout_s = refs[:8]
    emb_s, qkv_s, expo_s, ctx_s, inverse_s, cols_s, rows_s = refs[8:15]
    att_s, idx_s, bias_s, v_t, in_sems, out_sems = refs[15:]
    emb, qkv, expo, ctx_t, inverse, cols, rows = outputs
    sources = (places, boxes, mask, membed, table, raw, wqkv.at[m], wout.at[m])
    loads = start_all(list(zip(sources, refs[:8])), in_sems)
    wait_all(loads[:6])
    row_id = iota((8, PAGE), 0)
    place_row = iota((8, PAGE), 1) if m else jnp.broadcast_to(places_s[...], (8, PAGE))
    mask_row = jnp.where(row_id == 3, jnp.broadcast_to(mask_s[...], (8, PAGE)), 0)
    facts = jnp.where(row_id == 0, place_row, mask_row).astype(F32)
    turned = boxes_s[...].astype(F32)
    facts = jnp.where(row_id == 1, turned[0:1, :], facts)
    facts = jnp.where(row_id == 2, turned[1:2, :], facts)
    rows_s[...] = facts.astype(jnp.int32)
    cols_s[...] = facts.T.astype(jnp.int32)
    masked = cols_s[:, 3:4] == 1
    filler = membed_s[m : m + 1, :].astype(F32)
    embedded = jnp.where(masked, filler, raw_s[...].astype(F32)).astype(BF)
    emb_s[...] = embedded
    stores = start_all([(emb_s, emb), (cols_s, cols), (rows_s, rows)], out_sems)
    loads[6].wait()
    qkv_s[0] = (mm(embedded, wqkv_s[0]) * HD ** (-0.5)).astype(BF)
    qkv_s[1] = mm(embedded, wqkv_s[1]).astype(BF)
    values = mm(embedded, wqkv_s[2]).astype(BF)
    qkv_s[2] = values
    v_t[...] = values.T
    stores += start_all([(qkv_s, qkv)], out_sems, 3)
    idx_s[...] = line_buckets(cols_s, rows_s)
    onehot = place_lanes(cols_s).astype(BF)
    planes = jnp.concatenate([table_plane(table_s[h : h + 1, :]) for h in range(heads)], axis=1)
    bias_s[...] = mm(onehot, planes).astype(BF)
    inverse_s[...] = jnp.zeros((8, PAGE), F32)
    for h in range(heads):
        head = slice(HD * h, HD * (h + 1))
        keys = jnp.concatenate([onehot, qkv_s[1, :, head]], axis=1)
        queries = jnp.concatenate(
            [bias_s[:, 128 * h : 128 * (h + 1)], qkv_s[0, :, head]], axis=1
        )
        spread = jnp.broadcast_to(table_s[h : h + 1, :], (PAGE, 128))
        line = [
            jnp.take_along_axis(spread, idx_s[:, 128 * b : 128 * (b + 1)], axis=1)
            for b in range(PAGE // 128)
        ]
        scores = mm_nt(keys, queries) + jnp.concatenate(line, axis=1)
        exponent = jnp.exp(scores - jnp.max(scores, axis=0, keepdims=True))
        scale = 1.0 / col_sum(exponent)
        inverse_s[h : h + 1, :] = scale
        expo_s[h] = exponent.astype(BF)
        stores += start_all([(expo_s.at[h], expo.at[h])], out_sems, 4 + h)
        ctx_s[head, :] = (mm(v_t[head, :], expo_s[h]) * scale).astype(BF)
    stores += start_all([(ctx_s, ctx_t), (inverse_s, inverse)], out_sems, 4 + heads)
    loads[7].wait()
    attended = mm(ctx_s[...].T, wout_s[...])
    if has_partial:
        att_s[...] = (partial_ref[...] + attended).astype(BF)
        stores += start_all([(att_s, att)], out_sems, 6 + heads)
    else:
        att[...] = attended
    wait_all(stores)


def gelu_both(x):
    z = jnp.abs(x)
    t = 1.0 / (1.0 + (0.3275911 * 0.5**0.5) * z)
    poly = t * (
        0.127414796
        + t * (-0.142248368 + t * (0.7107068705 + t * (-0.7265760135 + t * 0.5307027145)))
    )
    bell = jnp.exp(-0.5 * x * x)
    tail = poly * bell
    phi = jnp.where(x >= 0, 1.0 - tail, tail)
    return x * phi, phi + x * bell * 0.3989422804014327


def copy_list(ids, up_own, down_own, up_recv, down_recv, up_s, down_s, sems):
    mp, q = ids[1], ids[2]
    half = up_own.shape[2]
    quarter = half // 4
    copies = []
    for t in range(half // BLOCK):
        span = slice(BLOCK * t, BLOCK * (t + 1))
        copies.append((up_own.at[mp, :, span], up_s.at[:, span]))
    for j in range(4):
        place = pl.multiple_of(half + quarter * (q ^ j), 128)
        copies.append((up_recv[j], up_s.at[:, pl.ds(place, quarter)]))
    for t in range(half // BLOCK):
        span = slice(BLOCK * t, BLOCK * (t + 1))
        copies.append((down_own.at[mp, span, :], down_s.at[span, :]))
    for j in range(4):
        place = pl.multiple_of(half + quarter * (q ^ j), 128)
        copies.append((down_recv[j], down_s.at[pl.ds(place, quarter), :]))
    return [pltpu.make_async_copy(a, b, sems.at[i]) for i, (a, b) in enumerate(copies)]


def ffn_kernel(
    ids,
    cols_text,
    cols_visual,
    emb_text,
    emb_visual,
    cot_text,
    cot_visual,
    att_own,
    att_peer,
    gain_both,
    shift_both,
    b_up_own,
    b_up_peer,
    b_down_both,
    up_own,
    down_own,
    uy,
    ux,
    uc,
    ud,
    dy,
    dx,
    dc,
    dd,
    out,
    dfirst,
    act,
    dpre,
    hid_low,
    dlow,
    small,
    up_s,
    down_s,
    slope_s,
    norm1,
    hidden,
    work,
    dcomb,
    out_s,
    dfirst_s,
    cols,
    emb,
    cot_s,
    att_own_s,
    att_peer_s,
    gain_s,
    shift_s,
    b_up_both,
    b_up_far,
    b_down_s,
    b_up,
    sems,
    own_sems,
    out_sems,
):
    mp = ids[1]
    text = mp == 0
    plain = start_all(
        [
            (att_own, att_own_s),
            (att_peer, att_peer_s),
            (gain_both, gain_s),
            (shift_both, shift_s),
            (b_up_own, b_up_both),
            (b_up_peer, b_up_far),
            (b_down_both, b_down_s),
        ],
        own_sems,
    )
    at = len(plain)

    @pl.when(text)
    def _():
        start_all([(emb_text, emb), (cols_text, cols), (cot_text, cot_s)], own_sems, at)

    @pl.when(mp != 0)
    def _():
        start_all([(emb_visual, emb), (cols_visual, cols), (cot_visual, cot_s)], own_sems, at)

    chosen = [
        pltpu.make_async_copy(a, b, own_sems.at[at + i])
        for i, (a, b) in enumerate([(emb_text, emb), (cols_text, cols), (cot_text, cot_s)])
    ]
    up_recv = (uy, uc, ux, ud)
    down_recv = (dy, dc, dx, dd)
    copies = copy_list(ids, up_own, down_own, up_recv, down_recv, up_s, down_s, sems)
    n_own = up_own.shape[2] // BLOCK
    per_side = n_own + 4
    for i in range(n_own):
        copies[i].start()
        copies[per_side + i].start()
    for i in range(n_own, per_side):
        copies[i].start()
        copies[per_side + i].start()
    wait_all(plain)
    wait_all(chosen)
    half_units = b_up_own.shape[1]
    b_up[:, :half_units] = jnp.where(text, b_up_both[0:1, :], b_up_both[1:2, :])
    b_up[:, half_units:] = b_up_far[...]
    gain = jnp.where(text, gain_s[0], gain_s[1])
    shift = jnp.where(text, shift_s[0], shift_s[1])
    b_down = jnp.where(text, b_down_s[0:1, :], b_down_s[1:2, :])
    total = emb[...].astype(F32) + (att_own_s[...].astype(F32) + att_peer_s[...].astype(F32))
    centred = total - row_mean(total)
    inv1 = lax.rsqrt(row_mean(centred * centred) + 1e-05)
    n1 = centred * inv1
    norm1[...] = n1
    hid = n1 * gain[0:1, :] + shift[0:1, :]
    hidden[...] = hid
    hid_low[...] = hid.astype(BF)
    n_blocks = up_s.shape[1] // BLOCK

    def landed(first):
        if first < n_own:
            copies[first].wait()
            copies[per_side + first].wait()
        elif first == n_own:
            for i in range(n_own, per_side):
                copies[i].wait()
                copies[per_side + i].wait()

    def before_gelu(t):
        landed(t)
        span = slice(BLOCK * t, BLOCK * (t + 1))
        return mm(hid_low[...], up_s[:, span]) + b_up[:, span]

    pre = before_gelu(0)
    low = None
    for t in range(n_blocks):
        following = before_gelu(t + 1) if t + 1 < n_blocks else None
        span = slice(BLOCK * t, BLOCK * (t + 1))
        value, slope = gelu_both(pre)
        low = value.astype(BF)
        act[:, span] = low
        slope_s[:, span] = slope
        down = mm(low, down_s[span, :])
        if t == 0:
            work[...] = down
        else:
            work[...] += down
        pre = following
    combined = hidden[...] + work[...] + b_down
    centred2 = combined - row_mean(combined)
    inv2 = lax.rsqrt(row_mean(centred2 * centred2) + 1e-05)
    n2 = centred2 * inv2
    out_s[...] = (n2 * gain[1:2, :] + shift[1:2, :]).astype(BF)
    stores = start_all([(out_s, out)], out_sems)
    cot = cot_s[...].astype(F32)
    small[5:6, :] = col_sum(cot * n2)
    small[6:7, :] = col_sum(cot)
    scaled = cot * gain[1:2, :]
    back = inv2 * (scaled - row_mean(scaled) - n2 * row_mean(scaled * n2))
    dcomb[...] = back
    small[4:5, :] = col_sum(back)
    dlow[...] = back.astype(BF)
    dact = mm_nt(dlow[...], down_s[0:BLOCK, :])
    for t in range(n_blocks):
        span = slice(BLOCK * t, BLOCK * (t + 1))
        later = slice(BLOCK * (t + 1), BLOCK * (t + 2))
        following = mm_nt(dlow[...], down_s[later, :]) if t + 1 < n_blocks else None
        low = (dact * slope_s[:, span]).astype(BF)
        dpre[:, span] = low
        small[t : t + 1, :] = col_sum(low.astype(F32))
        dhid = mm_nt(low, up_s[:, span])
        if t == 0:
            work[...] = dhid
        else:
            work[...] += dhid
        dact = following
    dhidden = dcomb[...] + work[...]
    n1 = norm1[...]
    small[7:8, :] = col_sum(dhidden * n1)
    small[8:9, :] = col_sum(dhidden)
    scaled1 = dhidden * gain[0:1, :]
    first = inv1 * (scaled1 - row_mean(scaled1) - n1 * row_mean(scaled1 * n1))
    dfirst_s[...] = first.astype(BF)
    stores += start_all([(dfirst_s, dfirst)], out_sems, 1)
    masked = cols[:, 3:4] == 1
    small[9:10, :] = col_sum(jnp.where(masked, first, 0.0))
    small[10:24, :] = jnp.zeros((14, D), F32)
    wait_all(stores)


def place_of(rel, z_first):
    x, low, high = rel & 1, (rel >> 1) & 1, rel >> 2
    if z_first:
        return (low << 2) | (x << 1) | high
    return (x << 2) | (low << 1) | high


def put_pairs(ids, values, rows, at, keep, send, span, z_first=False):
    upper = ids[0] & 1
    base = ids[0] >> 1
    spot = slice(at, at + rows)
    for i in range(values.shape[0] // (2 * rows)):
        a = values[2 * rows * i : 2 * rows * i + rows].astype(F32)
        b = values[2 * rows * i + rows : 2 * rows * (i + 1)].astype(F32)
        place = place_of(i ^ base, z_first)
        keep[place, spot, span] = jnp.where(upper == 0, a, b).astype(BF)
        send[place, spot, span] = jnp.where(upper == 0, b, a).astype(BF)


def put_small(ids, values, at, keep, send):
    upper = ids[0] & 1
    base = ids[0] >> 1
    half = keep.shape[2]
    spot = slice(at, at + 16)
    tall = jnp.concatenate([values[:, :half], values[:, half:]], axis=0)
    nothing = jnp.zeros((8, half), F32)
    blocks = [tall[8 * i : 8 * i + 8] for i in range(6)] + [nothing] * 10
    for i in range(COARSE // 2):
        a, b = (jnp.concatenate([blocks[2 * i + j], nothing], axis=0) for j in range(2))
        place = place_of(i ^ base, False)
        keep[place, spot, :] = jnp.where(upper == 0, a, b).astype(BF)
        send[place, spot, :] = jnp.where(upper == 0, b, a).astype(BF)


def weight_grad_kernel(z_first, ids, left, right, keep, send, keep_s, send_s, sems):
    left_t = left[...].T
    copies = []
    for t in range(right.shape[1] // BLOCK):
        span = slice(BLOCK * t, BLOCK * (t + 1))
        product = mm(left_t, right[:, span])
        put_pairs(ids, product, D // COARSE, 0, keep_s, send_s, span, z_first)
        for i, (source, target) in enumerate(((keep_s, keep), (send_s, send))):
            copy = pltpu.make_async_copy(
                source.at[:, :, span], target.at[:, :, span], sems.at[2 * t + i]
            )
            copy.start()
            copies.append(copy)
    for copy in copies:
        copy.wait()


def add_row(small, before, row, half, values):
    span = slice(128 * half, 128 * (half + 1))
    small[row : row + 1, span] = before[row : row + 1, span] + values


def backward_kernel(modality, heads, ids, *refs):
    n_in = 12 if modality == 0 else 11
    inputs, before, refs = refs[:n_in], refs[n_in], refs[n_in + 1 :]
    (keep, send, demb, small), refs = refs[:4], refs[4:]
    local, refs = refs[:n_in], refs[n_in:]
    cols, rows, inverse, wout, first_own, first_peer, qkv, ctx_t, expo, emb, wqkv = local[:11]
    keep_s, send_s, demb_s, idx_s, band_s, dctx, dctx_t, k_t, ds_s, dsb_s, dq_t, dk, dv = refs[:13]
    grads_s, hist_s, low_s, in_sems, out_sems = refs[13:]
    sources = list(inputs)
    sources[3] = sources[3].at[modality]
    sources[10] = sources[10].at[modality]
    pairs = []
    for i, (source, target) in enumerate(zip(sources, local)):
        if i == 8:
            pairs += [(source.at[h], target.at[h]) for h in range(heads)]
        else:
            pairs.append((source, target))
    loads = start_all(pairs, in_sems)
    wait_all(loads[:6])
    small[...] = before[...]
    dmixed = (first_own[...].astype(F32) + first_peer[...].astype(F32)).astype(BF)
    back = mm_nt(wout[...], dmixed)
    for h in range(heads):
        head = slice(HD * h, HD * (h + 1))
        dctx_t[head, :] = (back[HD * h : HD * (h + 1)] * inverse[h : h + 1, :]).astype(BF)
    dctx[...] = dctx_t[...].T
    buckets = line_buckets(cols, rows)
    idx_s[...] = buckets
    band_s[...] = jnp.where((buckets > 0) & (buckets < REL_1D - 1), 1.0, 0.0).astype(BF)
    lane = iota((PAGE, 128), 1)
    hot_boxes = place_lanes(cols)
    hot_places = jnp.where((cols[:, 0:1] & 63) == lane - 64, 1.0, 0.0)
    hot_right = jnp.where(lane < 64, hot_boxes, hot_places).astype(BF)
    r = iota((64, PAGE), 0)
    box_code = jnp.where(r < REL_2D, rows[1:2, :], rows[2:3, :] + REL_2D)
    boxes_t = jnp.where(box_code == r, 1.0, 0.0).astype(BF)
    places_t = jnp.where((rows[0:1, :] & 63) == r, 1.0, 0.0).astype(BF)
    b = iota((128, 128), 0)
    c = iota((128, 128), 1)
    box_at = (b & 31) - (c & 63) + 32
    box_index = jnp.clip(box_at, 0, 31) + jnp.where(b >= REL_2D, REL_2D, 0)
    place_index = 64 + ((b - c + 32) & 63)
    diagonal = jnp.where(b < 64, box_index, place_index)
    valid_box = (box_at >= 0) & (box_at < 32) & ((b >> 5) == (c >> 6))
    valid = jnp.where(
        b < 64, jnp.where(valid_box, 1.0, 0.0), jnp.where(c < 64, 1.0, 0.0)
    )
    lane_row = iota((1, 128), 1)
    wait_all(loads[6:8])
    k_t[...] = qkv[1].T
    overlap = back * ctx_t[...].astype(F32)
    shared = jnp.concatenate(
        [col_sum(overlap[HD * h : HD * (h + 1)]) for h in range(heads)], axis=0
    )
    shared = shared * inverse[0:heads, :]
    for h in range(heads):
        head = slice(HD * h, HD * (h + 1))
        loads[8 + h].wait()
        turn = h % 2
        dprobs = mm(qkv[2, :, head], dctx_t[head, :])
        low = (expo[h].astype(F32) * (dprobs - shared[h : h + 1, :])).astype(BF)
        ds_s[turn] = low
        dsb_s[turn] = low * band_s[...]
        low_s[h : h + 1, :] = col_sum(jnp.where(idx_s[...] == 0, low.astype(F32), 0.0))
        both = mm(jnp.concatenate([k_t[head, :], boxes_t], axis=0), ds_s[turn])
        dq_t[head, :] = (both[:HD] * HD ** (-0.5)).astype(BF)
        hist_s[h, 0:64, :] = both[HD:]
        hist_s[h, 64:128, :] = mm(places_t, dsb_s[turn])
        dk[:, head] = mm(ds_s[turn], qkv[0, :, head]).astype(BF)
        dv[:, head] = mm(expo[h], dctx[:, head]).astype(BF)
    first = hist_s[...].reshape(128 * heads, PAGE)
    high = first.astype(BF)
    rest = (first - high.astype(F32)).astype(BF)
    pairs = mm(high, hot_right) + mm(rest, hot_right)
    for h in range(heads):
        mine = pairs[128 * h : 128 * (h + 1)]
        folded = valid * jnp.take_along_axis(mine, diagonal, axis=1)
        add_row(small, before, 12 + h, 0, col_sum(folded[:64]))
        line = col_sum(folded[64:])
        tail = row_sum(low_s[h : h + 1, :])
        add_row(small, before, 12 + h, 1, jnp.where(lane_row == 0, tail, line))
    width = heads * HD
    span = slice(0, width)
    wait_all(loads[8 + heads :])
    emb_t = emb[...].T
    grads_s[0:D, :] = mm_nt(emb_t, dq_t[...]).astype(BF)
    grads_s[D : 2 * D, :] = mm(emb_t, dk[...]).astype(BF)
    grads_s[2 * D : 3 * D, :] = mm(emb_t, dv[...]).astype(BF)
    rows_qkv = 3 * D // COARSE
    rows_out = 2 * width // COARSE
    put_pairs(ids, grads_s[...], rows_qkv, 0, keep_s, send_s, span)
    for i, context in enumerate((ctx_t, local[11]) if modality == 0 else ()):
        out_grad = mm(context[...], dmixed)
        grads_s[0:width, :] = out_grad[:, :width].astype(BF)
        grads_s[width : 2 * width, :] = out_grad[:, width:].astype(BF)
        at = rows_qkv + rows_out * i
        put_pairs(ids, grads_s[0 : 2 * width, :], rows_out, at, keep_s, send_s, span)
    early = slice(0, rows_qkv if modality == 1 else keep_s.shape[1])
    pairs = [(a.at[:, early, :], b.at[:, early, :]) for a, b in ((send_s, send), (keep_s, keep))]
    stores = start_all(pairs, out_sems)
    part = mm_nt(dq_t[...].T, wqkv[0])
    part += mm_nt(dk[...], wqkv[1])
    part += mm_nt(dv[...], wqkv[2])
    demb_s[...] = part.astype(BF)
    stores += start_all([(demb_s, demb)], out_sems, 2)
    mask_row = col_sum(jnp.where(cols[:, 3:4] == 1, part, 0.0))
    small[10 + modality : 11 + modality, :] = before[10 + modality : 11 + modality, :] + mask_row
    if modality == 1:
        put_small(ids, small[...], rows_qkv, keep_s, send_s)
        late = slice(rows_qkv, rows_qkv + 16)
        pairs = [(a.at[:, late, :], b.at[:, late, :]) for a, b in ((send_s, send), (keep_s, keep))]
        stores += start_all(pairs, out_sems, 3)
    wait_all(stores)


def gate_kernel(ids, *refs):
    passed = refs[-1]
    for i in range(ids.shape[0]):
        passed[i] = ids[i]


def unpack_kernel(modality, groups, heads, ids, *refs):
    sources = refs[: len(groups)]
    extra = 6 * modality
    qkv_grad, out_grad = refs[-5 - extra : -3 - extra]
    small_refs, (small_s, stage, sems) = refs[-3 - extra : -3], refs[-3:]
    rows, width = sources[0].shape[1:]
    rows_qkv = 3 * D // COARSE
    rows_out = 2 * width // COARSE
    per_half = COARSE // 2
    count = 3 if modality == 0 else 1
    me = ids[0]
    copies = []
    slot = -1
    for (core, side, lower), source in zip(groups, sources):
        for at in range(source.shape[0]):
            slot += 1
            stage[slot] = source[at].astype(F32)
            low = (at >> 1) + lower
            rel = core | (side << 1) | (low << 2) | ((at & 1) << 3)
            s = rel ^ me
            spot = pl.ds(pl.multiple_of(rows_qkv * s, 8), rows_qkv)
            targets = [qkv_grad.at[modality, spot, :]]
            low = pl.ds(pl.multiple_of(rows_out * (s & (per_half - 1)), 8), rows_out)
            half = pl.ds(pl.multiple_of(width * (s // per_half), 128), width)
            if modality == 0:
                targets += [out_grad.at[m, low, half] for m in range(2)]
            else:
                place = pl.ds(pl.multiple_of(16 * s, 16), 16)
                small_s[place, :] = source[at, rows_qkv:, :].astype(F32)
            start = 0
            for i, target in enumerate(targets):
                size = rows_qkv if i == 0 else rows_out
                copy = pltpu.make_async_copy(
                    stage.at[slot, pl.ds(start, size), :], target, sems.at[count * slot + i]
                )
                copy.start()
                copies.append(copy)
                start += size
    if modality == 1:
        small_kernel(heads, ids, small_s, *small_refs)
    for copy in copies:
        copy.wait()


def fold_matrix():
    bucket = iota((128, 256), 0)
    source = iota((128, 256), 1)
    half = REL_2D // 2
    offset = jnp.clip((source & 63) - 32, -half, half - 1) + half
    plane = REL_1D + offset + jnp.where(source >= 64, REL_2D, 0)
    line = source - 128
    last = REL_1D - 1
    box_part = jnp.where(plane == bucket, 1.0, 0.0)
    box_part += jnp.where(source < 64, jnp.where(bucket == last, 1.0, 0.0), 0.0)
    line_part = jnp.where(line == bucket, 1.0, 0.0) - jnp.where(bucket == last, 1.0, 0.0)
    line_part = jnp.where(line < last, line_part, 0.0)
    return jnp.where(source < 128, box_part, line_part)


def small_kernel(
    heads, ids, pieces, mask_grad, table_grad, gain_grad, shift_grad, own, other
):
    for i, target in enumerate((own, other)):
        tall = [pieces[16 * j + 8 * i : 16 * j + 8 * i + 8, :] for j in range(6)]
        target[...] = jnp.concatenate(
            [jnp.concatenate(tall[:3], axis=0), jnp.concatenate(tall[3:], axis=0)], axis=1
        )
    first = ids[1] == 0
    slot = (
        jnp.where(first, own[...], other[...]),
        jnp.where(first, other[...], own[...]),
    )
    sums = own[12:24, 0:256]
    table = lax.dot_general(
        sums,
        fold_matrix(),
        (((1,), (1,)), ((), ())),
        precision=lax.Precision.HIGHEST,
        preferred_element_type=F32,
    )
    table_grad[...] = table[:heads]
    for m in range(2):
        mask_grad[m : m + 1, :] = (
            own[10 + m : 11 + m, :] + other[10 + m : 11 + m, :] + slot[m][9:10, :]
        )
        gain_grad[m, 0:1, :] = slot[m][7:8, :]
        gain_grad[m, 1:2, :] = slot[m][5:6, :]
        shift_grad[m, 0:1, :] = slot[m][8:9, :]
        shift_grad[m, 1:2, :] = slot[m][6:7, :]


def params(megabytes):
    return pltpu.CompilerParams(vmem_limit_bytes=megabytes * 1024 * 1024)


def cost(units=1000):
    return pl.CostEstimate(flops=units, bytes_accessed=1000, transcendentals=0)


def after(value, *others):
    return lax.optimization_barrier((value,) + others)[0]


VM = pl.BlockSpec(memory_space=pltpu.VMEM)
SM = pl.BlockSpec(memory_space=pltpu.SMEM)
ANY = pl.BlockSpec(memory_space=pl.ANY)


def sds(shape, dtype):
    return jax.ShapeDtypeStruct(shape, dtype)


def attention_forward(m, heads, places, boxes, mask, raw, membed, w_qkv, table, w_out, partial_sum):
    width = heads * HD
    has_partial = partial_sum is not None
    args = [places, boxes, mask, membed, table, raw, w_qkv, w_out]
    specs = [ANY] * len(args)
    locals_in = [
        pltpu.VMEM(a.shape if i < 6 else a.shape[1:], a.dtype) for i, a in enumerate(args)
    ]
    if has_partial:
        args.append(partial_sum)
        specs.append(VM)
    shapes = (
        ((PAGE, D), BF),
        ((3, PAGE, width), BF),
        ((heads, PAGE, PAGE), BF),
        ((width, PAGE), BF),
        ((8, PAGE), F32),
        ((PAGE, 8), jnp.int32),
        ((8, PAGE), jnp.int32),
        ((PAGE, D), BF if has_partial else F32),
    )
    return pl.pallas_call(
        partial(forward_kernel, m, heads, has_partial),
        in_specs=specs,
        out_specs=(ANY,) * 7 + ((ANY,) if has_partial else (VM,)),
        out_shape=tuple(sds(s, t) for s, t in shapes),
        scratch_shapes=locals_in
        + [pltpu.VMEM(s, t) for s, t in shapes[:7]]
        + [
            pltpu.VMEM((PAGE, D), BF),
            pltpu.VMEM((PAGE, PAGE), jnp.int32),
            pltpu.VMEM((PAGE, 128 * heads), BF),
            pltpu.VMEM((width, PAGE), BF),
            pltpu.SemaphoreType.DMA((8,)),
            pltpu.SemaphoreType.DMA((7 + heads,)),
        ],
        cost_estimate=cost(),
        compiler_params=params(WIDE),
    )(*args)


def feed_forward(ids, cols, embs, cots, att_own, att_peer, gain, shift, b_up, b_peer, b_down, own, recv):
    units = 2 * b_up.shape[1]
    up_own, down_own = own
    n_copies = 2 * (up_own.shape[2] // BLOCK + 4)
    args = [*cols, *embs, *cots, att_own, att_peer, gain, shift, b_up, b_peer, b_down]
    shapes = (
        ((PAGE, D), BF),
        ((PAGE, D), BF),
        ((PAGE, units), BF),
        ((PAGE, units), BF),
        ((PAGE, D), BF),
        ((PAGE, D), BF),
        ((24, D), F32),
    )
    rows_f32 = pltpu.VMEM((PAGE, D), F32)
    rows_low = pltpu.VMEM((PAGE, D), BF)
    return pl.pallas_call(
        ffn_kernel,
        in_specs=[SM] + [ANY] * (len(args) + 10),
        out_specs=(ANY, ANY) + (VM,) * 5,
        scratch_shapes=[
            pltpu.VMEM((D, units), BF),
            pltpu.VMEM((units, D), BF),
            pltpu.VMEM((PAGE, units), F32),
            rows_f32,
            rows_f32,
            rows_f32,
            rows_f32,
            rows_low,
            rows_low,
            pltpu.VMEM((PAGE, 8), jnp.int32),
            rows_low,
            rows_low,
        ]
        + [pltpu.VMEM(a.shape, a.dtype) for a in args[6:]]
        + [
            pltpu.VMEM((1, units), F32),
            pltpu.SemaphoreType.DMA((n_copies,)),
            pltpu.SemaphoreType.DMA((10,)),
            pltpu.SemaphoreType.DMA((2,)),
        ],
        out_shape=tuple(sds(s, t) for s, t in shapes),
        cost_estimate=cost(),
        compiler_params=params(52),
    )(ids, *args, up_own, down_own, *recv)


def weight_grad(ids, left, right, z_first):
    units = right.shape[1]
    shape = (COARSE // 2, D // COARSE, units)
    return pl.pallas_call(
        partial(weight_grad_kernel, z_first),
        in_specs=[SM, VM, VM],
        out_specs=(ANY, ANY),
        scratch_shapes=[
            pltpu.VMEM(shape, BF),
            pltpu.VMEM(shape, BF),
            pltpu.SemaphoreType.DMA((2 * (units // BLOCK),)),
        ],
        out_shape=(sds(shape, BF), sds(shape, BF)),
        cost_estimate=cost(),
        compiler_params=params(52),
    )(ids, left, right)


def gate(ids, units, *waited):
    return pl.pallas_call(
        gate_kernel,
        in_specs=[SM] + [ANY] * len(waited),
        out_specs=SM,
        out_shape=sds(ids.shape, ids.dtype),
        cost_estimate=cost(units),
        compiler_params=params(WIDE),
    )(ids, *waited)


def attention_backward(m, heads, ids, saved, w_out, w_qkv, firsts, before, ctx_other):
    emb, qkv, expo, ctx_t, inverse, cols, rows = saved
    width = heads * HD
    shard = 3 * D // COARSE
    args = [cols, rows, inverse, w_out, *firsts, qkv, ctx_t, expo, emb, w_qkv]
    if m == 1:
        shard += 16
    if m == 0:
        shard += 4 * width // COARSE
        args.append(ctx_other)
    shapes = (
        ((COARSE // 2, shard, width), BF),
        ((COARSE // 2, shard, width), BF),
        ((PAGE, D), BF),
        (before.shape, F32),
    )
    square = pltpu.VMEM((PAGE, PAGE), BF)
    flat = pltpu.VMEM((PAGE, width), BF)
    tall = pltpu.VMEM((width, PAGE), BF)
    return pl.pallas_call(
        partial(backward_kernel, m, heads),
        in_specs=[SM] + [ANY] * len(args) + [VM],
        out_specs=(ANY, ANY, ANY, VM),
        scratch_shapes=[
            pltpu.VMEM(a.shape[1:] if i in (3, 10) else a.shape, a.dtype)
            for i, a in enumerate(args)
        ]
        + [pltpu.VMEM(s, t) for s, t in shapes[:3]]
        + [
            pltpu.VMEM((PAGE, PAGE), jnp.int32),
            square,
            flat,
            tall,
            tall,
            pltpu.VMEM((2, PAGE, PAGE), BF),
            pltpu.VMEM((2, PAGE, PAGE), BF),
            tall,
            flat,
            flat,
            pltpu.VMEM((3 * D, width), BF),
            pltpu.VMEM((heads, 128, PAGE), F32),
            pltpu.VMEM((8, PAGE), F32),
            pltpu.SemaphoreType.DMA((len(args) + heads - 1,)),
            pltpu.SemaphoreType.DMA((5,)),
        ],
        out_shape=tuple(sds(s, t) for s, t in shapes),
        cost_estimate=cost(),
        compiler_params=params(WIDE),
    )(ids, *args, before)


def unpack(modality, ids, parts, groups, heads, filled):
    width = heads * HD
    shapes = ((2, 3 * D, width), (2, width, D))
    if modality == 1:
        rows24 = (24, D)
        shapes += ((2, D), (heads, REL_1D + 2 * REL_2D), (2, 2, D), (2, 2, D), rows24, rows24)
    rows = parts[0].shape[1]
    extra = () if filled is None else tuple(filled)
    return pl.pallas_call(
        partial(unpack_kernel, modality, groups, heads),
        in_specs=[SM] + [VM] * len(parts) + [ANY] * len(extra),
        out_specs=(ANY, ANY) + (VM,) * (len(shapes) - 2),
        scratch_shapes=[
            pltpu.VMEM((16 * COARSE, width), F32),
            pltpu.VMEM((COARSE, rows, width), F32),
            pltpu.SemaphoreType.DMA((3 * COARSE,)),
        ],
        out_shape=tuple(sds(s, F32) for s in shapes),
        input_output_aliases={len(parts) + 1: 0, len(parts) + 2: 1} if extra else {},
        cost_estimate=cost(),
        compiler_params=params(16),
    )(ids, *parts, *extra)


def on_device(
    n_dp,
    text_rows,
    visual_rows,
    text_mask,
    visual_mask,
    text_places,
    text_boxes,
    visual_boxes,
    mask_embed,
    w_qkv,
    w_out,
    rel_table,
    ln_gain,
    ln_bias,
    w_up,
    b_up,
    w_down,
    b_down,
    text_cotangent,
    visual_cotangent,
):
    heads = rel_table.shape[1]
    half_units = w_up.shape[2]
    quarter = half_units // 4
    dp = lax.axis_index("dp")
    mp = lax.axis_index("mp")
    bits = n_dp.bit_length() - 1
    fine_bits = bits - 4
    me = dp >> fine_bits
    q = dp & 3
    ids = jnp.stack([me, mp, q]).astype(jnp.int32)

    def swap(x, flip):
        return lax.ppermute(x, "dp", [(i, i ^ flip) for i in range(n_dp)])

    def cross(x):
        return lax.ppermute(x, "mp", [(0, 1), (1, 0)])

    up_y = cross(lax.dynamic_slice(w_up, (1 - mp, 0, quarter * q), (1, D, quarter))[0])
    b_up_peer = cross(lax.dynamic_slice(b_up, (1 - mp, 0), (1, half_units)))

    table = rel_table.T
    forward = partial(attention_forward, heads=heads, membed=mask_embed, w_qkv=w_qkv)
    forward = partial(forward, table=table, w_out=w_out)
    *saved_text, att_t = forward(
        0,
        places=text_places.reshape(1, PAGE),
        boxes=text_boxes.T,
        mask=text_mask.reshape(1, PAGE),
        raw=text_rows,
        partial_sum=None,
    )
    up_y = after(up_y, att_t)
    down_part = lax.dynamic_slice(
        after(w_down, att_t), (1 - mp, quarter * q, 0), (1, quarter, D)
    )
    down_y = cross(down_part[0])
    up_x = swap(up_y, 2)
    up_c = swap(up_y, 1)
    *saved_visual, att = forward(
        1,
        places=text_places.reshape(1, PAGE),
        boxes=visual_boxes.T,
        mask=visual_mask.reshape(1, PAGE),
        raw=visual_rows,
        partial_sum=att_t,
    )
    att_peer = cross(after(att, up_x))
    down_y = after(down_y, att)
    down_x = swap(down_y, 2)
    down_c = swap(down_y, 1)
    up_d = swap(up_x, 1)
    down_d = swap(down_x, 1)

    out, first_own, act, dpre, hid_low, dlow, small = feed_forward(
        ids,
        (saved_text[5], saved_visual[5]),
        (saved_text[0], saved_visual[0]),
        (text_cotangent, visual_cotangent),
        att,
        att_peer,
        ln_gain,
        ln_bias,
        b_up,
        b_up_peer,
        b_down,
        (w_up, w_down),
        (up_y, up_x, up_c, up_d, down_y, down_x, down_c, down_d),
    )
    first_peer = cross(first_own)

    f0 = 1 << fine_bits
    x_first = (f0, 2 * f0, 4 * f0, 8 * f0)
    z_first = (f0, 4 * f0, 2 * f0, 8 * f0)

    def half_sum(keep, *got, low=None, count=None):
        n = got[-1].shape[0] // 2 if count is None else count
        low = n if low is None else low
        total = keep[low : low + n].astype(F32)
        for g in got:
            total = total + g[low : low + n].astype(F32)
        return total.astype(BF)

    def last_sum(keep, *got):
        total = keep[0].astype(F32)
        for g in got:
            total = total + g[0].astype(F32)
        for b in range(fine_bits):
            total = total + swap(total, 1 << b)
        return total

    def after_all(values, *others):
        return lax.optimization_barrier((tuple(values), others))[0]

    def own_rows(total):
        count = D // n_dp
        return lax.dynamic_slice(total, (count * (dp & (f0 - 1)), 0), (count, total.shape[1]))

    def select_half(total, half):
        return lax.dynamic_slice(total, (0, half_units * half), (total.shape[0], half_units))

    backward = partial(attention_backward, heads=heads, w_out=w_out, w_qkv=w_qkv)

    dn_keep, dn_send = weight_grad(ids, dlow, act, False)
    dn_1 = swap(dn_send, f0)
    up_keep, up_send = weight_grad(ids, after(hid_low, dn_send), dpre, True)
    up_1 = swap(up_send, f0)
    ids = gate(ids, CLAIM, after(first_peer, up_send))
    dn_2s = half_sum(dn_keep, after(dn_1, ids))
    dn_2 = swap(dn_2s, x_first[1])
    up_2s = half_sum(up_keep, after(up_1, dn_2s))
    up_2 = swap(up_2s, z_first[1])
    out_peer = cross(after(out, up_send))
    firsts = (first_own, first_peer)
    t_keep, t_send, demb_t, small = backward(
        0, ids=after(ids, up_2s), saved=saved_text, firsts=firsts, before=small,
        ctx_other=saved_visual[3]
    )
    t_1 = swap(t_send, f0)
    v_keep, v_send, demb_v, small = backward(
        1, ids=after(ids, t_send, out_peer), saved=saved_visual, firsts=firsts, before=small,
        ctx_other=None
    )
    v_1 = swap(v_send, f0)
    def both(total, peer):
        own = select_half(total, 0)
        peer = peer.astype(F32)
        return jnp.stack([jnp.where(mp == 0, own, peer), jnp.where(mp == 0, peer, own)])

    def input_grad(m, part, part_peer, mask):
        first = jnp.where(mp == m, first_own, first_peer).astype(F32)
        total = first + (part.astype(F32) + part_peer.astype(F32))
        return jnp.where(mask[:, None] == 1, 0.0, total).astype(BF)

    ids = gate(after(ids, v_send), CLAIM, dn_2, up_2)
    t_1 = after(t_1, ids)
    t_2s = half_sum(t_keep, t_1)
    t_2 = swap(t_2s, x_first[1])
    at = v_keep.shape[1] - 16
    v_1 = after(v_1, t_2s)
    small_half = v_keep[:, at : at + 8].astype(F32) + v_1[:, at : at + 8].astype(F32)
    small_half = small_half.astype(BF)
    small_peer = cross(small_half)
    dn_3s = half_sum(dn_keep, dn_1, after(dn_2, small_half))
    dn_3 = swap(dn_3s, x_first[2])
    out_peer = after(out_peer, dn_3s)
    text_out = jnp.where(mp == 0, out, out_peer)
    visual_out = jnp.where(mp == 0, out_peer, out)
    small_peer = jnp.pad(after(small_peer, text_out), ((0, 0), (at + 8, 0), (0, 0)))
    v_2s = half_sum(v_keep, v_1, small_peer)
    v_2 = swap(v_2s, x_first[1])
    v_keep = half_sum(v_keep[:4], v_1[:4], small_peer[:4], low=0, count=4)
    demb_t_peer = cross(after(demb_t, v_2s))
    up_3s = half_sum(up_keep, up_1, after(up_2, v_2s))
    up_3 = swap(up_3s, z_first[2])
    t_3s = half_sum(t_keep, t_1, after(t_2, up_3s))
    t_3 = swap(t_3s, x_first[2])
    dn_4s = half_sum(dn_keep, dn_1, dn_2, after(dn_3, t_3s))
    dn_4 = swap(dn_4s, x_first[3])
    text_grad = input_grad(0, demb_t, after(demb_t_peer, dn_4s), text_mask)
    demb_v_peer = cross(after(demb_v, text_grad))
    v_3s = half_sum(v_keep, after(v_2, text_grad))
    v_3 = swap(v_3s, x_first[2])
    t_4s = half_sum(t_keep, t_1, t_2, after(t_3, v_3s))
    t_4 = swap(t_4s, x_first[3])
    v_4s = half_sum(v_keep, v_2, after(v_3, t_4s))
    v_4 = swap(v_4s, x_first[3])
    t_piece = last_sum(t_keep, t_1, t_2, t_3, after(t_4, v_4s)).astype(BF)
    t_g2 = swap(t_piece, x_first[3])
    up_4s = half_sum(up_keep, up_1, up_2, after(up_3, t_piece))
    up_4 = swap(up_4s, z_first[3])
    visual_grad = input_grad(1, demb_v, after(demb_v_peer, up_4s), visual_mask)
    v_piece = last_sum(v_keep, v_2, v_3, after(v_4, visual_grad)).astype(BF)
    v_g2 = swap(v_piece, x_first[3])
    dn_total = own_rows(last_sum(dn_keep, dn_1, dn_2, dn_3, after(dn_4, v_piece)))
    dn_cross = cross(select_half(dn_total, 1).astype(BF))
    t_two = jnp.stack([t_piece, after(t_g2, dn_total)])
    t_g1 = swap(t_two, x_first[2])
    t_x1 = swap(t_two, x_first[1])
    v_two = jnp.stack([v_piece, after(v_g2, t_two)])
    v_g1 = swap(v_two, x_first[2])
    v_x1 = swap(v_two, x_first[1])
    w_down_grad = jnp.transpose(both(dn_total, after(dn_cross, v_two)), (0, 2, 1))
    up_total = own_rows(last_sum(up_keep, up_1, up_2, up_3, after(up_4, w_down_grad)))
    up_cross = cross(select_half(up_total, 1).astype(BF))
    t_g1 = after(t_g1, up_total)
    t_x2 = swap(t_g1, x_first[1])
    t_four = jnp.concatenate([t_two, t_g1])
    v_g1 = after(v_g1, t_four)
    v_x2 = swap(v_g1, x_first[1])
    v_four = jnp.concatenate([v_two, v_g1])
    t_x1 = after(t_x1, v_four)
    v_x1 = after(v_x1, t_x1)
    v_c1 = swap(v_x1, f0)
    t_c = swap(t_four, f0)
    t_c1 = swap(t_x1, f0)
    v_c = swap(v_four, f0)
    w_up_grad = both(up_total, after(up_cross, t_x1))
    t_x2 = after(t_x2, w_up_grad)
    t_c2 = swap(t_x2, f0)
    text_parts = (t_four, t_x1, t_x2, t_c, t_c1, t_c2)
    text_groups = ((0, 0, 0), (0, 1, 0), (0, 1, 1), (1, 0, 0), (1, 1, 0), (1, 1, 1))
    filled = unpack(0, ids, text_parts, text_groups, heads, None)
    v_x2 = after(v_x2, *filled)
    v_c2 = swap(v_x2, f0)
    visual_parts = (v_four, v_x1, v_x2, v_c, v_c1, v_c2)
    visual_groups = text_groups
    w_qkv_grad, w_out_grad, mask_total, rel_grad, gain_grad, shift_grad, small, small_other = unpack(
        1, ids, visual_parts, visual_groups, heads, filled
    )
    per = half_units // n_dp
    own_bup = lax.dynamic_slice(small[:4].reshape(1, -1), (0, per * dp), (1, per))
    other_bup = lax.dynamic_slice(
        small_other[:4].reshape(1, -1), (0, half_units + per * dp), (1, per)
    )
    b_up_grad = jnp.where(
        jnp.arange(2, dtype=jnp.int32)[:, None] == mp, own_bup, other_bup
    )
    count = D // n_dp
    own_bd = lax.dynamic_slice(small, (4, count * dp), (1, count))
    other_bd = lax.dynamic_slice(small_other, (4, count * dp), (1, count))
    b_down_grad = jnp.where(jnp.arange(2, dtype=jnp.int32)[:, None] == mp, own_bd, other_bd)
    w_qkv_grad = w_qkv_grad.reshape(2, 3, D, heads * HD)

    rel_grad = rel_grad.T
    return (
        text_out,
        visual_out,
        text_grad,
        visual_grad,
        mask_total,
        w_qkv_grad,
        w_out_grad,
        rel_grad,
        gain_grad,
        shift_grad,
        w_up_grad,
        b_up_grad,
        w_down_grad,
        b_down_grad,
    )


def solution(mesh):
    in_specs = (
        P("dp", None),
        P("dp", None),
        P("dp"),
        P("dp"),
        P("dp"),
        P("dp", None),
        P("dp", None),
        P(),
        P(None, None, None, "mp"),
        P(None, "mp", None),
        P(None, "mp"),
        P(),
        P(),
        P(None, None, "mp"),
        P(None, "mp"),
        P(None, "mp", None),
        P(),
        P("dp", None),
        P("dp", None),
    )
    out_specs = (
        P("dp", None),
        P("dp", None),
        P("dp", None),
        P("dp", None),
        P(),
        P(None, None, None, "mp"),
        P(None, "mp", None),
        P(None, "mp"),
        P(),
        P(),
        P(None, "dp", "mp"),
        P(None, ("mp", "dp")),
        P(None, "mp", "dp"),
        P(None, "dp"),
    )
    return jax.shard_map(
        partial(on_device, mesh.shape["dp"]),
        mesh=mesh,
        in_specs=in_specs,
        out_specs=out_specs,
        check_vma=False,
    )
```

```python
from functools import partial

import jax
import jax.numpy as jnp
from jax import lax
from jax.experimental import pallas as pl
from jax.experimental.pallas import tpu as pltpu
from jax.sharding import PartitionSpec as P

D = 768
HD = 64
PAGE = 512
REL_1D = 64
REL_2D = 32
COARSE = 16
BLOCK = 768
BF = jnp.bfloat16
F32 = jnp.float32
CLAIM = 20_000_000_000
WIDE = 60


def mm(a, b):
    return lax.dot_general(a, b, (((1,), (0,)), ((), ())), preferred_element_type=F32)


def mm_nt(a, b):
    return lax.dot_general(a, b, (((1,), (1,)), ((), ())), preferred_element_type=F32)


def iota(shape, dim):
    return lax.broadcasted_iota(jnp.int32, shape, dim)


def row_sum(x):
    return jnp.sum(x, axis=-1, keepdims=True)


def row_mean(x):
    return jnp.mean(x, axis=-1, keepdims=True)


def col_sum(x):
    return jnp.sum(x, axis=0, keepdims=True)


def start_all(pairs, sems, first=0):
    copies = []
    for i, (source, target) in enumerate(pairs):
        copy = pltpu.make_async_copy(source, target, sems.at[first + i])
        copy.start()
        copies.append(copy)
    return copies


def wait_all(copies):
    for copy in copies:
        copy.wait()


def line_buckets(cols, rows):
    half = REL_1D // 2
    return jnp.clip(cols[:, 0:1] - rows[0:1, :], -half, half - 1) + half


def place_lanes(cols):
    lane = iota((PAGE, 128), 1)
    code = lane & 63
    across = jnp.broadcast_to(cols[:, 1:2], (PAGE, 128))
    down = jnp.broadcast_to(cols[:, 2:3], (PAGE, 128)) + REL_2D
    return jnp.where(jnp.where(code < REL_2D, across, down) == code, 1.0, 0.0)


def table_plane(table_row):
    b = iota((128, 128), 0)
    lane = iota((128, 128), 1)
    c = lane & 63
    half = REL_2D // 2
    shift = jnp.clip((c & 31) - (b & 31), -half, half - 1) + half + REL_1D
    index = jnp.where(c >= REL_2D, shift + REL_2D, shift)
    spread = jnp.broadcast_to(table_row, (128, 128))
    values = jnp.take_along_axis(spread, index, axis=1)
    values = jnp.where((b >> 5) == (c >> 5), values, 0.0)
    high = values.astype(BF).astype(F32)
    return jnp.where(lane < 64, high, values - high).astype(BF)


def forward_kernel(
    m, heads, has_partial, places, boxes, mask, membed, table, raw, wqkv, wout, *refs
):
    if has_partial:
        partial_ref, refs = refs[0], refs[1:]
    outputs, att, refs = refs[:7], refs[7], refs[8:]
    places_s, boxes_s, mask_s, membed_s, table_s, raw_s, wqkv_s, wout_s = refs[:8]
    emb_s, qkv_s, expo_s, ctx_s, inverse_s, cols_s, rows_s = refs[8:15]
    att_s, idx_s, bias_s, v_t, in_sems, out_sems = refs[15:]
    emb, qkv, expo, ctx_t, inverse, cols, rows = outputs
    sources = (places, boxes, mask, membed, table, raw, wqkv.at[m], wout.at[m])
    loads = start_all(list(zip(sources, refs[:8])), in_sems)
    wait_all(loads[:6])
    row_id = iota((8, PAGE), 0)
    place_row = iota((8, PAGE), 1) if m else jnp.broadcast_to(places_s[...], (8, PAGE))
    mask_row = jnp.where(row_id == 3, jnp.broadcast_to(mask_s[...], (8, PAGE)), 0)
    facts = jnp.where(row_id == 0, place_row, mask_row).astype(F32)
    turned = boxes_s[...].astype(F32)
    facts = jnp.where(row_id == 1, turned[0:1, :], facts)
    facts = jnp.where(row_id == 2, turned[1:2, :], facts)
    rows_s[...] = facts.astype(jnp.int32)
    cols_s[...] = facts.T.astype(jnp.int32)
    masked = cols_s[:, 3:4] == 1
    filler = membed_s[m : m + 1, :].astype(F32)
    embedded = jnp.where(masked, filler, raw_s[...].astype(F32)).astype(BF)
    emb_s[...] = embedded
    stores = start_all([(emb_s, emb), (cols_s, cols), (rows_s, rows)], out_sems)
    loads[6].wait()
    qkv_s[0] = (mm(embedded, wqkv_s[0]) * HD ** (-0.5)).astype(BF)
    qkv_s[1] = mm(embedded, wqkv_s[1]).astype(BF)
    values = mm(embedded, wqkv_s[2]).astype(BF)
    qkv_s[2] = values
    v_t[...] = values.T
    stores += start_all([(qkv_s, qkv)], out_sems, 3)
    idx_s[...] = line_buckets(cols_s, rows_s)
    onehot = place_lanes(cols_s).astype(BF)
    planes = jnp.concatenate([table_plane(table_s[h : h + 1, :]) for h in range(heads)], axis=1)
    bias_s[...] = mm(onehot, planes).astype(BF)
    inverse_s[...] = jnp.zeros((8, PAGE), F32)
    for h in range(heads):
        head = slice(HD * h, HD * (h + 1))
        keys = jnp.concatenate([onehot, qkv_s[1, :, head]], axis=1)
        queries = jnp.concatenate(
            [bias_s[:, 128 * h : 128 * (h + 1)], qkv_s[0, :, head]], axis=1
        )
        spread = jnp.broadcast_to(table_s[h : h + 1, :], (PAGE, 128))
        line = [
            jnp.take_along_axis(spread, idx_s[:, 128 * b : 128 * (b + 1)], axis=1)
            for b in range(PAGE // 128)
        ]
        scores = mm_nt(keys, queries) + jnp.concatenate(line, axis=1)
        exponent = jnp.exp(scores - jnp.max(scores, axis=0, keepdims=True))
        scale = 1.0 / col_sum(exponent)
        inverse_s[h : h + 1, :] = scale
        expo_s[h] = exponent.astype(BF)
        stores += start_all([(expo_s.at[h], expo.at[h])], out_sems, 4 + h)
        ctx_s[head, :] = (mm(v_t[head, :], expo_s[h]) * scale).astype(BF)
    stores += start_all([(ctx_s, ctx_t), (inverse_s, inverse)], out_sems, 4 + heads)
    loads[7].wait()
    attended = mm(ctx_s[...].T, wout_s[...])
    if has_partial:
        att_s[...] = (partial_ref[...] + attended).astype(BF)
        stores += start_all([(att_s, att)], out_sems, 6 + heads)
    else:
        att[...] = attended
    wait_all(stores)


def gelu_both(x):
    z = jnp.abs(x)
    t = 1.0 / (1.0 + (0.3275911 * 0.5**0.5) * z)
    poly = t * (
        0.127414796
        + t * (-0.142248368 + t * (0.7107068705 + t * (-0.7265760135 + t * 0.5307027145)))
    )
    bell = jnp.exp(-0.5 * x * x)
    tail = poly * bell
    phi = jnp.where(x >= 0, 1.0 - tail, tail)
    return x * phi, phi + x * bell * 0.3989422804014327


def copy_list(ids, up_own, down_own, up_recv, down_recv, up_s, down_s, sems):
    mp, q = ids[1], ids[2]
    half = up_own.shape[2]
    quarter = half // 4
    copies = []
    for t in range(half // BLOCK):
        span = slice(BLOCK * t, BLOCK * (t + 1))
        copies.append((up_own.at[mp, :, span], up_s.at[:, span]))
    for j in range(4):
        place = pl.multiple_of(half + quarter * (q ^ j), 128)
        copies.append((up_recv[j], up_s.at[:, pl.ds(place, quarter)]))
    for t in range(half // BLOCK):
        span = slice(BLOCK * t, BLOCK * (t + 1))
        copies.append((down_own.at[mp, span, :], down_s.at[span, :]))
    for j in range(4):
        place = pl.multiple_of(half + quarter * (q ^ j), 128)
        copies.append((down_recv[j], down_s.at[pl.ds(place, quarter), :]))
    return [pltpu.make_async_copy(a, b, sems.at[i]) for i, (a, b) in enumerate(copies)]


def ffn_kernel(
    ids,
    cols_text,
    cols_visual,
    emb_text,
    emb_visual,
    cot_text,
    cot_visual,
    att_own,
    att_peer,
    gain_both,
    shift_both,
    b_up_own,
    b_up_peer,
    b_down_both,
    up_own,
    down_own,
    uy,
    ux,
    uc,
    ud,
    dy,
    dx,
    dc,
    dd,
    out,
    dfirst,
    act,
    dpre,
    hid_low,
    dlow,
    small,
    up_s,
    down_s,
    slope_s,
    norm1,
    hidden,
    work,
    dcomb,
    out_s,
    dfirst_s,
    cols,
    emb,
    cot_s,
    att_own_s,
    att_peer_s,
    gain_s,
    shift_s,
    b_up_both,
    b_up_far,
    b_down_s,
    b_up,
    sems,
    own_sems,
    out_sems,
):
    mp = ids[1]
    text = mp == 0
    plain = start_all(
        [
            (att_own, att_own_s),
            (att_peer, att_peer_s),
            (gain_both, gain_s),
            (shift_both, shift_s),
            (b_up_own, b_up_both),
            (b_up_peer, b_up_far),
            (b_down_both, b_down_s),
        ],
        own_sems,
    )
    at = len(plain)

    @pl.when(text)
    def _():
        start_all([(emb_text, emb), (cols_text, cols), (cot_text, cot_s)], own_sems, at)

    @pl.when(mp != 0)
    def _():
        start_all([(emb_visual, emb), (cols_visual, cols), (cot_visual, cot_s)], own_sems, at)

    chosen = [
        pltpu.make_async_copy(a, b, own_sems.at[at + i])
        for i, (a, b) in enumerate([(emb_text, emb), (cols_text, cols), (cot_text, cot_s)])
    ]
    up_recv = (uy, uc, ux, ud)
    down_recv = (dy, dc, dx, dd)
    copies = copy_list(ids, up_own, down_own, up_recv, down_recv, up_s, down_s, sems)
    n_own = up_own.shape[2] // BLOCK
    per_side = n_own + 4
    for i in range(n_own):
        copies[i].start()
        copies[per_side + i].start()
    for i in range(n_own, per_side):
        copies[i].start()
        copies[per_side + i].start()
    wait_all(plain)
    wait_all(chosen)
    half_units = b_up_own.shape[1]
    b_up[:, :half_units] = jnp.where(text, b_up_both[0:1, :], b_up_both[1:2, :])
    b_up[:, half_units:] = b_up_far[...]
    gain = jnp.where(text, gain_s[0], gain_s[1])
    shift = jnp.where(text, shift_s[0], shift_s[1])
    b_down = jnp.where(text, b_down_s[0:1, :], b_down_s[1:2, :])
    total = emb[...].astype(F32) + (att_own_s[...].astype(F32) + att_peer_s[...].astype(F32))
    centred = total - row_mean(total)
    inv1 = lax.rsqrt(row_mean(centred * centred) + 1e-05)
    n1 = centred * inv1
    norm1[...] = n1
    hid = n1 * gain[0:1, :] + shift[0:1, :]
    hidden[...] = hid
    hid_low[...] = hid.astype(BF)
    n_blocks = up_s.shape[1] // BLOCK

    def landed(first):
        if first < n_own:
            copies[first].wait()
            copies[per_side + first].wait()
        elif first == n_own:
            for i in range(n_own, per_side):
                copies[i].wait()
                copies[per_side + i].wait()

    def before_gelu(t):
        landed(t)
        span = slice(BLOCK * t, BLOCK * (t + 1))
        return mm(hid_low[...], up_s[:, span]) + b_up[:, span]

    pre = before_gelu(0)
    low = None
    for t in range(n_blocks):
        following = before_gelu(t + 1) if t + 1 < n_blocks else None
        span = slice(BLOCK * t, BLOCK * (t + 1))
        value, slope = gelu_both(pre)
        low = value.astype(BF)
        act[:, span] = low
        slope_s[:, span] = slope
        down = mm(low, down_s[span, :])
        if t == 0:
            work[...] = down
        else:
            work[...] += down
        pre = following
    combined = hidden[...] + work[...] + b_down
    centred2 = combined - row_mean(combined)
    inv2 = lax.rsqrt(row_mean(centred2 * centred2) + 1e-05)
    n2 = centred2 * inv2
    out_s[...] = (n2 * gain[1:2, :] + shift[1:2, :]).astype(BF)
    stores = start_all([(out_s, out)], out_sems)
    cot = cot_s[...].astype(F32)
    small[5:6, :] = col_sum(cot * n2)
    small[6:7, :] = col_sum(cot)
    scaled = cot * gain[1:2, :]
    back = inv2 * (scaled - row_mean(scaled) - n2 * row_mean(scaled * n2))
    dcomb[...] = back
    small[4:5, :] = col_sum(back)
    dlow[...] = back.astype(BF)
    dact = mm_nt(dlow[...], down_s[0:BLOCK, :])
    for t in range(n_blocks):
        span = slice(BLOCK * t, BLOCK * (t + 1))
        later = slice(BLOCK * (t + 1), BLOCK * (t + 2))
        following = mm_nt(dlow[...], down_s[later, :]) if t + 1 < n_blocks else None
        low = (dact * slope_s[:, span]).astype(BF)
        dpre[:, span] = low
        small[t : t + 1, :] = col_sum(low.astype(F32))
        dhid = mm_nt(low, up_s[:, span])
        if t == 0:
            work[...] = dhid
        else:
            work[...] += dhid
        dact = following
    dhidden = dcomb[...] + work[...]
    n1 = norm1[...]
    small[7:8, :] = col_sum(dhidden * n1)
    small[8:9, :] = col_sum(dhidden)
    scaled1 = dhidden * gain[0:1, :]
    first = inv1 * (scaled1 - row_mean(scaled1) - n1 * row_mean(scaled1 * n1))
    dfirst_s[...] = first.astype(BF)
    stores += start_all([(dfirst_s, dfirst)], out_sems, 1)
    masked = cols[:, 3:4] == 1
    small[9:10, :] = col_sum(jnp.where(masked, first, 0.0))
    small[10:24, :] = jnp.zeros((14, D), F32)
    wait_all(stores)


def place_of(rel, z_first):
    x, low, high = rel & 1, (rel >> 1) & 1, rel >> 2
    if z_first:
        return (low << 2) | (x << 1) | high
    return (x << 2) | (low << 1) | high


def put_pairs(ids, values, rows, at, keep, send, span, z_first=False):
    upper = ids[0] & 1
    base = ids[0] >> 1
    spot = slice(at, at + rows)
    for i in range(values.shape[0] // (2 * rows)):
        a = values[2 * rows * i : 2 * rows * i + rows].astype(F32)
        b = values[2 * rows * i + rows : 2 * rows * (i + 1)].astype(F32)
        place = place_of(i ^ base, z_first)
        keep[place, spot, span] = jnp.where(upper == 0, a, b).astype(BF)
        send[place, spot, span] = jnp.where(upper == 0, b, a).astype(BF)


def put_small(ids, values, at, keep, send):
    upper = ids[0] & 1
    base = ids[0] >> 1
    half = keep.shape[2]
    spot = slice(at, at + 16)
    tall = jnp.concatenate([values[:, :half], values[:, half:]], axis=0)
    nothing = jnp.zeros((8, half), F32)
    blocks = [tall[8 * i : 8 * i + 8] for i in range(6)] + [nothing] * 10
    for i in range(COARSE // 2):
        a, b = (jnp.concatenate([blocks[2 * i + j], nothing], axis=0) for j in range(2))
        place = place_of(i ^ base, False)
        keep[place, spot, :] = jnp.where(upper == 0, a, b).astype(BF)
        send[place, spot, :] = jnp.where(upper == 0, b, a).astype(BF)


def weight_grad_kernel(z_first, ids, left, right, keep, send, keep_s, send_s, sems):
    left_t = left[...].T
    copies = []
    for t in range(right.shape[1] // BLOCK):
        span = slice(BLOCK * t, BLOCK * (t + 1))
        product = mm(left_t, right[:, span])
        put_pairs(ids, product, D // COARSE, 0, keep_s, send_s, span, z_first)
        for i, (source, target) in enumerate(((keep_s, keep), (send_s, send))):
            copy = pltpu.make_async_copy(
                source.at[:, :, span], target.at[:, :, span], sems.at[2 * t + i]
            )
            copy.start()
            copies.append(copy)
    for copy in copies:
        copy.wait()


def add_row(small, before, row, half, values):
    span = slice(128 * half, 128 * (half + 1))
    small[row : row + 1, span] = before[row : row + 1, span] + values


def backward_kernel(modality, heads, ids, *refs):
    n_in = 12 if modality == 0 else 11
    inputs, before, refs = refs[:n_in], refs[n_in], refs[n_in + 1 :]
    (keep, send, demb, small), refs = refs[:4], refs[4:]
    local, refs = refs[:n_in], refs[n_in:]
    cols, rows, inverse, wout, first_own, first_peer, qkv, ctx_t, expo, emb, wqkv = local[:11]
    keep_s, send_s, demb_s, idx_s, band_s, dctx, dctx_t, k_t, ds_s, dsb_s, dq_t, dk, dv = refs[:13]
    grads_s, hist_s, low_s, in_sems, out_sems = refs[13:]
    sources = list(inputs)
    sources[3] = sources[3].at[modality]
    sources[10] = sources[10].at[modality]
    pairs = []
    for i, (source, target) in enumerate(zip(sources, local)):
        if i == 8:
            pairs += [(source.at[h], target.at[h]) for h in range(heads)]
        else:
            pairs.append((source, target))
    loads = start_all(pairs, in_sems)
    wait_all(loads[:6])
    small[...] = before[...]
    dmixed = (first_own[...].astype(F32) + first_peer[...].astype(F32)).astype(BF)
    back = mm_nt(wout[...], dmixed)
    for h in range(heads):
        head = slice(HD * h, HD * (h + 1))
        dctx_t[head, :] = (back[HD * h : HD * (h + 1)] * inverse[h : h + 1, :]).astype(BF)
    dctx[...] = dctx_t[...].T
    buckets = line_buckets(cols, rows)
    idx_s[...] = buckets
    band_s[...] = jnp.where((buckets > 0) & (buckets < REL_1D - 1), 1.0, 0.0).astype(BF)
    lane = iota((PAGE, 128), 1)
    hot_boxes = place_lanes(cols)
    hot_places = jnp.where((cols[:, 0:1] & 63) == lane - 64, 1.0, 0.0)
    hot_right = jnp.where(lane < 64, hot_boxes, hot_places).astype(BF)
    r = iota((64, PAGE), 0)
    box_code = jnp.where(r < REL_2D, rows[1:2, :], rows[2:3, :] + REL_2D)
    boxes_t = jnp.where(box_code == r, 1.0, 0.0).astype(BF)
    places_t = jnp.where((rows[0:1, :] & 63) == r, 1.0, 0.0).astype(BF)
    b = iota((128, 128), 0)
    c = iota((128, 128), 1)
    box_at = (b & 31) - (c & 63) + 32
    box_index = jnp.clip(box_at, 0, 31) + jnp.where(b >= REL_2D, REL_2D, 0)
    place_index = 64 + ((b - c + 32) & 63)
    diagonal = jnp.where(b < 64, box_index, place_index)
    valid_box = (box_at >= 0) & (box_at < 32) & ((b >> 5) == (c >> 6))
    valid = jnp.where(
        b < 64, jnp.where(valid_box, 1.0, 0.0), jnp.where(c < 64, 1.0, 0.0)
    )
    lane_row = iota((1, 128), 1)
    wait_all(loads[6:8])
    k_t[...] = qkv[1].T
    overlap = back * ctx_t[...].astype(F32)
    shared = jnp.concatenate(
        [col_sum(overlap[HD * h : HD * (h + 1)]) for h in range(heads)], axis=0
    )
    shared = shared * inverse[0:heads, :]
    for h in range(heads):
        head = slice(HD * h, HD * (h + 1))
        loads[8 + h].wait()
        turn = h % 2
        dprobs = mm(qkv[2, :, head], dctx_t[head, :])
        low = (expo[h].astype(F32) * (dprobs - shared[h : h + 1, :])).astype(BF)
        ds_s[turn] = low
        dsb_s[turn] = low * band_s[...]
        low_s[h : h + 1, :] = col_sum(jnp.where(idx_s[...] == 0, low.astype(F32), 0.0))
        both = mm(jnp.concatenate([k_t[head, :], boxes_t], axis=0), ds_s[turn])
        dq_t[head, :] = (both[:HD] * HD ** (-0.5)).astype(BF)
        hist_s[h, 0:64, :] = both[HD:]
        hist_s[h, 64:128, :] = mm(places_t, dsb_s[turn])
        dk[:, head] = mm(ds_s[turn], qkv[0, :, head]).astype(BF)
        dv[:, head] = mm(expo[h], dctx[:, head]).astype(BF)
    first = hist_s[...].reshape(128 * heads, PAGE)
    high = first.astype(BF)
    rest = (first - high.astype(F32)).astype(BF)
    pairs = mm(high, hot_right) + mm(rest, hot_right)
    for h in range(heads):
        mine = pairs[128 * h : 128 * (h + 1)]
        folded = valid * jnp.take_along_axis(mine, diagonal, axis=1)
        add_row(small, before, 12 + h, 0, col_sum(folded[:64]))
        line = col_sum(folded[64:])
        tail = row_sum(low_s[h : h + 1, :])
        add_row(small, before, 12 + h, 1, jnp.where(lane_row == 0, tail, line))
    width = heads * HD
    span = slice(0, width)
    wait_all(loads[8 + heads :])
    emb_t = emb[...].T
    grads_s[0:D, :] = mm_nt(emb_t, dq_t[...]).astype(BF)
    grads_s[D : 2 * D, :] = mm(emb_t, dk[...]).astype(BF)
    grads_s[2 * D : 3 * D, :] = mm(emb_t, dv[...]).astype(BF)
    rows_qkv = 3 * D // COARSE
    rows_out = 2 * width // COARSE
    put_pairs(ids, grads_s[...], rows_qkv, 0, keep_s, send_s, span)
    for i, context in enumerate((ctx_t, local[11]) if modality == 0 else ()):
        out_grad = mm(context[...], dmixed)
        grads_s[0:width, :] = out_grad[:, :width].astype(BF)
        grads_s[width : 2 * width, :] = out_grad[:, width:].astype(BF)
        at = rows_qkv + rows_out * i
        put_pairs(ids, grads_s[0 : 2 * width, :], rows_out, at, keep_s, send_s, span)
    early = slice(0, rows_qkv if modality == 1 else keep_s.shape[1])
    pairs = [(a.at[:, early, :], b.at[:, early, :]) for a, b in ((send_s, send), (keep_s, keep))]
    stores = start_all(pairs, out_sems)
    part = mm_nt(dq_t[...].T, wqkv[0])
    part += mm_nt(dk[...], wqkv[1])
    part += mm_nt(dv[...], wqkv[2])
    demb_s[...] = part.astype(BF)
    stores += start_all([(demb_s, demb)], out_sems, 2)
    mask_row = col_sum(jnp.where(cols[:, 3:4] == 1, part, 0.0))
    small[10 + modality : 11 + modality, :] = before[10 + modality : 11 + modality, :] + mask_row
    if modality == 1:
        put_small(ids, small[...], rows_qkv, keep_s, send_s)
        late = slice(rows_qkv, rows_qkv + 16)
        pairs = [(a.at[:, late, :], b.at[:, late, :]) for a, b in ((send_s, send), (keep_s, keep))]
        stores += start_all(pairs, out_sems, 3)
    wait_all(stores)


def gate_kernel(ids, *refs):
    passed = refs[-1]
    for i in range(ids.shape[0]):
        passed[i] = ids[i]


def unpack_kernel(modality, groups, heads, ids, *refs):
    sources = refs[: len(groups)]
    extra = 6 * modality
    qkv_grad, out_grad = refs[-5 - extra : -3 - extra]
    small_refs, (small_s, stage, sems) = refs[-3 - extra : -3], refs[-3:]
    rows, width = sources[0].shape[1:]
    rows_qkv = 3 * D // COARSE
    rows_out = 2 * width // COARSE
    per_half = COARSE // 2
    count = 3 if modality == 0 else 1
    me = ids[0]
    copies = []
    slot = -1
    for (core, side, lower), source in zip(groups, sources):
        for at in range(source.shape[0]):
            slot += 1
            stage[slot] = source[at].astype(F32)
            low = (at >> 1) + lower
            rel = core | (side << 1) | (low << 2) | ((at & 1) << 3)
            s = rel ^ me
            spot = pl.ds(pl.multiple_of(rows_qkv * s, 8), rows_qkv)
            targets = [qkv_grad.at[modality, spot, :]]
            low = pl.ds(pl.multiple_of(rows_out * (s & (per_half - 1)), 8), rows_out)
            half = pl.ds(pl.multiple_of(width * (s // per_half), 128), width)
            if modality == 0:
                targets += [out_grad.at[m, low, half] for m in range(2)]
            else:
                place = pl.ds(pl.multiple_of(16 * s, 16), 16)
                small_s[place, :] = source[at, rows_qkv:, :].astype(F32)
            start = 0
            for i, target in enumerate(targets):
                size = rows_qkv if i == 0 else rows_out
                copy = pltpu.make_async_copy(
                    stage.at[slot, pl.ds(start, size), :], target, sems.at[count * slot + i]
                )
                copy.start()
                copies.append(copy)
                start += size
    if modality == 1:
        small_kernel(heads, ids, small_s, *small_refs)
    for copy in copies:
        copy.wait()


def fold_matrix():
    bucket = iota((128, 256), 0)
    source = iota((128, 256), 1)
    half = REL_2D // 2
    offset = jnp.clip((source & 63) - 32, -half, half - 1) + half
    plane = REL_1D + offset + jnp.where(source >= 64, REL_2D, 0)
    line = source - 128
    last = REL_1D - 1
    box_part = jnp.where(plane == bucket, 1.0, 0.0)
    box_part += jnp.where(source < 64, jnp.where(bucket == last, 1.0, 0.0), 0.0)
    line_part = jnp.where(line == bucket, 1.0, 0.0) - jnp.where(bucket == last, 1.0, 0.0)
    line_part = jnp.where(line < last, line_part, 0.0)
    return jnp.where(source < 128, box_part, line_part)


def small_kernel(
    heads, ids, pieces, mask_grad, table_grad, gain_grad, shift_grad, own, other
):
    for i, target in enumerate((own, other)):
        tall = [pieces[16 * j + 8 * i : 16 * j + 8 * i + 8, :] for j in range(6)]
        target[...] = jnp.concatenate(
            [jnp.concatenate(tall[:3], axis=0), jnp.concatenate(tall[3:], axis=0)], axis=1
        )
    first = ids[1] == 0
    slot = (
        jnp.where(first, own[...], other[...]),
        jnp.where(first, other[...], own[...]),
    )
    sums = own[12:24, 0:256]
    table = lax.dot_general(
        sums,
        fold_matrix(),
        (((1,), (1,)), ((), ())),
        precision=lax.Precision.HIGHEST,
        preferred_element_type=F32,
    )
    table_grad[...] = table[:heads]
    for m in range(2):
        mask_grad[m : m + 1, :] = (
            own[10 + m : 11 + m, :] + other[10 + m : 11 + m, :] + slot[m][9:10, :]
        )
        gain_grad[m, 0:1, :] = slot[m][7:8, :]
        gain_grad[m, 1:2, :] = slot[m][5:6, :]
        shift_grad[m, 0:1, :] = slot[m][8:9, :]
        shift_grad[m, 1:2, :] = slot[m][6:7, :]


def params(megabytes):
    return pltpu.CompilerParams(vmem_limit_bytes=megabytes * 1024 * 1024)


def cost(units=1000):
    return pl.CostEstimate(flops=units, bytes_accessed=1000, transcendentals=0)


def after(value, *others):
    return lax.optimization_barrier((value,) + others)[0]


VM = pl.BlockSpec(memory_space=pltpu.VMEM)
SM = pl.BlockSpec(memory_space=pltpu.SMEM)
ANY = pl.BlockSpec(memory_space=pl.ANY)


def sds(shape, dtype):
    return jax.ShapeDtypeStruct(shape, dtype)


def attention_forward(m, heads, places, boxes, mask, raw, membed, w_qkv, table, w_out, partial_sum):
    width = heads * HD
    has_partial = partial_sum is not None
    args = [places, boxes, mask, membed, table, raw, w_qkv, w_out]
    specs = [ANY] * len(args)
    locals_in = [
        pltpu.VMEM(a.shape if i < 6 else a.shape[1:], a.dtype) for i, a in enumerate(args)
    ]
    if has_partial:
        args.append(partial_sum)
        specs.append(VM)
    shapes = (
        ((PAGE, D), BF),
        ((3, PAGE, width), BF),
        ((heads, PAGE, PAGE), BF),
        ((width, PAGE), BF),
        ((8, PAGE), F32),
        ((PAGE, 8), jnp.int32),
        ((8, PAGE), jnp.int32),
        ((PAGE, D), BF if has_partial else F32),
    )
    return pl.pallas_call(
        partial(forward_kernel, m, heads, has_partial),
        in_specs=specs,
        out_specs=(ANY,) * 7 + ((ANY,) if has_partial else (VM,)),
        out_shape=tuple(sds(s, t) for s, t in shapes),
        scratch_shapes=locals_in
        + [pltpu.VMEM(s, t) for s, t in shapes[:7]]
        + [
            pltpu.VMEM((PAGE, D), BF),
            pltpu.VMEM((PAGE, PAGE), jnp.int32),
            pltpu.VMEM((PAGE, 128 * heads), BF),
            pltpu.VMEM((width, PAGE), BF),
            pltpu.SemaphoreType.DMA((8,)),
            pltpu.SemaphoreType.DMA((7 + heads,)),
        ],
        cost_estimate=cost(),
        compiler_params=params(WIDE),
    )(*args)


def feed_forward(ids, cols, embs, cots, att_own, att_peer, gain, shift, b_up, b_peer, b_down, own, recv):
    units = 2 * b_up.shape[1]
    up_own, down_own = own
    n_copies = 2 * (up_own.shape[2] // BLOCK + 4)
    args = [*cols, *embs, *cots, att_own, att_peer, gain, shift, b_up, b_peer, b_down]
    shapes = (
        ((PAGE, D), BF),
        ((PAGE, D), BF),
        ((PAGE, units), BF),
        ((PAGE, units), BF),
        ((PAGE, D), BF),
        ((PAGE, D), BF),
        ((24, D), F32),
    )
    rows_f32 = pltpu.VMEM((PAGE, D), F32)
    rows_low = pltpu.VMEM((PAGE, D), BF)
    return pl.pallas_call(
        ffn_kernel,
        in_specs=[SM] + [ANY] * (len(args) + 10),
        out_specs=(ANY, ANY) + (VM,) * 5,
        scratch_shapes=[
            pltpu.VMEM((D, units), BF),
            pltpu.VMEM((units, D), BF),
            pltpu.VMEM((PAGE, units), F32),
            rows_f32,
            rows_f32,
            rows_f32,
            rows_f32,
            rows_low,
            rows_low,
            pltpu.VMEM((PAGE, 8), jnp.int32),
            rows_low,
            rows_low,
        ]
        + [pltpu.VMEM(a.shape, a.dtype) for a in args[6:]]
        + [
            pltpu.VMEM((1, units), F32),
            pltpu.SemaphoreType.DMA((n_copies,)),
            pltpu.SemaphoreType.DMA((10,)),
            pltpu.SemaphoreType.DMA((2,)),
        ],
        out_shape=tuple(sds(s, t) for s, t in shapes),
        cost_estimate=cost(),
        compiler_params=params(48),
    )(ids, *args, up_own, down_own, *recv)


def weight_grad(ids, left, right, z_first):
    units = right.shape[1]
    shape = (COARSE // 2, D // COARSE, units)
    return pl.pallas_call(
        partial(weight_grad_kernel, z_first),
        in_specs=[SM, VM, VM],
        out_specs=(ANY, ANY),
        scratch_shapes=[
            pltpu.VMEM(shape, BF),
            pltpu.VMEM(shape, BF),
            pltpu.SemaphoreType.DMA((2 * (units // BLOCK),)),
        ],
        out_shape=(sds(shape, BF), sds(shape, BF)),
        cost_estimate=cost(),
        compiler_params=params(52),
    )(ids, left, right)


def gate(ids, units, *waited):
    return pl.pallas_call(
        gate_kernel,
        in_specs=[SM] + [ANY] * len(waited),
        out_specs=SM,
        out_shape=sds(ids.shape, ids.dtype),
        cost_estimate=cost(units),
        compiler_params=params(WIDE),
    )(ids, *waited)


def attention_backward(m, heads, ids, saved, w_out, w_qkv, firsts, before, ctx_other):
    emb, qkv, expo, ctx_t, inverse, cols, rows = saved
    width = heads * HD
    shard = 3 * D // COARSE
    args = [cols, rows, inverse, w_out, *firsts, qkv, ctx_t, expo, emb, w_qkv]
    if m == 1:
        shard += 16
    if m == 0:
        shard += 4 * width // COARSE
        args.append(ctx_other)
    shapes = (
        ((COARSE // 2, shard, width), BF),
        ((COARSE // 2, shard, width), BF),
        ((PAGE, D), BF),
        (before.shape, F32),
    )
    square = pltpu.VMEM((PAGE, PAGE), BF)
    flat = pltpu.VMEM((PAGE, width), BF)
    tall = pltpu.VMEM((width, PAGE), BF)
    return pl.pallas_call(
        partial(backward_kernel, m, heads),
        in_specs=[SM] + [ANY] * len(args) + [VM],
        out_specs=(ANY, ANY, ANY, VM),
        scratch_shapes=[
            pltpu.VMEM(a.shape[1:] if i in (3, 10) else a.shape, a.dtype)
            for i, a in enumerate(args)
        ]
        + [pltpu.VMEM(s, t) for s, t in shapes[:3]]
        + [
            pltpu.VMEM((PAGE, PAGE), jnp.int32),
            square,
            flat,
            tall,
            tall,
            pltpu.VMEM((2, PAGE, PAGE), BF),
            pltpu.VMEM((2, PAGE, PAGE), BF),
            tall,
            flat,
            flat,
            pltpu.VMEM((3 * D, width), BF),
            pltpu.VMEM((heads, 128, PAGE), F32),
            pltpu.VMEM((8, PAGE), F32),
            pltpu.SemaphoreType.DMA((len(args) + heads - 1,)),
            pltpu.SemaphoreType.DMA((5,)),
        ],
        out_shape=tuple(sds(s, t) for s, t in shapes),
        cost_estimate=cost(),
        compiler_params=params(WIDE),
    )(ids, *args, before)


def unpack(modality, ids, parts, groups, heads, filled):
    width = heads * HD
    shapes = ((2, 3 * D, width), (2, width, D))
    if modality == 1:
        rows24 = (24, D)
        shapes += ((2, D), (heads, REL_1D + 2 * REL_2D), (2, 2, D), (2, 2, D), rows24, rows24)
    rows = parts[0].shape[1]
    extra = () if filled is None else tuple(filled)
    return pl.pallas_call(
        partial(unpack_kernel, modality, groups, heads),
        in_specs=[SM] + [VM] * len(parts) + [ANY] * len(extra),
        out_specs=(ANY, ANY) + (VM,) * (len(shapes) - 2),
        scratch_shapes=[
            pltpu.VMEM((16 * COARSE, width), F32),
            pltpu.VMEM((COARSE, rows, width), F32),
            pltpu.SemaphoreType.DMA((3 * COARSE,)),
        ],
        out_shape=tuple(sds(s, F32) for s in shapes),
        input_output_aliases={len(parts) + 1: 0, len(parts) + 2: 1} if extra else {},
        cost_estimate=cost(),
        compiler_params=params(16),
    )(ids, *parts, *extra)


def on_device(
    n_dp,
    text_rows,
    visual_rows,
    text_mask,
    visual_mask,
    text_places,
    text_boxes,
    visual_boxes,
    mask_embed,
    w_qkv,
    w_out,
    rel_table,
    ln_gain,
    ln_bias,
    w_up,
    b_up,
    w_down,
    b_down,
    text_cotangent,
    visual_cotangent,
):
    heads = rel_table.shape[1]
    half_units = w_up.shape[2]
    quarter = half_units // 4
    dp = lax.axis_index("dp")
    mp = lax.axis_index("mp")
    bits = n_dp.bit_length() - 1
    fine_bits = bits - 4
    me = dp >> fine_bits
    q = dp & 3
    ids = jnp.stack([me, mp, q]).astype(jnp.int32)

    def swap(x, flip):
        return lax.ppermute(x, "dp", [(i, i ^ flip) for i in range(n_dp)])

    def cross(x):
        return lax.ppermute(x, "mp", [(0, 1), (1, 0)])

    up_y = cross(lax.dynamic_slice(w_up, (1 - mp, 0, quarter * q), (1, D, quarter))[0])
    b_up_peer = cross(lax.dynamic_slice(b_up, (1 - mp, 0), (1, half_units)))

    table = rel_table.T
    forward = partial(attention_forward, heads=heads, membed=mask_embed, w_qkv=w_qkv)
    forward = partial(forward, table=table, w_out=w_out)
    *saved_text, att_t = forward(
        0,
        places=text_places.reshape(1, PAGE),
        boxes=text_boxes.T,
        mask=text_mask.reshape(1, PAGE),
        raw=text_rows,
        partial_sum=None,
    )
    up_y = after(up_y, att_t)
    down_part = lax.dynamic_slice(
        after(w_down, att_t), (1 - mp, quarter * q, 0), (1, quarter, D)
    )
    down_y = cross(down_part[0])
    up_x = swap(up_y, 2)
    up_c = swap(up_y, 1)
    *saved_visual, att = forward(
        1,
        places=text_places.reshape(1, PAGE),
        boxes=visual_boxes.T,
        mask=visual_mask.reshape(1, PAGE),
        raw=visual_rows,
        partial_sum=att_t,
    )
    att_peer = cross(after(att, up_x))
    down_y = after(down_y, att)
    down_x = swap(down_y, 2)
    down_c = swap(down_y, 1)
    up_d = swap(up_x, 1)
    down_d = swap(down_x, 1)

    out, first_own, act, dpre, hid_low, dlow, small = feed_forward(
        ids,
        (saved_text[5], saved_visual[5]),
        (saved_text[0], saved_visual[0]),
        (text_cotangent, visual_cotangent),
        att,
        att_peer,
        ln_gain,
        ln_bias,
        b_up,
        b_up_peer,
        b_down,
        (w_up, w_down),
        (up_y, up_x, up_c, up_d, down_y, down_x, down_c, down_d),
    )
    first_peer = cross(first_own)

    f0 = 1 << fine_bits
    x_first = (f0, 2 * f0, 4 * f0, 8 * f0)
    z_first = (f0, 4 * f0, 2 * f0, 8 * f0)

    def half_sum(keep, *got, low=None, count=None):
        n = got[-1].shape[0] // 2 if count is None else count
        low = n if low is None else low
        total = keep[low : low + n].astype(F32)
        for g in got:
            total = total + g[low : low + n].astype(F32)
        return total.astype(BF)

    def last_sum(keep, *got):
        total = keep[0].astype(F32)
        for g in got:
            total = total + g[0].astype(F32)
        for b in range(fine_bits):
            total = total + swap(total, 1 << b)
        return total

    def after_all(values, *others):
        return lax.optimization_barrier((tuple(values), others))[0]

    def own_rows(total):
        count = D // n_dp
        return lax.dynamic_slice(total, (count * (dp & (f0 - 1)), 0), (count, total.shape[1]))

    def select_half(total, half):
        return lax.dynamic_slice(total, (0, half_units * half), (total.shape[0], half_units))

    backward = partial(attention_backward, heads=heads, w_out=w_out, w_qkv=w_qkv)

    dn_keep, dn_send = weight_grad(ids, dlow, act, False)
    dn_1 = swap(dn_send, f0)
    up_keep, up_send = weight_grad(ids, after(hid_low, dn_send), dpre, True)
    up_1 = swap(up_send, f0)
    ids = gate(ids, CLAIM, after(first_peer, up_send))
    dn_2s = half_sum(dn_keep, after(dn_1, ids))
    dn_2 = swap(dn_2s, x_first[1])
    up_2s = half_sum(up_keep, after(up_1, dn_2s))
    up_2 = swap(up_2s, z_first[1])
    out_peer = cross(after(out, up_send))
    firsts = (first_own, first_peer)
    t_keep, t_send, demb_t, small = backward(
        0, ids=after(ids, up_2s), saved=saved_text, firsts=firsts, before=small,
        ctx_other=saved_visual[3]
    )
    t_1 = swap(t_send, f0)
    v_keep, v_send, demb_v, small = backward(
        1, ids=after(ids, t_send, out_peer), saved=saved_visual, firsts=firsts, before=small,
        ctx_other=None
    )
    v_1 = swap(v_send, f0)
    def both(total, peer):
        own = select_half(total, 0)
        peer = peer.astype(F32)
        return jnp.stack([jnp.where(mp == 0, own, peer), jnp.where(mp == 0, peer, own)])

    def input_grad(m, part, part_peer, mask):
        first = jnp.where(mp == m, first_own, first_peer).astype(F32)
        total = first + (part.astype(F32) + part_peer.astype(F32))
        return jnp.where(mask[:, None] == 1, 0.0, total).astype(BF)

    ids = gate(after(ids, v_send), CLAIM, dn_2, up_2)
    t_1 = after(t_1, ids)
    t_2s = half_sum(t_keep, t_1)
    t_2 = swap(t_2s, x_first[1])
    at = v_keep.shape[1] - 16
    v_1 = after(v_1, t_2s)
    small_half = v_keep[:, at : at + 8].astype(F32) + v_1[:, at : at + 8].astype(F32)
    small_half = small_half.astype(BF)
    small_peer = cross(small_half)
    dn_3s = half_sum(dn_keep, dn_1, after(dn_2, small_half))
    dn_3 = swap(dn_3s, x_first[2])
    out_peer = after(out_peer, dn_3s)
    text_out = jnp.where(mp == 0, out, out_peer)
    visual_out = jnp.where(mp == 0, out_peer, out)
    small_peer = jnp.pad(after(small_peer, text_out), ((0, 0), (at + 8, 0), (0, 0)))
    v_2s = half_sum(v_keep, v_1, small_peer)
    v_2 = swap(v_2s, x_first[1])
    v_keep = half_sum(v_keep[:4], v_1[:4], small_peer[:4], low=0, count=4)
    demb_t_peer = cross(after(demb_t, v_2s))
    up_3s = half_sum(up_keep, up_1, after(up_2, v_2s))
    up_3 = swap(up_3s, z_first[2])
    t_3s = half_sum(t_keep, t_1, after(t_2, up_3s))
    t_3 = swap(t_3s, x_first[2])
    dn_4s = half_sum(dn_keep, dn_1, dn_2, after(dn_3, t_3s))
    dn_4 = swap(dn_4s, x_first[3])
    text_grad = input_grad(0, demb_t, after(demb_t_peer, dn_4s), text_mask)
    demb_v_peer = cross(after(demb_v, text_grad))
    v_3s = half_sum(v_keep, after(v_2, text_grad))
    v_3 = swap(v_3s, x_first[2])
    t_4s = half_sum(t_keep, t_1, t_2, after(t_3, v_3s))
    t_4 = swap(t_4s, x_first[3])
    v_4s = half_sum(v_keep, v_2, after(v_3, t_4s))
    v_4 = swap(v_4s, x_first[3])
    t_piece = last_sum(t_keep, t_1, t_2, t_3, after(t_4, v_4s)).astype(BF)
    t_g2 = swap(t_piece, x_first[3])
    up_4s = half_sum(up_keep, up_1, up_2, after(up_3, t_piece))
    up_4 = swap(up_4s, z_first[3])
    visual_grad = input_grad(1, demb_v, after(demb_v_peer, up_4s), visual_mask)
    v_piece = last_sum(v_keep, v_2, v_3, after(v_4, visual_grad)).astype(BF)
    v_g2 = swap(v_piece, x_first[3])
    dn_total = own_rows(last_sum(dn_keep, dn_1, dn_2, dn_3, after(dn_4, v_piece)))
    dn_cross = cross(select_half(dn_total, 1).astype(BF))
    t_two = jnp.stack([t_piece, after(t_g2, dn_total)])
    t_g1 = swap(t_two, x_first[2])
    t_x1 = swap(t_two, x_first[1])
    v_two = jnp.stack([v_piece, after(v_g2, t_two)])
    v_g1 = swap(v_two, x_first[2])
    v_x1 = swap(v_two, x_first[1])
    w_down_grad = jnp.transpose(both(dn_total, after(dn_cross, v_two)), (0, 2, 1))
    up_total = own_rows(last_sum(up_keep, up_1, up_2, up_3, after(up_4, w_down_grad)))
    up_cross = cross(select_half(up_total, 1).astype(BF))
    t_g1 = after(t_g1, up_total)
    t_x2 = swap(t_g1, x_first[1])
    t_four = jnp.concatenate([t_two, t_g1])
    v_g1 = after(v_g1, t_four)
    v_x2 = swap(v_g1, x_first[1])
    v_four = jnp.concatenate([v_two, v_g1])
    t_x1 = after(t_x1, v_four)
    v_x1 = after(v_x1, t_x1)
    v_c1 = swap(v_x1, f0)
    t_c = swap(t_four, f0)
    t_c1 = swap(t_x1, f0)
    v_c = swap(v_four, f0)
    w_up_grad = both(up_total, after(up_cross, t_x1))
    t_x2 = after(t_x2, w_up_grad)
    t_c2 = swap(t_x2, f0)
    text_parts = (t_four, t_x1, t_x2, t_c, t_c1, t_c2)
    text_groups = ((0, 0, 0), (0, 1, 0), (0, 1, 1), (1, 0, 0), (1, 1, 0), (1, 1, 1))
    filled = unpack(0, ids, text_parts, text_groups, heads, None)
    v_x2 = after(v_x2, *filled)
    v_c2 = swap(v_x2, f0)
    visual_parts = (v_four, v_x1, v_x2, v_c, v_c1, v_c2)
    visual_groups = text_groups
    w_qkv_grad, w_out_grad, mask_total, rel_grad, gain_grad, shift_grad, small, small_other = unpack(
        1, ids, visual_parts, visual_groups, heads, filled
    )
    per = half_units // n_dp
    own_bup = lax.dynamic_slice(small[:4].reshape(1, -1), (0, per * dp), (1, per))
    other_bup = lax.dynamic_slice(
        small_other[:4].reshape(1, -1), (0, half_units + per * dp), (1, per)
    )
    b_up_grad = jnp.where(
        jnp.arange(2, dtype=jnp.int32)[:, None] == mp, own_bup, other_bup
    )
    count = D // n_dp
    own_bd = lax.dynamic_slice(small, (4, count * dp), (1, count))
    other_bd = lax.dynamic_slice(small_other, (4, count * dp), (1, count))
    b_down_grad = jnp.where(jnp.arange(2, dtype=jnp.int32)[:, None] == mp, own_bd, other_bd)
    w_qkv_grad = w_qkv_grad.reshape(2, 3, D, heads * HD)

    rel_grad = rel_grad.T
    return (
        text_out,
        visual_out,
        text_grad,
        visual_grad,
        mask_total,
        w_qkv_grad,
        w_out_grad,
        rel_grad,
        gain_grad,
        shift_grad,
        w_up_grad,
        b_up_grad,
        w_down_grad,
        b_down_grad,
    )


def solution(mesh):
    in_specs = (
        P("dp", None),
        P("dp", None),
        P("dp"),
        P("dp"),
        P("dp"),
        P("dp", None),
        P("dp", None),
        P(),
        P(None, None, None, "mp"),
        P(None, "mp", None),
        P(None, "mp"),
        P(),
        P(),
        P(None, None, "mp"),
        P(None, "mp"),
        P(None, "mp", None),
        P(),
        P("dp", None),
        P("dp", None),
    )
    out_specs = (
        P("dp", None),
        P("dp", None),
        P("dp", None),
        P("dp", None),
        P(),
        P(None, None, None, "mp"),
        P(None, "mp", None),
        P(None, "mp"),
        P(),
        P(),
        P(None, "dp", "mp"),
        P(None, ("mp", "dp")),
        P(None, "mp", "dp"),
        P(None, "dp"),
    )
    return jax.shard_map(
        partial(on_device, mesh.shape["dp"]),
        mesh=mesh,
        in_specs=in_specs,
        out_specs=out_specs,
        check_vma=False,
    )
```
